32 devices in a mesh: groups: 2 (over y), shard: 8 (over z, x), owner: 2 (over core).
Axes of the slice: x: 2, y: 2, z: 4, core: 2. Of those that a mesh axis runs over, the one named last changes fastest.
Arguments:
- embeddings: bfloat16 [4096, 768], P(('groups', 'shard', 'owner')), parts along dimension 0, may hold values from -6 to 6
- cluster_id: int32 [4096, 1], P(('groups', 'shard', 'owner')), parts along dimension 0, may hold values from 0 to 7; in each aligned block of 128 rows (0 to 127, 128 to 255, ...) at most 32 rows name the same one
- priority: int32 [4096], P(('groups', 'shard', 'owner')), parts along dimension 0, may hold values from 0 to 2047, each once
Outputs:
- dup_score: float32 [4096], P(('groups', 'shard', 'owner')), parts along dimension 0
- readout: float32 [4096, 768], P(('groups', 'shard', 'owner')), parts along dimension 0
The draws below stay inside these ranges and needn't reach their ends.
There are 2 independent parts, one for each index of `groups`. The reference program is written for one: setup_inputs(seed, part) draws one part's arguments, and reference() takes and returns one part's arrays. A program takes and returns all parts, laid end to end along the dimension named above; each array names one. Nothing has to cross between parts.
Inputs may be any that keep to these rules, and one draw needn't show every extreme that they name: `cluster_id`: among the rows of one device no cluster is named more than 32 times. `priority`: all ranks within one part (one index of groups) are distinct.
All inputs are finite; a program needn't handle non-finite values.
Results may differ from the reference program's by a relative error of at most 0.0041.
Values may be sent and summed in bfloat16 or wider, within the bound.
No kernel may reach another device: no remote copies, remote signals or barrier semaphores. Data moves between devices by JAX's collectives and lax.ppermute only.
A program may use at most 64 MiB of HBM per device.

```python
import math
import jax
import jax.numpy as jnp
import numpy as np
from jax import lax

D = 768
ROWS = 128
CAP = 32
CLUSTERS = 8
IMAGES = 2048
KEYS = 512


def steps_of(key, extent, split, smallest, top_value):
    gain = 1.0
    for axis_at, shards_of in split:
        heights = jax.random.uniform(jax.random.fold_in(jax.random.fold_in(key, 6), axis_at), (shards_of,), jnp.float32, smallest / len(split), top_value / len(split))
        gain = gain * jnp.repeat(jnp.exp(heights), extent[axis_at] // shards_of).reshape((-1,) + (1,) * (len(extent) - 1 - axis_at))
    return gain


def shared_out(own_key, own, number, rows, amount, top, limit, skew):
    ranking = jax.random.permutation(own_key, amount)
    packed, usual = load_shares(amount, rows * top, limit, skew, True), load_shares(amount, rows * top, limit, skew, False)
    places = jnp.arange(amount)

    def named(tallies, turn):
        used = int((tallies > 0).sum())
        fixed = max(1, used // 4)
        shifted = fixed + (places - fixed + turn * (used - fixed)) % max(1, amount - fixed)
        return jnp.zeros((amount,), jnp.int32).at[ranking[jnp.where(places < fixed, places, shifted)]].set(jnp.asarray(tallies, jnp.int32))

    tallies = jnp.where(number % 4 == 0, named(packed, number // 4), named(usual, number - number // 4 - 1))
    mixed = jax.random.permutation(jax.random.fold_in(own, 3), amount)
    giver, sink = mixed[0:amount // 2 * 2:2], mixed[1:amount // 2 * 2:2]
    margin = jnp.minimum(tallies[giver] - 1, limit - tallies[sink]) // 2
    margin = jnp.where((giver == ranking[0]) | (sink == ranking[0]) | (tallies[sink] == 0), 0, jnp.maximum(margin, 0))
    shifted = jax.random.randint(jax.random.fold_in(own, 4), (amount // 2,), 0, 1 << 20) % (margin + 1)
    tallies = tallies.at[giver].add(-shifted).at[sink].add(shifted)
    members = jnp.searchsorted(jnp.cumsum(tallies), jnp.arange(rows * top), side="right").astype(jnp.int32)
    table = members.reshape(top, rows).T
    table = table[jax.random.permutation(jax.random.fold_in(own, 1), rows)]
    turn = jax.random.randint(jax.random.fold_in(own, 2), (rows, 1), 0, top)
    return jnp.take_along_axis(table, (jnp.arange(top)[None, :] + turn) % top, axis=1)


def load_shares(count, total, reach, lean, full):
    weights = [(1 << 20) // math.isqrt(rank ** lean) + 1 for rank in range(1, count + 1)]
    largest = reach if full else min(reach, max(-(-total // count), total * weights[0] // sum(weights)))
    least = 1 if total - largest >= count - 1 else 0
    given, rest = [largest] + [least] * (count - 1), total - largest - least * (count - 1)
    while rest > 0:
        candidates = [i for i in range(1, count) if given[i] < largest] or [i for i in range(1, count) if given[i] < reach]
        pool, budget = sum([weights[i] for i in candidates]), rest
        for i in candidates:
            addition = min(reach - given[i], max(1, budget * weights[i] // pool), rest)
            given[i] = given[i] + addition
            rest = rest - addition
    return np.array(given)


def centred(rng, extent, width, reach, shards=(), kind=jnp.bfloat16):
    array = jax.random.normal(rng, extent, jnp.float32) * width
    if len(shards) > 0:
        array = steps_of(rng, extent, shards, -0.22, 0.18) * array
    return jnp.clip(array, min=-reach, max=reach).astype(kind)


def setup_inputs(seed: int = 0, part: int = 0) -> dict:
    key_list = jax.random.split(jax.random.key(seed), 4)
    part_keys = jax.random.split(jax.random.fold_in(key_list[3], part), 4)
    embeddings = centred(part_keys[0], (IMAGES, D), 1.0, 6.0, ((0, 16),))
    cluster_id_keys = jax.random.split(jax.random.fold_in(part_keys[1], 1), IMAGES // ROWS)
    cluster_id_turns = jax.random.permutation(jax.random.fold_in(part_keys[1], 3), IMAGES // ROWS)
    cluster_id = jax.vmap(lambda own, number: shared_out(jax.random.fold_in(part_keys[1], 2), own, number, ROWS, CLUSTERS, 1, CAP, 2))(cluster_id_keys, cluster_id_turns).reshape((IMAGES, 1))
    priority = jax.random.permutation(part_keys[2], IMAGES).astype(jnp.int32)
    return {"embeddings": embeddings, "cluster_id": cluster_id, "priority": priority}


def make_unit(rows):
    wide = rows.astype(jnp.float32)
    scale = lax.rsqrt(lax.optimization_barrier(jnp.mean(wide * wide, axis=-1, keepdims=True)) + 1e-06) / jnp.sqrt(jnp.float32(rows.shape[-1]))
    return (wide * scale).astype(jnp.bfloat16)

def reference(embeddings, cluster_id, priority):
    images = embeddings.shape[0]
    labels = cluster_id[:, 0]
    order = jnp.argsort(labels, stable=True).astype(jnp.int32)
    counts = lax.optimization_barrier(jnp.sum((labels[None, :] == jnp.arange(CLUSTERS, dtype=jnp.int32)[:, None]).astype(jnp.int32), axis=1))
    starts = jnp.cumsum(counts) - counts

    def one_cluster(label):
        places = jnp.arange(KEYS, dtype=jnp.int32)
        live = places < counts[label]
        where_at = jnp.clip(starts[label] + places, 0, images - 1).astype(jnp.int32)
        member = order[where_at]
        rows = jnp.where(live[:, None], embeddings[member], jnp.zeros((), jnp.bfloat16))
        ranks = jnp.where(live, priority[member], -1)
        unit = make_unit(rows)
        cosine = jnp.dot(unit, unit.T, preferred_element_type=jnp.float32)
        weight = jax.nn.sigmoid(40.0 * (cosine - 0.05))
        earlier = live[None, :] & (ranks[None, :] < ranks[:, None])
        others = live[None, :] & (ranks[None, :] != ranks[:, None])
        dup = jnp.log1p(lax.optimization_barrier(jnp.sum(jnp.where(earlier, weight, 0.0), axis=1)))
        near = jnp.where(others, weight, 0.0)
        total = lax.optimization_barrier(jnp.sum(near, axis=1))
        mixed = jnp.dot(near.astype(jnp.bfloat16), rows, preferred_element_type=jnp.float32)
        mixed = mixed / jnp.sqrt(1.0 + total)[:, None]
        target = jnp.where(live, member, images).astype(jnp.int32)
        return (dup, mixed, target)
    dups, mixes, targets = lax.map(one_cluster, jnp.arange(CLUSTERS, dtype=jnp.int32))
    flat = targets.reshape(-1)
    dup_score = jnp.zeros((images,), jnp.float32).at[flat].set(dups.reshape(-1), mode='drop')
    readout = jnp.zeros((images, embeddings.shape[1]), jnp.float32).at[flat].set(mixes.reshape(-1, embeddings.shape[1]), mode='drop')
    return (dup_score, readout)
```

```python
import jax
import jax.numpy as jnp
from jax import lax
from jax.experimental import pallas as pl
from jax.experimental.pallas import tpu as pltpu
from jax.sharding import PartitionSpec as P

EXTRA = 16
VMEM = 48 * 1024 * 1024


def make_unit(rows):
    wide = rows.astype(jnp.float32)
    scale = lax.rsqrt(jnp.mean(wide * wide, axis=-1, keepdims=True) + 1e-06) / jnp.sqrt(
        jnp.float32(rows.shape[-1])
    )
    return (wide * scale).astype(jnp.bfloat16)


def diagonal(count):
    down = lax.broadcasted_iota(jnp.int32, (count, count), 0)
    return down == lax.broadcasted_iota(jnp.int32, (count, count), 1)


def as_row(column):
    return jnp.sum(jnp.where(diagonal(column.shape[0]), column, 0.0), axis=0, keepdims=True)


def as_column(row):
    return jnp.sum(jnp.where(diagonal(row.shape[1]), row, 0.0), axis=1, keepdims=True)


def pack_kernel(rows_ref, label_ref, rank_ref, packed_ref):
    count, width = rows_ref.shape
    packed_ref[:count, :] = rows_ref[...]
    packed_ref[count:, :] = jnp.zeros((EXTRA, width), jnp.bfloat16)
    rank = rank_ref[...]
    high = lax.shift_right_logical(rank, 8)
    low = rank - lax.shift_left(high, 8)
    pieces = (
        as_row(label_ref[...].astype(jnp.float32)),
        high.astype(jnp.float32),
        low.astype(jnp.float32),
    )
    for at, piece in enumerate(pieces):
        packed_ref[count : count + EXTRA, at * count : (at + 1) * count] = jnp.broadcast_to(
            piece, (EXTRA, count)
        ).astype(jnp.bfloat16)


def labels_and_ranks(extra, count):
    line = extra.astype(jnp.float32)[:1]
    label, high, low = (line[:, at * count : (at + 1) * count] for at in range(3))
    return label, high * 256.0 + low


def score_kernel(own_ref, blocks_ref, dup_ref, mixed_ref, unit_ref, side_ref, sums_ref):
    step = pl.program_id(0)
    many, height, width = blocks_ref.shape
    count = height - EXTRA

    @pl.when(step == 0)
    def _():
        unit_ref[...] = make_unit(own_ref[:count, :])
        label, rank = labels_and_ranks(own_ref[count:, :], count)
        side_ref[:, 0:1] = as_column(label)
        side_ref[:, 1:2] = as_column(rank)
        sums_ref[...] = jnp.zeros_like(sums_ref)
        mixed_ref[...] = jnp.zeros_like(mixed_ref)

    own_label = side_ref[:, 0:1]
    own_rank = side_ref[:, 1:2]
    keys = jnp.concatenate([blocks_ref[at, :count, :] for at in range(many)], axis=0)
    sides = [labels_and_ranks(blocks_ref[at, count:, :], count) for at in range(many)]
    label = jnp.concatenate([side[0] for side in sides], axis=1)
    rank = jnp.concatenate([side[1] for side in sides], axis=1)
    cosine = lax.dot_general(
        unit_ref[...],
        make_unit(keys),
        (((1,), (1,)), ((), ())),
        preferred_element_type=jnp.float32,
    )
    weight = 1.0 / (1.0 + jnp.exp(-40.0 * (cosine - 0.05)))
    near = jnp.where((label == own_label) & (rank != own_rank), weight, 0.0)
    sums_ref[:, 0:1] += jnp.sum(jnp.where(rank < own_rank, near, 0.0), axis=1, keepdims=True)
    sums_ref[:, 1:2] += jnp.sum(near, axis=1, keepdims=True)
    mixed_ref[...] += jnp.dot(near.astype(jnp.bfloat16), keys, preferred_element_type=jnp.float32)

    @pl.when(step == pl.num_programs(0) - 1)
    def _():
        dup_ref[...] = as_row(jnp.log1p(sums_ref[:, 0:1]))
        mixed_ref[...] = mixed_ref[...] / jnp.sqrt(1.0 + sums_ref[:, 1:2])


def local(embeddings, cluster_id, priority):
    count, width = embeddings.shape
    packed = pl.pallas_call(
        pack_kernel,
        out_shape=jax.ShapeDtypeStruct((count + EXTRA, width), jnp.bfloat16),
        name="pack",
    )(embeddings, cluster_id, priority[None, :])
    blocks = lax.all_gather(packed, ("shard", "owner"), axis=0, tiled=False)
    total = blocks.shape[0]
    many = 2
    dup, mixed = pl.pallas_call(
        score_kernel,
        grid=(total // many,),
        in_specs=[
            pl.BlockSpec((count + EXTRA, width), lambda i: (0, 0)),
            pl.BlockSpec((many, count + EXTRA, width), lambda i: (i, 0, 0)),
        ],
        out_specs=[
            pl.BlockSpec((1, count), lambda i: (0, 0)),
            pl.BlockSpec((count, width), lambda i: (0, 0)),
        ],
        out_shape=[
            jax.ShapeDtypeStruct((1, count), jnp.float32),
            jax.ShapeDtypeStruct((count, width), jnp.float32),
        ],
        scratch_shapes=[
            pltpu.VMEM((count, width), jnp.bfloat16),
            pltpu.VMEM((count, 128), jnp.float32),
            pltpu.VMEM((count, 128), jnp.float32),
        ],
        compiler_params=pltpu.CompilerParams(vmem_limit_bytes=VMEM),
        name="score",
    )(packed, blocks)
    return dup[0], mixed


def solution(mesh):
    placed = (
        P(("groups", "shard", "owner"), None),
        P(("groups", "shard", "owner"), None),
        P(("groups", "shard", "owner")),
    )
    return jax.shard_map(
        local,
        mesh=mesh,
        in_specs=placed,
        out_specs=(P(("groups", "shard", "owner")), P(("groups", "shard", "owner"), None)),
        check_vma=False,
    )
```

```python
import jax
import jax.numpy as jnp
from jax import lax
from jax.experimental import pallas as pl
from jax.experimental.pallas import tpu as pltpu
from jax.sharding import PartitionSpec as P

EXTRA = 16
VMEM = 48 * 1024 * 1024


def make_unit(rows):
    wide = rows.astype(jnp.float32)
    scale = lax.rsqrt(jnp.mean(wide * wide, axis=-1, keepdims=True) + 1e-06) / jnp.sqrt(
        jnp.float32(rows.shape[-1])
    )
    return (wide * scale).astype(jnp.bfloat16)


def diagonal(count):
    down = lax.broadcasted_iota(jnp.int32, (count, count), 0)
    return down == lax.broadcasted_iota(jnp.int32, (count, count), 1)


def as_row(column):
    return jnp.sum(jnp.where(diagonal(column.shape[0]), column, 0.0), axis=0, keepdims=True)


def as_column(row):
    return jnp.sum(jnp.where(diagonal(row.shape[1]), row, 0.0), axis=1, keepdims=True)


def pack_kernel(rows_ref, label_ref, rank_ref, packed_ref):
    count, width = rows_ref.shape
    packed_ref[:count, :] = rows_ref[...]
    packed_ref[count:, :] = jnp.zeros((EXTRA, width), jnp.bfloat16)
    rank = rank_ref[...]
    high = lax.shift_right_logical(rank, 8)
    low = rank - lax.shift_left(high, 8)
    pieces = (
        label_ref[...].astype(jnp.float32),
        high.astype(jnp.float32),
        low.astype(jnp.float32),
    )
    for at, piece in enumerate(pieces):
        packed_ref[count : count + EXTRA, at * count : (at + 1) * count] = jnp.broadcast_to(
            piece, (EXTRA, count)
        ).astype(jnp.bfloat16)


def labels_and_ranks(extra, count):
    line = extra.astype(jnp.float32)[:1]
    label, high, low = (line[:, at * count : (at + 1) * count] for at in range(3))
    return label, high * 256.0 + low


def score_pair(unit, own_label, own_rank, blocks):
    count = blocks[0].shape[0] - EXTRA
    keys = jnp.concatenate([block[:count, :] for block in blocks], axis=0)
    sides = [labels_and_ranks(block[count:, :], count) for block in blocks]
    label = jnp.concatenate([side[0] for side in sides], axis=1)
    rank = jnp.concatenate([side[1] for side in sides], axis=1)
    cosine = lax.dot_general(
        unit, make_unit(keys), (((1,), (1,)), ((), ())), preferred_element_type=jnp.float32
    )
    weight = 1.0 / (1.0 + jnp.exp(-40.0 * (cosine - 0.05)))
    near = jnp.where((label == own_label) & (rank != own_rank), weight, 0.0)
    earlier = jnp.sum(jnp.where(rank < own_rank, near, 0.0), axis=1, keepdims=True)
    every = jnp.sum(near, axis=1, keepdims=True)
    mixed = jnp.dot(near.astype(jnp.bfloat16), keys, preferred_element_type=jnp.float32)
    return earlier, every, mixed


def first_kernel(own_ref, other_ref, *refs):
    blocks, (unit_ref, side_ref, sums_ref, mixed_ref) = refs[:-4], refs[-4:]
    count = own_ref.shape[0] - EXTRA
    side_ref[...] = jnp.zeros_like(side_ref)
    sums_ref[...] = jnp.zeros_like(sums_ref)
    for at, ref in enumerate((own_ref, other_ref)):
        here = slice(at * count, (at + 1) * count)
        unit_ref[here, :] = make_unit(ref[:count, :])
        label, rank = labels_and_ranks(ref[count:, :], count)
        side_ref[here, 0:1] = as_column(label)
        side_ref[here, 1:2] = as_column(rank)
    sums_ref[:, 0:1], sums_ref[:, 1:2], mixed_ref[...] = score_pair(
        unit_ref[...], side_ref[:, 0:1], side_ref[:, 1:2], [own_ref] + list(blocks)
    )


def next_kernel(unit_ref, side_ref, old_sums_ref, old_mixed_ref, *refs):
    blocks, (sums_ref, mixed_ref) = refs[:-2], refs[-2:]
    earlier, every, mixed = score_pair(
        unit_ref[...], side_ref[:, 0:1], side_ref[:, 1:2], blocks
    )
    sums_ref[...] = old_sums_ref[...]
    sums_ref[:, 0:1] += earlier
    sums_ref[:, 1:2] += every
    mixed_ref[...] = old_mixed_ref[...] + mixed


def last_kernel(sums_ref, mixed_ref, other_sums_ref, other_mixed_ref, dup_ref, out_ref):
    earlier = sums_ref[:, 0:1] + other_sums_ref[:, 0:1]
    every = sums_ref[:, 1:2] + other_sums_ref[:, 1:2]
    dup_ref[...] = as_row(jnp.log1p(earlier))
    out_ref[...] = (mixed_ref[...] + other_mixed_ref[...]) / jnp.sqrt(1.0 + every)


def cost(queries, keys, width):
    return pl.CostEstimate(
        flops=4 * queries * keys * width,
        bytes_accessed=8 * queries * width + 2 * keys * width,
        transcendentals=queries * keys,
    )


def local(embeddings, cluster_id, priority):
    count, width = embeddings.shape
    shards = lax.axis_size("shard")
    lanes = lax.axis_size("owner")
    packed = pl.pallas_call(
        pack_kernel,
        out_shape=jax.ShapeDtypeStruct((count + EXTRA, width), jnp.bfloat16),
        name="pack",
    )(embeddings, cluster_id.reshape(1, count), priority.reshape(1, count))

    def across(array):
        return lax.ppermute(array, "shard", [(at, at ^ 1) for at in range(shards)])

    def along(array):
        return lax.ppermute(array, "shard", [(at, (at + 2) % shards) for at in range(shards)])

    def swap(array):
        return lax.ppermute(array, "owner", [(at, lanes - 1 - at) for at in range(lanes)])

    queries = 2 * count
    f32 = jnp.float32
    sums_shape = jax.ShapeDtypeStruct((queries, 128), f32)
    mixed_shape = jax.ShapeDtypeStruct((queries, width), f32)
    params = pltpu.CompilerParams(vmem_limit_bytes=VMEM)

    def first(*blocks):
        return pl.pallas_call(
            first_kernel,
            out_shape=[
                jax.ShapeDtypeStruct((queries, width), jnp.bfloat16),
                jax.ShapeDtypeStruct((queries, 128), f32),
                sums_shape,
                mixed_shape,
            ],
            cost_estimate=cost(queries, (len(blocks) - 1) * count, width),
            compiler_params=params,
            name="first_scores",
        )(*blocks)

    def more(unit, side, sums, mixed, *blocks):
        return pl.pallas_call(
            next_kernel,
            out_shape=[sums_shape, mixed_shape],
            input_output_aliases={2: 0, 3: 1},
            cost_estimate=cost(queries, len(blocks) * count, width),
            compiler_params=params,
            name="more_scores",
        )(unit, side, sums, mixed, *blocks)

    other = swap(packed)
    beside = across(packed)
    rounds = shards // 2
    moved = along(packed)
    moved, beside, other = lax.optimization_barrier((moved, beside, other))
    unit, side, sums, mixed = first(packed, other, beside)
    if rounds <= 4:
        for turn in range(1, rounds):
            beside = across(moved)
            ahead = along(moved) if turn + 1 < rounds else None
            held = moved
            if ahead is not None:
                moved, beside = lax.optimization_barrier((ahead, beside))
            sums, mixed = more(unit, side, sums, mixed, held, beside)
    else:

        def turn_body(turn, state):
            moved, sums, mixed = state
            beside = across(moved)
            ahead = along(moved)
            sums, mixed = more(unit, side, sums, mixed, moved, beside)
            return ahead, sums, mixed

        moved, sums, mixed = lax.fori_loop(1, rounds, turn_body, (moved, sums, mixed))
    other_sums, other_mixed = swap(sums[count:]), swap(mixed[count:])
    dup, out = pl.pallas_call(
        last_kernel,
        out_shape=[
            jax.ShapeDtypeStruct((1, count), f32),
            jax.ShapeDtypeStruct((count, width), f32),
        ],
        compiler_params=params,
        name="combine",
    )(sums[:count], mixed[:count], other_sums, other_mixed)
    return dup[0], out


def solution(mesh):
    placed = (
        P(("groups", "shard", "owner"), None),
        P(("groups", "shard", "owner"), None),
        P(("groups", "shard", "owner")),
    )
    return jax.shard_map(
        local,
        mesh=mesh,
        in_specs=placed,
        out_specs=(P(("groups", "shard", "owner")), P(("groups", "shard", "owner"), None)),
        check_vma=False,
    )
```

```python
import jax
import jax.numpy as jnp
from jax import lax
from jax.experimental import pallas as pl
from jax.experimental.pallas import tpu as pltpu
from jax.sharding import PartitionSpec as P

EXTRA = 8
VMEM = 48 * 1024 * 1024


def make_unit(rows):
    wide = rows.astype(jnp.float32)
    scale = lax.rsqrt(jnp.mean(wide * wide, axis=-1, keepdims=True) + 1e-06) / jnp.sqrt(
        jnp.float32(rows.shape[-1])
    )
    return (wide * scale).astype(jnp.bfloat16)


def diagonal(count):
    down = lax.broadcasted_iota(jnp.int32, (count, count), 0)
    return down == lax.broadcasted_iota(jnp.int32, (count, count), 1)


def as_row(column):
    return jnp.sum(jnp.where(diagonal(column.shape[0]), column, 0.0), axis=0, keepdims=True)


def as_column(row):
    return jnp.sum(jnp.where(diagonal(row.shape[1]), row, 0.0), axis=1, keepdims=True)


def pack_kernel(rows_ref, label_ref, rank_ref, front_ref, rear_ref):
    count, width = rows_ref.shape
    half = count // 2
    front_ref[:half, :] = rows_ref[:half, :]
    rear_ref[...] = rows_ref[half:, :]
    rank = rank_ref[...]
    high = lax.shift_right_logical(rank, 8)
    low = rank - lax.shift_left(high, 8)
    pieces = [piece.astype(jnp.float32) for piece in (label_ref[...], high, low)]
    pieces.append(jnp.zeros((1, width - 3 * count), jnp.float32))
    line = jnp.concatenate(pieces, axis=1)
    front_ref[half:, :] = jnp.broadcast_to(line, (EXTRA, width)).astype(jnp.bfloat16)


def labels_and_ranks(front):
    half = front.shape[0] - EXTRA
    count = 2 * half
    line = front[half:, :].astype(jnp.float32)[:1]
    label, high, low = (line[:, at * count : (at + 1) * count] for at in range(3))
    return label, high * 256.0 + low


def rows_of(blocks):
    pieces = []
    for front, rear in blocks:
        pieces += [front[: rear.shape[0], :], rear[...]]
    return jnp.concatenate(pieces, axis=0)


def score(unit, side, blocks):
    own_label, own_rank = side[:, 0:1], side[:, 1:2]
    keys = rows_of(blocks)
    sides = [labels_and_ranks(front) for front, _ in blocks]
    label = jnp.concatenate([item[0] for item in sides], axis=1)
    rank = jnp.concatenate([item[1] for item in sides], axis=1)
    cosine = lax.dot_general(
        unit, make_unit(keys), (((1,), (1,)), ((), ())), preferred_element_type=jnp.float32
    )
    weight = 1.0 / (1.0 + jnp.exp(-40.0 * (cosine - 0.05)))
    near = jnp.where((label == own_label) & (rank != own_rank), weight, 0.0)
    earlier = jnp.sum(jnp.where(rank < own_rank, near, 0.0), axis=1, keepdims=True)
    every = jnp.sum(near, axis=1, keepdims=True)
    mixed = jnp.dot(near.astype(jnp.bfloat16), keys, preferred_element_type=jnp.float32)
    return earlier, every, mixed


def pairs(refs):
    return [(refs[at], refs[at + 1]) for at in range(0, len(refs), 2)]


def first_kernel(*refs):
    ins, (unit_ref, side_ref, sums_ref, mixed_ref) = pairs(refs[:-4]), refs[-4:]
    own, other = ins[0], ins[1]
    count = 2 * own[1].shape[0]
    side_ref[...] = jnp.zeros_like(side_ref)
    sums_ref[...] = jnp.zeros_like(sums_ref)
    unit_ref[...] = make_unit(rows_of([own, other]))
    for at, (front, _) in enumerate((own, other)):
        here = slice(at * count, (at + 1) * count)
        label, rank = labels_and_ranks(front)
        side_ref[here, 0:1] = as_column(label)
        side_ref[here, 1:2] = as_column(rank)
    sums_ref[:, 0:1], sums_ref[:, 1:2], mixed_ref[...] = score(
        unit_ref[...], side_ref, [own] + ins[2:]
    )


def next_kernel(unit_ref, side_ref, old_sums_ref, old_mixed_ref, *refs):
    blocks, (sums_ref, mixed_ref) = pairs(refs[:-2]), refs[-2:]
    earlier, every, mixed = score(unit_ref[...], side_ref, blocks)
    sums_ref[...] = old_sums_ref[...]
    sums_ref[:, 0:1] += earlier
    sums_ref[:, 1:2] += every
    mixed_ref[...] = old_mixed_ref[...] + mixed


def last_kernel(sums_ref, mixed_ref, other_sums_ref, other_mixed_ref, dup_ref, out_ref):
    earlier = sums_ref[:, 0:1] + other_sums_ref[:, 0:1]
    every = sums_ref[:, 1:2] + other_sums_ref[:, 1:2]
    dup_ref[...] = as_row(jnp.log1p(earlier))
    out_ref[...] = (mixed_ref[...] + other_mixed_ref[...]) / jnp.sqrt(1.0 + every)


def cost(queries, keys, width):
    return pl.CostEstimate(
        flops=4 * queries * keys * width,
        bytes_accessed=8 * queries * width + 2 * keys * width,
        transcendentals=queries * keys,
    )


def local(embeddings, cluster_id, priority):
    count, width = embeddings.shape
    half = count // 2
    shards = lax.axis_size("shard")
    lanes = lax.axis_size("owner")
    rounds = shards // 2
    bf16, f32 = jnp.bfloat16, jnp.float32
    own = pl.pallas_call(
        pack_kernel,
        out_shape=[
            jax.ShapeDtypeStruct((half + EXTRA, width), bf16),
            jax.ShapeDtypeStruct((half, width), bf16),
        ],
        name="pack",
    )(embeddings, cluster_id.reshape(1, count), priority.reshape(1, count))

    def across(array):
        return lax.ppermute(array, "shard", [(at, at ^ 1) for at in range(shards)])

    def along(array, step=2):
        return lax.ppermute(array, "shard", [(at, (at + step) % shards) for at in range(shards)])

    def swap(array):
        return lax.ppermute(array, "owner", [(at, lanes - 1 - at) for at in range(lanes)])

    queries = 2 * count
    sums_shape = jax.ShapeDtypeStruct((queries, 128), f32)
    mixed_shape = jax.ShapeDtypeStruct((queries, width), f32)
    params = pltpu.CompilerParams(vmem_limit_bytes=VMEM)

    def first(*blocks):
        return pl.pallas_call(
            first_kernel,
            out_shape=[
                jax.ShapeDtypeStruct((queries, width), bf16),
                jax.ShapeDtypeStruct((queries, 128), f32),
                sums_shape,
                mixed_shape,
            ],
            cost_estimate=cost(queries, (len(blocks) - 1) * count, width),
            compiler_params=params,
            name="first_scores",
        )(*[piece for block in blocks for piece in block])

    def more(unit, side, sums, mixed, *blocks):
        return pl.pallas_call(
            next_kernel,
            out_shape=[sums_shape, mixed_shape],
            input_output_aliases={2: 0, 3: 1},
            cost_estimate=cost(queries, len(blocks) * count, width),
            compiler_params=params,
            name="more_scores",
        )(unit, side, sums, mixed, *[piece for block in blocks for piece in block])

    if rounds <= 4:
        moved, beside = ([], []), ([], [])
        for at in range(2):
            moved[at].append(along(own[at]))
            beside[at].append(across(own[at]))
            for turn in range(1, rounds):
                here, there = lax.optimization_barrier((moved[at][-1], beside[at][-1]))
                moved[at][-1], beside[at][-1] = here, there
                if turn + 1 < rounds:
                    moved[at].append(along(here))
                    beside[at].append(across(here))
                elif at == 0:
                    beside[at].append(across(here))
                else:
                    beside[at].append(along(beside[at][0], -2))
        other = [swap(piece) for piece in own]
        moved, beside = list(zip(*moved)), list(zip(*beside))
        unit, side, sums, mixed = first(own, other, beside[0])
        for turn in range(1, rounds - 1):
            sums, mixed = more(unit, side, sums, mixed, moved[turn - 1], beside[turn])
        sums, mixed = more(unit, side, sums, mixed, moved[-1])
        sums, mixed = more(unit, side, sums, mixed, beside[-1])
    else:
        other = [swap(piece) for piece in own]
        unit, side, sums, mixed = first(own, other, [across(piece) for piece in own])

        def turn_body(turn, state):
            moved, sums, mixed = state
            beside = [across(piece) for piece in moved]
            ahead = [along(piece) for piece in moved]
            sums, mixed = more(unit, side, sums, mixed, moved, beside)
            return ahead, sums, mixed

        start = ([along(piece) for piece in own], sums, mixed)
        _, sums, mixed = lax.fori_loop(1, rounds, turn_body, start)
    other_sums, other_mixed = swap(sums[count:]), swap(mixed[count:])
    dup, out = pl.pallas_call(
        last_kernel,
        out_shape=[
            jax.ShapeDtypeStruct((1, count), f32),
            jax.ShapeDtypeStruct((count, width), f32),
        ],
        compiler_params=params,
        name="combine",
    )(sums[:count], mixed[:count], other_sums, other_mixed)
    return dup[0], out


def solution(mesh):
    placed = (
        P(("groups", "shard", "owner"), None),
        P(("groups", "shard", "owner"), None),
        P(("groups", "shard", "owner")),
    )
    return jax.shard_map(
        local,
        mesh=mesh,
        in_specs=placed,
        out_specs=(P(("groups", "shard", "owner")), P(("groups", "shard", "owner"), None)),
        check_vma=False,
    )
```

```python
import jax
import jax.numpy as jnp
from jax import lax
from jax.experimental import pallas as pl
from jax.experimental.pallas import tpu as pltpu
from jax.sharding import PartitionSpec as P

EXTRA = 8
VMEM = 24 * 1024 * 1024


def make_unit(rows):
    wide = rows.astype(jnp.float32)
    scale = lax.rsqrt(jnp.mean(wide * wide, axis=-1, keepdims=True) + 1e-06) / jnp.sqrt(
        jnp.float32(rows.shape[-1])
    )
    return (wide * scale).astype(jnp.bfloat16)


def diagonal(count):
    down = lax.broadcasted_iota(jnp.int32, (count, count), 0)
    return down == lax.broadcasted_iota(jnp.int32, (count, count), 1)


def as_row(column):
    return jnp.sum(jnp.where(diagonal(column.shape[0]), column, 0.0), axis=0, keepdims=True)


def as_column(row):
    return jnp.sum(jnp.where(diagonal(row.shape[1]), row, 0.0), axis=1, keepdims=True)


def halves(value):
    high = value.astype(jnp.bfloat16)
    return high, (value - high.astype(jnp.float32)).astype(jnp.bfloat16)


def pack_kernel(rows_ref, label_ref, rank_ref, packed_ref):
    count, width = rows_ref.shape
    packed_ref[:count, :] = rows_ref[...]
    rank = rank_ref[...]
    high = lax.shift_right_logical(rank, 8)
    low = rank - lax.shift_left(high, 8)
    pieces = [piece.astype(jnp.float32) for piece in (label_ref[...], high, low)]
    pieces.append(jnp.zeros((1, width - 3 * count), jnp.float32))
    line = jnp.concatenate(pieces, axis=1)
    packed_ref[count:, :] = jnp.broadcast_to(line, (EXTRA, width)).astype(jnp.bfloat16)


def labels_and_ranks(block):
    count = block.shape[0] - EXTRA
    line = block[count:, :].astype(jnp.float32)[:1]
    label, high, low = (line[:, at * count : (at + 1) * count] for at in range(3))
    return label, high * 256.0 + low


def rows_of(blocks):
    return jnp.concatenate([block[: block.shape[0] - EXTRA, :] for block in blocks], axis=0)


def score(unit, side, blocks):
    own_label, own_rank = side[:, 0:1], side[:, 1:2]
    keys = rows_of(blocks)
    sides = [labels_and_ranks(block) for block in blocks]
    label = jnp.concatenate([item[0] for item in sides], axis=1)
    rank = jnp.concatenate([item[1] for item in sides], axis=1)
    cosine = lax.dot_general(
        unit, make_unit(keys), (((1,), (1,)), ((), ())), preferred_element_type=jnp.float32
    )
    weight = 1.0 / (1.0 + jnp.exp(-40.0 * (cosine - 0.05)))
    near = jnp.where((label == own_label) & (rank != own_rank), weight, 0.0)
    earlier = jnp.sum(jnp.where(rank < own_rank, near, 0.0), axis=1, keepdims=True)
    every = jnp.sum(near, axis=1, keepdims=True)
    mixed = jnp.dot(near.astype(jnp.bfloat16), keys, preferred_element_type=jnp.float32)
    return earlier, every, mixed


def first_kernel(own_ref, other_ref, *refs):
    blocks, (unit_ref, side_ref, sums_ref, mixed_ref) = refs[:-4], refs[-4:]
    count = own_ref.shape[0] - EXTRA
    side_ref[...] = jnp.zeros_like(side_ref)
    sums_ref[...] = jnp.zeros_like(sums_ref)
    unit_ref[...] = make_unit(rows_of([own_ref, other_ref]))
    for at, ref in enumerate((own_ref, other_ref)):
        here = slice(at * count, (at + 1) * count)
        label, rank = labels_and_ranks(ref)
        side_ref[here, 0:1] = as_column(label)
        side_ref[here, 1:2] = as_column(rank)
    sums_ref[:, 0:1], sums_ref[:, 1:2], mixed_ref[...] = score(
        unit_ref[...], side_ref, (own_ref,) + blocks
    )


def more_kernel(unit_ref, side_ref, old_sums_ref, old_mixed_ref, *refs):
    blocks, (sums_ref, mixed_ref) = refs[:-2], refs[-2:]
    earlier, every, mixed = score(unit_ref[...], side_ref, blocks)
    sums_ref[...] = old_sums_ref[...]
    sums_ref[:, 0:1] += earlier
    sums_ref[:, 1:2] += every
    mixed_ref[...] = old_mixed_ref[...] + mixed


def final_kernel(unit_ref, side_ref, old_sums_ref, old_mixed_ref, *refs):
    blocks, (keep_sums_ref, keep_ref, send_ref) = refs[:-3], refs[-3:]
    count, width = keep_ref.shape
    earlier, every, mixed = score(unit_ref[...], side_ref, blocks)
    earlier += old_sums_ref[:, 0:1]
    every += old_sums_ref[:, 1:2]
    mixed += old_mixed_ref[...]
    keep_sums_ref[...] = jnp.zeros_like(keep_sums_ref)
    keep_sums_ref[:, 0:1] = earlier[:count]
    keep_sums_ref[:, 1:2] = every[:count]
    keep_ref[...] = mixed[:count]
    send_ref[:count, :] = mixed[count:].astype(jnp.bfloat16)
    pieces = halves(as_row(earlier[count:])) + halves(as_row(every[count:]))
    pieces = [piece.astype(jnp.float32) for piece in pieces]
    pieces.append(jnp.zeros((1, width - 4 * count), jnp.float32))
    line = jnp.concatenate(pieces, axis=1)
    send_ref[count:, :] = jnp.broadcast_to(line, (EXTRA, width)).astype(jnp.bfloat16)


def combine_kernel(sums_ref, mixed_ref, got_ref, dup_ref, out_ref):
    count = mixed_ref.shape[0]
    line = got_ref[count:, :].astype(jnp.float32)[:1]
    parts = [line[:, at * count : (at + 1) * count] for at in range(4)]
    every = sums_ref[:, 1:2] + as_column(parts[2] + parts[3])
    dup_ref[...] = jnp.log1p(as_row(sums_ref[:, 0:1]) + parts[0] + parts[1])
    mixed = mixed_ref[...] + got_ref[:count, :].astype(jnp.float32)
    out_ref[...] = mixed / jnp.sqrt(1.0 + every)


def cost(queries, keys, width):
    return pl.CostEstimate(
        flops=400 * queries * keys * width,
        bytes_accessed=8 * queries * width + 2 * keys * width,
        transcendentals=100 * queries * keys,
    )


def local(embeddings, cluster_id, priority):
    count, width = embeddings.shape
    height = count + EXTRA
    shards = lax.axis_size("shard")
    lanes = lax.axis_size("owner")
    rounds = shards // 2
    queries = 2 * count
    bf16, f32 = jnp.bfloat16, jnp.float32
    params = pltpu.CompilerParams(vmem_limit_bytes=VMEM)

    def shape(*dims, dtype=f32):
        return jax.ShapeDtypeStruct(dims, dtype)

    ring = list(range(0, rounds, 2)) + list(range(1, rounds, 2))[::-1]

    def along(array, step):
        pairs = [
            (2 * ring[at] + side, 2 * ring[(at + step) % rounds] + side)
            for at in range(rounds)
            for side in range(2)
        ]
        return lax.ppermute(array, "shard", pairs)

    def across(array):
        return lax.ppermute(array, "shard", [(at, at ^ 1) for at in range(shards)])

    def swap(array):
        return lax.ppermute(array, "owner", [(at, lanes - 1 - at) for at in range(lanes)])

    def first(*blocks):
        return pl.pallas_call(
            first_kernel,
            out_shape=[
                shape(queries, width, dtype=bf16),
                shape(queries, 128),
                shape(queries, 128),
                shape(queries, width),
            ],
            cost_estimate=cost(queries, (len(blocks) - 1) * count, width),
            compiler_params=params,
            name="first_scores",
        )(*blocks)

    def more(unit, side, sums, mixed, *blocks):
        return pl.pallas_call(
            more_kernel,
            out_shape=[shape(queries, 128), shape(queries, width)],
            input_output_aliases={2: 0, 3: 1},
            cost_estimate=cost(queries, len(blocks) * count, width),
            compiler_params=params,
            name="more_scores",
        )(unit, side, sums, mixed, *blocks)

    def final(unit, side, sums, mixed, *blocks):
        return pl.pallas_call(
            final_kernel,
            out_shape=[
                shape(count, 128),
                shape(count, width),
                shape(height, width, dtype=bf16),
            ],
            cost_estimate=cost(queries, len(blocks) * count, width),
            compiler_params=params,
            name="final_scores",
        )(unit, side, sums, mixed, *blocks)

    own = pl.pallas_call(
        pack_kernel,
        out_shape=shape(height, width, dtype=bf16),
        compiler_params=params,
        name="pack",
    )(embeddings, cluster_id.reshape(1, count), priority.reshape(1, count))

    moved, beside = along(own, 1), across(own)
    other = swap(own)
    if rounds == 4:
        moved, beside, other = lax.optimization_barrier((moved, beside, other))
        corner = along(beside, -1)
        moved_1, beside_1 = along(moved, 1), across(moved)
        state = first(own, other, beside)
        unit, side = state[:2]
        moved_1, beside_1 = lax.optimization_barrier((moved_1, beside_1))
        moved_2, beside_2 = along(moved_1, 1), across(moved_1)
        sums, mixed = more(*state, moved, moved_1, beside_1)
        sums, mixed = more(unit, side, sums, mixed, corner)
        moved, beside = moved_2, beside_2
    else:
        unit, side, sums, mixed = first(own, other, beside)

        def turn(at, state):
            moved, sums, mixed = state
            ahead, beside = along(moved, 1), across(moved)
            sums, mixed = more(unit, side, sums, mixed, moved, beside)
            return ahead, sums, mixed

        moved, sums, mixed = lax.fori_loop(1, rounds - 1, turn, (moved, sums, mixed))
        beside = across(moved)
    keep_sums, keep, send = final(unit, side, sums, mixed, moved, beside)
    dup, out = pl.pallas_call(
        combine_kernel,
        out_shape=[shape(1, count), shape(count, width)],
        compiler_params=params,
        name="combine",
    )(keep_sums, keep, swap(send))
    return dup[0], out


def solution(mesh):
    placed = (
        P(("groups", "shard", "owner"), None),
        P(("groups", "shard", "owner"), None),
        P(("groups", "shard", "owner")),
    )
    return jax.shard_map(
        local,
        mesh=mesh,
        in_specs=placed,
        out_specs=(P(("groups", "shard", "owner")), P(("groups", "shard", "owner"), None)),
        check_vma=False,
    )
```

```python
import jax
import jax.numpy as jnp
from jax import lax
from jax.experimental import pallas as pl
from jax.experimental.pallas import tpu as pltpu
from jax.sharding import PartitionSpec as P

EXTRA = 8
VMEM = 24 * 1024 * 1024


def make_unit(rows):
    wide = rows.astype(jnp.float32)
    scale = lax.rsqrt(jnp.mean(wide * wide, axis=-1, keepdims=True) + 1e-06) / jnp.sqrt(
        jnp.float32(rows.shape[-1])
    )
    return (wide * scale).astype(jnp.bfloat16)


def diagonal(count):
    down = lax.broadcasted_iota(jnp.int32, (count, count), 0)
    return down == lax.broadcasted_iota(jnp.int32, (count, count), 1)


def as_row(column):
    return jnp.sum(jnp.where(diagonal(column.shape[0]), column, 0.0), axis=0, keepdims=True)


def as_column(row):
    return jnp.sum(jnp.where(diagonal(row.shape[1]), row, 0.0), axis=1, keepdims=True)


def halves(value):
    high = value.astype(jnp.bfloat16)
    return high, (value - high.astype(jnp.float32)).astype(jnp.bfloat16)


def pack_kernel(rows_ref, label_ref, rank_ref, packed_ref):
    count, width = rows_ref.shape
    packed_ref[:count, :] = rows_ref[...]
    rank = rank_ref[...]
    high = lax.shift_right_logical(rank, 8)
    low = rank - lax.shift_left(high, 8)
    pieces = [piece.astype(jnp.float32) for piece in (label_ref[...], high, low)]
    pieces.append(jnp.zeros((1, width - 3 * count), jnp.float32))
    line = jnp.concatenate(pieces, axis=1)
    packed_ref[count:, :] = jnp.broadcast_to(line, (EXTRA, width)).astype(jnp.bfloat16)


def labels_and_ranks(block):
    count = block.shape[0] - EXTRA
    line = block[count:, :].astype(jnp.float32)[:1]
    label, high, low = (line[:, at * count : (at + 1) * count] for at in range(3))
    return label, high * 256.0 + low


def rows_of(blocks):
    return jnp.concatenate([block[: block.shape[0] - EXTRA, :] for block in blocks], axis=0)


def score(unit, side, blocks):
    own_label, own_rank = side[:, 0:1], side[:, 1:2]
    keys = rows_of(blocks)
    sides = [labels_and_ranks(block) for block in blocks]
    label = jnp.concatenate([item[0] for item in sides], axis=1)
    rank = jnp.concatenate([item[1] for item in sides], axis=1)
    cosine = lax.dot_general(
        unit, make_unit(keys), (((1,), (1,)), ((), ())), preferred_element_type=jnp.float32
    )
    weight = 1.0 / (1.0 + jnp.exp(-40.0 * (cosine - 0.05)))
    near = jnp.where((label == own_label) & (rank != own_rank), weight, 0.0)
    earlier = jnp.sum(jnp.where(rank < own_rank, near, 0.0), axis=1, keepdims=True)
    every = jnp.sum(near, axis=1, keepdims=True)
    mixed = jnp.dot(near.astype(jnp.bfloat16), keys, preferred_element_type=jnp.float32)
    return earlier, every, mixed


def first_kernel(own_ref, other_ref, *refs):
    blocks, (unit_ref, side_ref, sums_ref, mixed_ref) = refs[:-4], refs[-4:]
    count = own_ref.shape[0] - EXTRA
    side_ref[...] = jnp.zeros_like(side_ref)
    sums_ref[...] = jnp.zeros_like(sums_ref)
    unit_ref[...] = make_unit(rows_of([own_ref, other_ref]))
    for at, ref in enumerate((own_ref, other_ref)):
        here = slice(at * count, (at + 1) * count)
        label, rank = labels_and_ranks(ref)
        side_ref[here, 0:1] = as_column(label)
        side_ref[here, 1:2] = as_column(rank)
    sums_ref[:, 0:1], sums_ref[:, 1:2], mixed_ref[...] = score(
        unit_ref[...], side_ref, (own_ref,) + blocks
    )


def more_kernel(unit_ref, side_ref, old_sums_ref, old_mixed_ref, *refs):
    blocks, (sums_ref, mixed_ref) = refs[:-2], refs[-2:]
    earlier, every, mixed = score(unit_ref[...], side_ref, blocks)
    sums_ref[...] = old_sums_ref[...]
    sums_ref[:, 0:1] += earlier
    sums_ref[:, 1:2] += every
    mixed_ref[...] = old_mixed_ref[...] + mixed


def final_kernel(unit_ref, side_ref, old_sums_ref, old_mixed_ref, *refs):
    blocks, (keep_sums_ref, keep_ref, send_ref) = refs[:-3], refs[-3:]
    count, width = keep_ref.shape
    earlier, every, mixed = score(unit_ref[...], side_ref, blocks)
    earlier += old_sums_ref[:, 0:1]
    every += old_sums_ref[:, 1:2]
    mixed += old_mixed_ref[...]
    keep_sums_ref[...] = jnp.zeros_like(keep_sums_ref)
    keep_sums_ref[:, 0:1] = earlier[:count]
    keep_sums_ref[:, 1:2] = every[:count]
    keep_ref[...] = mixed[:count]
    send_ref[:count, :] = mixed[count:].astype(jnp.bfloat16)
    pieces = halves(as_row(earlier[count:])) + halves(as_row(every[count:]))
    pieces = [piece.astype(jnp.float32) for piece in pieces]
    pieces.append(jnp.zeros((1, width - 4 * count), jnp.float32))
    line = jnp.concatenate(pieces, axis=1)
    send_ref[count:, :] = jnp.broadcast_to(line, (EXTRA, width)).astype(jnp.bfloat16)


def combine_kernel(sums_ref, mixed_ref, got_ref, dup_ref, out_ref):
    count = mixed_ref.shape[0]
    line = got_ref[count:, :].astype(jnp.float32)[:1]
    parts = [line[:, at * count : (at + 1) * count] for at in range(4)]
    every = sums_ref[:, 1:2] + as_column(parts[2] + parts[3])
    dup_ref[...] = jnp.log1p(as_row(sums_ref[:, 0:1]) + parts[0] + parts[1])
    mixed = mixed_ref[...] + got_ref[:count, :].astype(jnp.float32)
    out_ref[...] = mixed / jnp.sqrt(1.0 + every)


def cost(queries, keys, width):
    return pl.CostEstimate(
        flops=400 * queries * keys * width,
        bytes_accessed=8 * queries * width + 2 * keys * width,
        transcendentals=100 * queries * keys,
    )


def local(embeddings, cluster_id, priority):
    count, width = embeddings.shape
    height = count + EXTRA
    shards = lax.axis_size("shard")
    lanes = lax.axis_size("owner")
    rounds = shards // 2
    queries = 2 * count
    bf16, f32 = jnp.bfloat16, jnp.float32
    params = pltpu.CompilerParams(vmem_limit_bytes=VMEM)

    def shape(*dims, dtype=f32):
        return jax.ShapeDtypeStruct(dims, dtype)

    ring = list(range(0, rounds, 2)) + list(range(1, rounds, 2))[::-1]

    def along(array, step):
        pairs = [
            (2 * ring[at] + side, 2 * ring[(at + step) % rounds] + side)
            for at in range(rounds)
            for side in range(2)
        ]
        return lax.ppermute(array, "shard", pairs)

    def across(array):
        return lax.ppermute(array, "shard", [(at, at ^ 1) for at in range(shards)])

    def swap(array):
        return lax.ppermute(array, "owner", [(at, lanes - 1 - at) for at in range(lanes)])

    def first(*blocks):
        return pl.pallas_call(
            first_kernel,
            out_shape=[
                shape(queries, width, dtype=bf16),
                shape(queries, 128),
                shape(queries, 128),
                shape(queries, width),
            ],
            cost_estimate=cost(queries, (len(blocks) - 1) * count, width),
            compiler_params=params,
            name="first_scores",
        )(*blocks)

    def more(unit, side, sums, mixed, *blocks):
        return pl.pallas_call(
            more_kernel,
            out_shape=[shape(queries, 128), shape(queries, width)],
            input_output_aliases={2: 0, 3: 1},
            cost_estimate=cost(queries, len(blocks) * count, width),
            compiler_params=params,
            name="more_scores",
        )(unit, side, sums, mixed, *blocks)

    def final(unit, side, sums, mixed, *blocks):
        return pl.pallas_call(
            final_kernel,
            out_shape=[
                shape(count, 128),
                shape(count, width),
                shape(height, width, dtype=bf16),
            ],
            cost_estimate=cost(queries, len(blocks) * count, width),
            compiler_params=params,
            name="final_scores",
        )(unit, side, sums, mixed, *blocks)

    own = pl.pallas_call(
        pack_kernel,
        out_shape=shape(height, width, dtype=bf16),
        compiler_params=params,
        name="pack",
    )(embeddings, cluster_id.reshape(1, count), priority.reshape(1, count))

    moved, beside = along(own, 1), across(own)
    other = swap(own)
    if rounds == 4:
        ahead = along(own, -1)
        moved, beside, other = lax.optimization_barrier((moved, beside, other))
        opposite = along(moved, 1)
        moved_beside = across(moved)
        ahead_beside = along(beside, -1)
        state = first(own, other, beside, ahead)
        unit, side = state[:2]
        opposite, moved_beside = lax.optimization_barrier((opposite, moved_beside))
        last = [across(opposite)]
        sums, mixed = more(*state, moved, moved_beside)
        sums, mixed = more(unit, side, sums, mixed, opposite, ahead_beside)
    else:
        unit, side, sums, mixed = first(own, other, beside)

        def turn(at, state):
            moved, sums, mixed = state
            ahead, beside = along(moved, 1), across(moved)
            sums, mixed = more(unit, side, sums, mixed, moved, beside)
            return ahead, sums, mixed

        moved, sums, mixed = lax.fori_loop(1, rounds - 1, turn, (moved, sums, mixed))
        last = [moved, across(moved)]
    keep_sums, keep, send = final(unit, side, sums, mixed, *last)
    dup, out = pl.pallas_call(
        combine_kernel,
        out_shape=[shape(1, count), shape(count, width)],
        compiler_params=params,
        name="combine",
    )(keep_sums, keep, swap(send))
    return dup[0], out


def solution(mesh):
    placed = (
        P(("groups", "shard", "owner"), None),
        P(("groups", "shard", "owner"), None),
        P(("groups", "shard", "owner")),
    )
    return jax.shard_map(
        local,
        mesh=mesh,
        in_specs=placed,
        out_specs=(P(("groups", "shard", "owner")), P(("groups", "shard", "owner"), None)),
        check_vma=False,
    )
```

```python
import jax
import jax.numpy as jnp
from jax import lax
from jax.experimental import pallas as pl
from jax.experimental.pallas import tpu as pltpu
from jax.sharding import PartitionSpec as P

EXTRA = 8
VMEM = 24 * 1024 * 1024


def make_unit(rows):
    wide = rows.astype(jnp.float32)
    scale = lax.rsqrt(jnp.mean(wide * wide, axis=-1, keepdims=True) + 1e-06) / jnp.sqrt(
        jnp.float32(rows.shape[-1])
    )
    return (wide * scale).astype(jnp.bfloat16)


def diagonal(count):
    down = lax.broadcasted_iota(jnp.int32, (count, count), 0)
    return down == lax.broadcasted_iota(jnp.int32, (count, count), 1)


def as_row(column):
    return jnp.sum(jnp.where(diagonal(column.shape[0]), column, 0.0), axis=0, keepdims=True)


def as_column(row):
    return jnp.sum(jnp.where(diagonal(row.shape[1]), row, 0.0), axis=1, keepdims=True)


def halves(value):
    high = value.astype(jnp.bfloat16)
    return high, (value - high.astype(jnp.float32)).astype(jnp.bfloat16)


def pack_kernel(rows_ref, label_ref, rank_ref, packed_ref):
    count, width = rows_ref.shape
    packed_ref[:count, :] = rows_ref[...]
    rank = rank_ref[...]
    high = lax.shift_right_logical(rank, 8)
    low = rank - lax.shift_left(high, 8)
    pieces = [piece.astype(jnp.float32) for piece in (label_ref[...], high, low)]
    pieces.append(jnp.zeros((1, width - 3 * count), jnp.float32))
    line = jnp.concatenate(pieces, axis=1)
    packed_ref[count:, :] = jnp.broadcast_to(line, (EXTRA, width)).astype(jnp.bfloat16)


def labels_and_ranks(block):
    count = block.shape[0] - EXTRA
    line = block[count:, :].astype(jnp.float32)[:1]
    label, high, low = (line[:, at * count : (at + 1) * count] for at in range(3))
    return label, high * 256.0 + low


def rows_of(blocks):
    return jnp.concatenate([block[: block.shape[0] - EXTRA, :] for block in blocks], axis=0)


def score(unit, side, blocks):
    own_label, own_rank = side[:, 0:1], side[:, 1:2]
    keys = rows_of(blocks)
    sides = [labels_and_ranks(block) for block in blocks]
    label = jnp.concatenate([item[0] for item in sides], axis=1)
    rank = jnp.concatenate([item[1] for item in sides], axis=1)
    cosine = lax.dot_general(
        unit, make_unit(keys), (((1,), (1,)), ((), ())), preferred_element_type=jnp.float32
    )
    weight = 1.0 / (1.0 + jnp.exp(-40.0 * (cosine - 0.05)))
    near = jnp.where((label == own_label) & (rank != own_rank), weight, 0.0)
    earlier = jnp.sum(jnp.where(rank < own_rank, near, 0.0), axis=1, keepdims=True)
    every = jnp.sum(near, axis=1, keepdims=True)
    mixed = jnp.dot(near.astype(jnp.bfloat16), keys, preferred_element_type=jnp.float32)
    return earlier, every, mixed


def first_kernel(own_ref, other_ref, *refs):
    blocks, (unit_ref, side_ref, sums_ref, mixed_ref) = refs[:-4], refs[-4:]
    count = own_ref.shape[0] - EXTRA
    side_ref[...] = jnp.zeros_like(side_ref)
    sums_ref[...] = jnp.zeros_like(sums_ref)
    unit_ref[...] = make_unit(rows_of([own_ref, other_ref]))
    for at, ref in enumerate((own_ref, other_ref)):
        here = slice(at * count, (at + 1) * count)
        label, rank = labels_and_ranks(ref)
        side_ref[here, 0:1] = as_column(label)
        side_ref[here, 1:2] = as_column(rank)
    sums_ref[:, 0:1], sums_ref[:, 1:2], mixed_ref[...] = score(
        unit_ref[...], side_ref, (own_ref,) + blocks
    )


def more_kernel(unit_ref, side_ref, old_sums_ref, old_mixed_ref, *refs):
    blocks, (sums_ref, mixed_ref) = refs[:-2], refs[-2:]
    earlier, every, mixed = score(unit_ref[...], side_ref, blocks)
    sums_ref[...] = old_sums_ref[...]
    sums_ref[:, 0:1] += earlier
    sums_ref[:, 1:2] += every
    mixed_ref[...] = old_mixed_ref[...] + mixed


def final_kernel(unit_ref, side_ref, old_sums_ref, old_mixed_ref, *refs):
    blocks, (keep_sums_ref, keep_ref, send_ref) = refs[:-3], refs[-3:]
    count, width = keep_ref.shape
    earlier, every, mixed = score(unit_ref[...], side_ref, blocks)
    earlier += old_sums_ref[:, 0:1]
    every += old_sums_ref[:, 1:2]
    mixed += old_mixed_ref[...]
    keep_sums_ref[...] = jnp.zeros_like(keep_sums_ref)
    keep_sums_ref[:, 0:1] = earlier[:count]
    keep_sums_ref[:, 1:2] = every[:count]
    keep_ref[...] = mixed[:count]
    send_ref[:count, :] = mixed[count:].astype(jnp.bfloat16)
    pieces = halves(as_row(earlier[count:])) + halves(as_row(every[count:]))
    pieces = [piece.astype(jnp.float32) for piece in pieces]
    pieces.append(jnp.zeros((1, width - 4 * count), jnp.float32))
    line = jnp.concatenate(pieces, axis=1)
    send_ref[count:, :] = jnp.broadcast_to(line, (EXTRA, width)).astype(jnp.bfloat16)


def combine_kernel(sums_ref, mixed_ref, got_ref, dup_ref, out_ref):
    count = mixed_ref.shape[0]
    line = got_ref[count:, :].astype(jnp.float32)[:1]
    parts = [line[:, at * count : (at + 1) * count] for at in range(4)]
    every = sums_ref[:, 1:2] + as_column(parts[2] + parts[3])
    dup_ref[...] = jnp.log1p(as_row(sums_ref[:, 0:1]) + parts[0] + parts[1])
    mixed = mixed_ref[...] + got_ref[:count, :].astype(jnp.float32)
    out_ref[...] = mixed / jnp.sqrt(1.0 + every)


def cost(queries, keys, width):
    return pl.CostEstimate(
        flops=400 * queries * keys * width,
        bytes_accessed=8 * queries * width + 2 * keys * width,
        transcendentals=100 * queries * keys,
    )


def local(embeddings, cluster_id, priority):
    count, width = embeddings.shape
    height = count + EXTRA
    shards = lax.axis_size("shard")
    lanes = lax.axis_size("owner")
    rounds = shards // 2
    queries = 2 * count
    bf16, f32 = jnp.bfloat16, jnp.float32
    params = pltpu.CompilerParams(vmem_limit_bytes=VMEM)

    def shape(*dims, dtype=f32):
        return jax.ShapeDtypeStruct(dims, dtype)

    ring = list(range(0, rounds, 2)) + list(range(1, rounds, 2))[::-1]

    def along(array, step):
        pairs = [
            (2 * ring[at] + side, 2 * ring[(at + step) % rounds] + side)
            for at in range(rounds)
            for side in range(2)
        ]
        return lax.ppermute(array, "shard", pairs)

    def across(array):
        return lax.ppermute(array, "shard", [(at, at ^ 1) for at in range(shards)])

    def corner(beside, ahead):
        pairs = []
        for at in range(rounds):
            for side in range(2):
                here = 2 * ring[at] + side
                pairs.append((here * lanes, (2 * ring[at - 1] + side) * lanes))
                pairs += [(here * lanes + lane, (here ^ 1) * lanes + lane) for lane in range(1, lanes)]
        source = jnp.where(lax.axis_index("owner") == 0, beside, ahead)
        return lax.ppermute(source, ("shard", "owner"), pairs)

    def swap(array):
        return lax.ppermute(array, "owner", [(at, lanes - 1 - at) for at in range(lanes)])

    def first(*blocks):
        return pl.pallas_call(
            first_kernel,
            out_shape=[
                shape(queries, width, dtype=bf16),
                shape(queries, 128),
                shape(queries, 128),
                shape(queries, width),
            ],
            cost_estimate=cost(queries, (len(blocks) - 1) * count, width),
            compiler_params=params,
            name="first_scores",
        )(*blocks)

    def more(unit, side, sums, mixed, *blocks):
        return pl.pallas_call(
            more_kernel,
            out_shape=[shape(queries, 128), shape(queries, width)],
            input_output_aliases={2: 0, 3: 1},
            cost_estimate=cost(queries, len(blocks) * count, width),
            compiler_params=params,
            name="more_scores",
        )(unit, side, sums, mixed, *blocks)

    def final(unit, side, sums, mixed, *blocks):
        return pl.pallas_call(
            final_kernel,
            out_shape=[
                shape(count, 128),
                shape(count, width),
                shape(height, width, dtype=bf16),
            ],
            cost_estimate=cost(queries, len(blocks) * count, width),
            compiler_params=params,
            name="final_scores",
        )(unit, side, sums, mixed, *blocks)

    own = pl.pallas_call(
        pack_kernel,
        out_shape=shape(height, width, dtype=bf16),
        compiler_params=params,
        name="pack",
    )(embeddings, cluster_id.reshape(1, count), priority.reshape(1, count))

    moved, beside = along(own, 1), across(own)
    other = swap(own)
    if rounds == 4:
        ahead = along(own, -1)
        other, beside, moved = lax.optimization_barrier((other, beside, moved))
        opposite = along(moved, 1)
        moved_beside = across(moved)
        ahead_beside = corner(beside, ahead)
        state = first(own, other, beside, ahead)
        unit, side = state[:2]
        moved_beside, opposite = lax.optimization_barrier((moved_beside, opposite))
        last = [across(opposite)]
        sums, mixed = more(*state, moved, moved_beside)
        sums, mixed = more(unit, side, sums, mixed, opposite, ahead_beside)
    else:
        unit, side, sums, mixed = first(own, other, beside)

        def turn(at, state):
            moved, sums, mixed = state
            ahead, beside = along(moved, 1), across(moved)
            sums, mixed = more(unit, side, sums, mixed, moved, beside)
            return ahead, sums, mixed

        moved, sums, mixed = lax.fori_loop(1, rounds - 1, turn, (moved, sums, mixed))
        last = [moved, across(moved)]
    keep_sums, keep, send = final(unit, side, sums, mixed, *last)
    dup, out = pl.pallas_call(
        combine_kernel,
        out_shape=[shape(1, count), shape(count, width)],
        compiler_params=params,
        name="combine",
    )(keep_sums, keep, swap(send))
    return dup[0], out


def solution(mesh):
    placed = (
        P(("groups", "shard", "owner"), None),
        P(("groups", "shard", "owner"), None),
        P(("groups", "shard", "owner")),
    )
    return jax.shard_map(
        local,
        mesh=mesh,
        in_specs=placed,
        out_specs=(P(("groups", "shard", "owner")), P(("groups", "shard", "owner"), None)),
        check_vma=False,
    )
```

```python
import jax
import jax.numpy as jnp
from jax import lax
from jax.experimental import pallas as pl
from jax.experimental.pallas import tpu as pltpu
from jax.sharding import PartitionSpec as P

EXTRA = 8
VMEM = 24 * 1024 * 1024


def make_unit(rows):
    wide = rows.astype(jnp.float32)
    scale = lax.rsqrt(jnp.mean(wide * wide, axis=-1, keepdims=True) + 1e-06) / jnp.sqrt(
        jnp.float32(rows.shape[-1])
    )
    return (wide * scale).astype(jnp.bfloat16)


def diagonal(count):
    down = lax.broadcasted_iota(jnp.int32, (count, count), 0)
    return down == lax.broadcasted_iota(jnp.int32, (count, count), 1)


def as_row(column):
    return jnp.sum(jnp.where(diagonal(column.shape[0]), column, 0.0), axis=0, keepdims=True)


def as_column(row):
    return jnp.sum(jnp.where(diagonal(row.shape[1]), row, 0.0), axis=1, keepdims=True)


def halves(value):
    high = value.astype(jnp.bfloat16)
    return high, (value - high.astype(jnp.float32)).astype(jnp.bfloat16)


def pack_kernel(rows_ref, label_ref, rank_ref, packed_ref):
    count, width = rows_ref.shape
    packed_ref[:count, :] = rows_ref[...]
    rank = rank_ref[...]
    high = lax.shift_right_logical(rank, 8)
    low = rank - lax.shift_left(high, 8)
    pieces = [piece.astype(jnp.float32) for piece in (label_ref[...], high, low)]
    pieces.append(jnp.zeros((1, width - 3 * count), jnp.float32))
    line = jnp.concatenate(pieces, axis=1)
    packed_ref[count:, :] = jnp.broadcast_to(line, (EXTRA, width)).astype(jnp.bfloat16)


def labels_and_ranks(block):
    count = block.shape[0] - EXTRA
    line = block[count:, :].astype(jnp.float32)[:1]
    label, high, low = (line[:, at * count : (at + 1) * count] for at in range(3))
    return label, high * 256.0 + low


def rows_of(blocks):
    return jnp.concatenate([block[: block.shape[0] - EXTRA, :] for block in blocks], axis=0)


def score(unit, side, blocks):
    own_label, own_rank = side[:, 0:1], side[:, 1:2]
    keys = rows_of(blocks)
    sides = [labels_and_ranks(block) for block in blocks]
    label = jnp.concatenate([item[0] for item in sides], axis=1)
    rank = jnp.concatenate([item[1] for item in sides], axis=1)
    cosine = lax.dot_general(
        unit, make_unit(keys), (((1,), (1,)), ((), ())), preferred_element_type=jnp.float32
    )
    weight = 1.0 / (1.0 + jnp.exp(-40.0 * (cosine - 0.05)))
    near = jnp.where((label == own_label) & (rank != own_rank), weight, 0.0)
    earlier = jnp.sum(jnp.where(rank < own_rank, near, 0.0), axis=1, keepdims=True)
    every = jnp.sum(near, axis=1, keepdims=True)
    mixed = jnp.dot(near.astype(jnp.bfloat16), keys, preferred_element_type=jnp.float32)
    return earlier, every, mixed


def first_kernel(own_ref, other_ref, *refs):
    blocks, (unit_ref, side_ref, sums_ref, mixed_ref) = refs[:-4], refs[-4:]
    count = own_ref.shape[0] - EXTRA
    side_ref[...] = jnp.zeros_like(side_ref)
    sums_ref[...] = jnp.zeros_like(sums_ref)
    unit_ref[...] = make_unit(rows_of([own_ref, other_ref]))
    for at, ref in enumerate((own_ref, other_ref)):
        here = slice(at * count, (at + 1) * count)
        label, rank = labels_and_ranks(ref)
        side_ref[here, 0:1] = as_column(label)
        side_ref[here, 1:2] = as_column(rank)
    sums_ref[:, 0:1], sums_ref[:, 1:2], mixed_ref[...] = score(
        unit_ref[...], side_ref, (own_ref,) + blocks
    )


def more_kernel(unit_ref, side_ref, old_sums_ref, old_mixed_ref, *refs):
    blocks, (sums_ref, mixed_ref) = refs[:-2], refs[-2:]
    earlier, every, mixed = score(unit_ref[...], side_ref, blocks)
    sums_ref[...] = old_sums_ref[...]
    sums_ref[:, 0:1] += earlier
    sums_ref[:, 1:2] += every
    mixed_ref[...] = old_mixed_ref[...] + mixed


def final_kernel(unit_ref, side_ref, old_sums_ref, old_mixed_ref, *refs):
    blocks, (keep_sums_ref, keep_ref, send_ref) = refs[:-3], refs[-3:]
    count, width = keep_ref.shape
    earlier, every, mixed = score(unit_ref[...], side_ref, blocks)
    earlier += old_sums_ref[:, 0:1]
    every += old_sums_ref[:, 1:2]
    mixed += old_mixed_ref[...]
    keep_sums_ref[...] = jnp.zeros_like(keep_sums_ref)
    keep_sums_ref[:, 0:1] = earlier[:count]
    keep_sums_ref[:, 1:2] = every[:count]
    keep_ref[...] = mixed[:count]
    send_ref[:count, :] = mixed[count:].astype(jnp.bfloat16)
    pieces = halves(as_row(earlier[count:])) + halves(as_row(every[count:]))
    pieces = [piece.astype(jnp.float32) for piece in pieces]
    pieces.append(jnp.zeros((1, width - 4 * count), jnp.float32))
    line = jnp.concatenate(pieces, axis=1)
    send_ref[count:, :] = jnp.broadcast_to(line, (EXTRA, width)).astype(jnp.bfloat16)


def combine_kernel(sums_ref, mixed_ref, got_ref, dup_ref, out_ref):
    count = mixed_ref.shape[0]
    line = got_ref[count:, :].astype(jnp.float32)[:1]
    parts = [line[:, at * count : (at + 1) * count] for at in range(4)]
    every = sums_ref[:, 1:2] + as_column(parts[2] + parts[3])
    dup_ref[...] = jnp.log1p(as_row(sums_ref[:, 0:1]) + parts[0] + parts[1])
    mixed = mixed_ref[...] + got_ref[:count, :].astype(jnp.float32)
    out_ref[...] = mixed / jnp.sqrt(1.0 + every)


def cost(queries, keys, width):
    return pl.CostEstimate(
        flops=400 * queries * keys * width,
        bytes_accessed=8 * queries * width + 2 * keys * width,
        transcendentals=100 * queries * keys,
    )


def local(embeddings, cluster_id, priority):
    count, width = embeddings.shape
    height = count + EXTRA
    shards = lax.axis_size("shard")
    lanes = lax.axis_size("owner")
    rounds = shards // 2
    queries = 2 * count
    bf16, f32 = jnp.bfloat16, jnp.float32
    params = pltpu.CompilerParams(vmem_limit_bytes=VMEM)

    def shape(*dims, dtype=f32):
        return jax.ShapeDtypeStruct(dims, dtype)

    ring = list(range(0, rounds, 2)) + list(range(1, rounds, 2))[::-1]

    def along(array, step):
        pairs = [
            (2 * ring[at] + side, 2 * ring[(at + step) % rounds] + side)
            for at in range(rounds)
            for side in range(2)
        ]
        return lax.ppermute(array, "shard", pairs)

    def across(array):
        return lax.ppermute(array, "shard", [(at, at ^ 1) for at in range(shards)])

    def swap(array):
        return lax.ppermute(array, "owner", [(at, lanes - 1 - at) for at in range(lanes)])

    def first(*blocks):
        return pl.pallas_call(
            first_kernel,
            out_shape=[
                shape(queries, width, dtype=bf16),
                shape(queries, 128),
                shape(queries, 128),
                shape(queries, width),
            ],
            cost_estimate=cost(queries, (len(blocks) - 1) * count, width),
            compiler_params=params,
            name="first_scores",
        )(*blocks)

    def more(unit, side, sums, mixed, *blocks):
        return pl.pallas_call(
            more_kernel,
            out_shape=[shape(queries, 128), shape(queries, width)],
            input_output_aliases={2: 0, 3: 1},
            cost_estimate=cost(queries, len(blocks) * count, width),
            compiler_params=params,
            name="more_scores",
        )(unit, side, sums, mixed, *blocks)

    def final(unit, side, sums, mixed, *blocks):
        return pl.pallas_call(
            final_kernel,
            out_shape=[
                shape(count, 128),
                shape(count, width),
                shape(height, width, dtype=bf16),
            ],
            cost_estimate=cost(queries, len(blocks) * count, width),
            compiler_params=params,
            name="final_scores",
        )(unit, side, sums, mixed, *blocks)

    own = pl.pallas_call(
        pack_kernel,
        out_shape=shape(height, width, dtype=bf16),
        compiler_params=params,
        name="pack",
    )(embeddings, cluster_id.reshape(1, count), priority.reshape(1, count))

    moved, other, guest = along(own, 1), swap(own), across(own)
    if rounds == 4:
        ahead = along(own, -1)
        other, guest, moved = lax.optimization_barrier((other, guest, moved))
        last = along(moved, 1)
        far = swap(moved)
        unit, side, sums, mixed = first(own, guest, other, moved)
        sums, far, last = lax.optimization_barrier((sums, far, last))
        blocks = [far, ahead, swap(ahead), last]
    else:
        unit, side, sums, mixed = first(own, guest, other)

        def turn(at, state):
            moved, sums, mixed = state
            ahead = along(moved, 1)
            sums, mixed = more(unit, side, sums, mixed, moved, swap(moved))
            return ahead, sums, mixed

        last, sums, mixed = lax.fori_loop(1, rounds - 1, turn, (moved, sums, mixed))
        blocks = [last]
    sums, mixed = more(unit, side, sums, mixed, *blocks)
    keep_sums, keep, send = final(unit, side, sums, mixed, swap(last))
    dup, out = pl.pallas_call(
        combine_kernel,
        out_shape=[shape(1, count), shape(count, width)],
        compiler_params=params,
        name="combine",
    )(keep_sums, keep, across(send))
    return dup[0], out


def solution(mesh):
    placed = (
        P(("groups", "shard", "owner"), None),
        P(("groups", "shard", "owner"), None),
        P(("groups", "shard", "owner")),
    )
    return jax.shard_map(
        local,
        mesh=mesh,
        in_specs=placed,
        out_specs=(P(("groups", "shard", "owner")), P(("groups", "shard", "owner"), None)),
        check_vma=False,
    )
```

```python
import jax
import jax.numpy as jnp
from jax import lax
from jax.experimental import pallas as pl
from jax.experimental.pallas import tpu as pltpu
from jax.sharding import PartitionSpec as P

EXTRA = 8
VMEM = 24 * 1024 * 1024


def make_unit(rows):
    wide = rows.astype(jnp.float32)
    scale = lax.rsqrt(jnp.mean(wide * wide, axis=-1, keepdims=True) + 1e-06) / jnp.sqrt(
        jnp.float32(rows.shape[-1])
    )
    return (wide * scale).astype(jnp.bfloat16)


def diagonal(count):
    down = lax.broadcasted_iota(jnp.int32, (count, count), 0)
    return down == lax.broadcasted_iota(jnp.int32, (count, count), 1)


def as_row(column):
    return jnp.sum(jnp.where(diagonal(column.shape[0]), column, 0.0), axis=0, keepdims=True)


def as_column(row):
    return jnp.sum(jnp.where(diagonal(row.shape[1]), row, 0.0), axis=1, keepdims=True)


def halves(value):
    high = value.astype(jnp.bfloat16)
    return high, (value - high.astype(jnp.float32)).astype(jnp.bfloat16)


def pack_kernel(rows_ref, label_ref, rank_ref, packed_ref):
    count, width = rows_ref.shape
    packed_ref[:count, :] = rows_ref[...]
    rank = rank_ref[...]
    high = lax.shift_right_logical(rank, 8)
    low = rank - lax.shift_left(high, 8)
    pieces = [piece.astype(jnp.float32) for piece in (label_ref[...], high, low)]
    pieces.append(jnp.zeros((1, width - 3 * count), jnp.float32))
    line = jnp.concatenate(pieces, axis=1)
    packed_ref[count:, :] = jnp.broadcast_to(line, (EXTRA, width)).astype(jnp.bfloat16)


def labels_and_ranks(block):
    count = block.shape[0] - EXTRA
    line = block[count:, :].astype(jnp.float32)[:1]
    label, high, low = (line[:, at * count : (at + 1) * count] for at in range(3))
    return label, high * 256.0 + low


def rows_of(blocks):
    return jnp.concatenate([block[: block.shape[0] - EXTRA, :] for block in blocks], axis=0)


def score(unit, side, blocks):
    own_label, own_rank = side[:, 0:1], side[:, 1:2]
    keys = rows_of(blocks)
    sides = [labels_and_ranks(block) for block in blocks]
    label = jnp.concatenate([item[0] for item in sides], axis=1)
    rank = jnp.concatenate([item[1] for item in sides], axis=1)
    cosine = lax.dot_general(
        unit, make_unit(keys), (((1,), (1,)), ((), ())), preferred_element_type=jnp.float32
    )
    weight = 1.0 / (1.0 + jnp.exp(-40.0 * (cosine - 0.05)))
    near = jnp.where((label == own_label) & (rank != own_rank), weight, 0.0)
    earlier = jnp.sum(jnp.where(rank < own_rank, near, 0.0), axis=1, keepdims=True)
    every = jnp.sum(near, axis=1, keepdims=True)
    mixed = jnp.dot(near.astype(jnp.bfloat16), keys, preferred_element_type=jnp.float32)
    return earlier, every, mixed


def first_kernel(own_ref, other_ref, *refs):
    blocks, (unit_ref, side_ref, sums_ref, mixed_ref) = refs[:-4], refs[-4:]
    count = own_ref.shape[0] - EXTRA
    side_ref[...] = jnp.zeros_like(side_ref)
    sums_ref[...] = jnp.zeros_like(sums_ref)
    unit_ref[...] = make_unit(rows_of([own_ref, other_ref]))
    for at, ref in enumerate((own_ref, other_ref)):
        here = slice(at * count, (at + 1) * count)
        label, rank = labels_and_ranks(ref)
        side_ref[here, 0:1] = as_column(label)
        side_ref[here, 1:2] = as_column(rank)
    sums_ref[:, 0:1], sums_ref[:, 1:2], mixed_ref[...] = score(
        unit_ref[...], side_ref, (own_ref,) + blocks
    )


def more_kernel(unit_ref, side_ref, old_sums_ref, old_mixed_ref, *refs):
    blocks, (sums_ref, mixed_ref) = refs[:-2], refs[-2:]
    earlier, every, mixed = score(unit_ref[...], side_ref, blocks)
    sums_ref[...] = old_sums_ref[...]
    sums_ref[:, 0:1] += earlier
    sums_ref[:, 1:2] += every
    mixed_ref[...] = old_mixed_ref[...] + mixed


def final_kernel(unit_ref, side_ref, old_sums_ref, old_mixed_ref, *refs):
    blocks, (keep_sums_ref, keep_ref, send_ref) = refs[:-3], refs[-3:]
    count, width = keep_ref.shape
    earlier, every, mixed = score(unit_ref[...], side_ref, blocks)
    earlier += old_sums_ref[:, 0:1]
    every += old_sums_ref[:, 1:2]
    mixed += old_mixed_ref[...]
    keep_sums_ref[...] = jnp.zeros_like(keep_sums_ref)
    keep_sums_ref[:, 0:1] = earlier[:count]
    keep_sums_ref[:, 1:2] = every[:count]
    keep_ref[...] = mixed[:count]
    send_ref[:count, :] = mixed[count:].astype(jnp.bfloat16)
    pieces = halves(as_row(earlier[count:])) + halves(as_row(every[count:]))
    pieces = [piece.astype(jnp.float32) for piece in pieces]
    pieces.append(jnp.zeros((1, width - 4 * count), jnp.float32))
    line = jnp.concatenate(pieces, axis=1)
    send_ref[count:, :] = jnp.broadcast_to(line, (EXTRA, width)).astype(jnp.bfloat16)


def combine_kernel(sums_ref, mixed_ref, got_ref, dup_ref, out_ref):
    count = mixed_ref.shape[0]
    line = got_ref[count:, :].astype(jnp.float32)[:1]
    parts = [line[:, at * count : (at + 1) * count] for at in range(4)]
    every = sums_ref[:, 1:2] + as_column(parts[2] + parts[3])
    dup_ref[...] = jnp.log1p(as_row(sums_ref[:, 0:1]) + parts[0] + parts[1])
    mixed = mixed_ref[...] + got_ref[:count, :].astype(jnp.float32)
    out_ref[...] = mixed / jnp.sqrt(1.0 + every)


def cost(queries, keys, width):
    return pl.CostEstimate(
        flops=400 * queries * keys * width,
        bytes_accessed=8 * queries * width + 2 * keys * width,
        transcendentals=100 * queries * keys,
    )


def local(embeddings, cluster_id, priority):
    count, width = embeddings.shape
    height = count + EXTRA
    shards = lax.axis_size("shard")
    lanes = lax.axis_size("owner")
    rounds = shards // 2
    queries = 2 * count
    bf16, f32 = jnp.bfloat16, jnp.float32
    params = pltpu.CompilerParams(vmem_limit_bytes=VMEM)

    def shape(*dims, dtype=f32):
        return jax.ShapeDtypeStruct(dims, dtype)

    ring = list(range(0, rounds, 2)) + list(range(1, rounds, 2))[::-1]

    def along(array, step):
        pairs = [
            (2 * ring[at] + side, 2 * ring[(at + step) % rounds] + side)
            for at in range(rounds)
            for side in range(2)
        ]
        return lax.ppermute(array, "shard", pairs)

    def across(array):
        return lax.ppermute(array, "shard", [(at, at ^ 1) for at in range(shards)])

    def two_ways(by_ring, step, by_side):
        pairs = []
        for at in range(rounds):
            for side in range(2):
                here, there = 2 * ring[at] + side, 2 * ring[(at + step) % rounds] + side
                pairs.append((here * lanes, there * lanes))
                pairs += [(here * lanes + lane, (here ^ 1) * lanes + lane) for lane in range(1, lanes)]
        source = jnp.where(lax.axis_index("owner") == 0, by_ring, by_side)
        return lax.ppermute(source, ("shard", "owner"), pairs)

    def swap(array):
        return lax.ppermute(array, "owner", [(at, lanes - 1 - at) for at in range(lanes)])

    def first(*blocks):
        return pl.pallas_call(
            first_kernel,
            out_shape=[
                shape(queries, width, dtype=bf16),
                shape(queries, 128),
                shape(queries, 128),
                shape(queries, width),
            ],
            cost_estimate=cost(queries, (len(blocks) - 1) * count, width),
            compiler_params=params,
            name="first_scores",
        )(*blocks)

    def more(unit, side, sums, mixed, *blocks):
        return pl.pallas_call(
            more_kernel,
            out_shape=[shape(queries, 128), shape(queries, width)],
            input_output_aliases={2: 0, 3: 1},
            cost_estimate=cost(queries, len(blocks) * count, width),
            compiler_params=params,
            name="more_scores",
        )(unit, side, sums, mixed, *blocks)

    def final(unit, side, sums, mixed, *blocks):
        return pl.pallas_call(
            final_kernel,
            out_shape=[
                shape(count, 128),
                shape(count, width),
                shape(height, width, dtype=bf16),
            ],
            cost_estimate=cost(queries, len(blocks) * count, width),
            compiler_params=params,
            name="final_scores",
        )(unit, side, sums, mixed, *blocks)

    own = pl.pallas_call(
        pack_kernel,
        out_shape=shape(height, width, dtype=bf16),
        compiler_params=params,
        name="pack",
    )(embeddings, cluster_id.reshape(1, count), priority.reshape(1, count))

    moved, beside = along(own, 1), across(own)
    other = swap(own)
    if rounds == 4:
        ahead = along(own, -1)
        other, beside, moved = lax.optimization_barrier((other, beside, moved))
        opposite = along(moved, 1)
        moved_beside = across(moved)
        ahead_beside = two_ways(beside, -1, ahead)
        state = first(own, other, beside, ahead)
        unit, side = state[:2]
        moved_beside, opposite = lax.optimization_barrier((moved_beside, opposite))
        last = [two_ways(moved_beside, 1, opposite)]
        sums, mixed = more(*state, moved, moved_beside)
        sums, mixed = more(unit, side, sums, mixed, opposite, ahead_beside)
    else:
        unit, side, sums, mixed = first(own, other, beside)

        def turn(at, state):
            moved, sums, mixed = state
            ahead, beside = along(moved, 1), across(moved)
            sums, mixed = more(unit, side, sums, mixed, moved, beside)
            return ahead, sums, mixed

        moved, sums, mixed = lax.fori_loop(1, rounds - 1, turn, (moved, sums, mixed))
        last = [moved, across(moved)]
    keep_sums, keep, send = final(unit, side, sums, mixed, *last)
    dup, out = pl.pallas_call(
        combine_kernel,
        out_shape=[shape(1, count), shape(count, width)],
        compiler_params=params,
        name="combine",
    )(keep_sums, keep, swap(send))
    return dup[0], out


def solution(mesh):
    placed = (
        P(("groups", "shard", "owner"), None),
        P(("groups", "shard", "owner"), None),
        P(("groups", "shard", "owner")),
    )
    return jax.shard_map(
        local,
        mesh=mesh,
        in_specs=placed,
        out_specs=(P(("groups", "shard", "owner")), P(("groups", "shard", "owner"), None)),
        check_vma=False,
    )
```

```python
import functools

import jax
import jax.numpy as jnp
from jax import lax
from jax.experimental import pallas as pl
from jax.experimental.pallas import tpu as pltpu
from jax.sharding import PartitionSpec as P

EXTRA = 8
VMEM = 24 * 1024 * 1024


def make_unit(rows):
    wide = rows.astype(jnp.float32)
    scale = lax.rsqrt(jnp.mean(wide * wide, axis=-1, keepdims=True) + 1e-06) / jnp.sqrt(
        jnp.float32(rows.shape[-1])
    )
    return (wide * scale).astype(jnp.bfloat16)


def diagonal(count):
    down = lax.broadcasted_iota(jnp.int32, (count, count), 0)
    return down == lax.broadcasted_iota(jnp.int32, (count, count), 1)


def as_row(column):
    return jnp.sum(jnp.where(diagonal(column.shape[0]), column, 0.0), axis=0, keepdims=True)


def as_column(row):
    return jnp.sum(jnp.where(diagonal(row.shape[1]), row, 0.0), axis=1, keepdims=True)


def halves(value):
    high = value.astype(jnp.bfloat16)
    return high, (value - high.astype(jnp.float32)).astype(jnp.bfloat16)


def tags_kernel(label_ref, rank_ref, tags_ref):
    tags_ref[0:1, :] = label_ref[...]
    tags_ref[1:2, :] = rank_ref[...]


def score(unit, side, blocks, tags):
    own_label, own_rank = side[:, 0:1], side[:, 1:2]
    keys = jnp.concatenate([block[...] for block in blocks], axis=0)
    label = jnp.concatenate([tag[0:1] for tag in tags], axis=1)
    rank = jnp.concatenate([tag[1:2] for tag in tags], axis=1)
    cosine = lax.dot_general(
        unit, make_unit(keys), (((1,), (1,)), ((), ())), preferred_element_type=jnp.float32
    )
    weight = 1.0 / (1.0 + jnp.exp(-40.0 * (cosine - 0.05)))
    near = jnp.where((label == own_label) & (rank != own_rank), weight, 0.0)
    earlier = jnp.sum(jnp.where(rank < own_rank, near, 0.0), axis=1, keepdims=True)
    every = jnp.sum(near, axis=1, keepdims=True)
    mixed = jnp.dot(near.astype(jnp.bfloat16), keys, preferred_element_type=jnp.float32)
    return earlier, every, mixed


def tags_of(tags_ref, order):
    tags = tags_ref[...].astype(jnp.float32)
    return [tags[2 * at : 2 * at + 2] for at in order]


def first_kernel(own_ref, other_ref, beside_ref, tags_ref, other_tags_ref, *outs):
    unit_ref, side_ref, sums_ref, mixed_ref = outs
    count = own_ref.shape[0]
    side_ref[...] = jnp.zeros_like(side_ref)
    sums_ref[...] = jnp.zeros_like(sums_ref)
    tags = tags_of(tags_ref, (0, 1))
    for at, (ref, tag) in enumerate(
        ((own_ref, tags[0]), (other_ref, tags_of(other_tags_ref, (0,))[0]))
    ):
        here = slice(at * count, (at + 1) * count)
        unit_ref[here, :] = make_unit(ref[...])
        side_ref[here, 0:1] = as_column(tag[0:1])
        side_ref[here, 1:2] = as_column(tag[1:2])
    sums_ref[:, 0:1], sums_ref[:, 1:2], mixed_ref[...] = score(
        unit_ref[...], side_ref, (own_ref, beside_ref), tags
    )


def more_kernel(order, unit_ref, side_ref, old_sums_ref, old_mixed_ref, tags_ref, *refs):
    blocks, (sums_ref, mixed_ref) = refs[:-2], refs[-2:]
    tags = tags_of(tags_ref, order)
    earlier, every, mixed = score(unit_ref[...], side_ref, blocks, tags)
    sums_ref[...] = old_sums_ref[...]
    sums_ref[:, 0:1] += earlier
    sums_ref[:, 1:2] += every
    mixed_ref[...] = old_mixed_ref[...] + mixed


def final_kernel(order, unit_ref, side_ref, old_sums_ref, old_mixed_ref, tags_ref, *refs):
    blocks, (keep_sums_ref, keep_ref, send_ref) = refs[:-3], refs[-3:]
    count, width = keep_ref.shape
    tags = tags_of(tags_ref, order)
    earlier, every, mixed = score(unit_ref[...], side_ref, blocks, tags)
    earlier += old_sums_ref[:, 0:1]
    every += old_sums_ref[:, 1:2]
    mixed += old_mixed_ref[...]
    keep_sums_ref[...] = jnp.zeros_like(keep_sums_ref)
    keep_sums_ref[:, 0:1] = earlier[:count]
    keep_sums_ref[:, 1:2] = every[:count]
    keep_ref[...] = mixed[:count]
    send_ref[:count, :] = mixed[count:].astype(jnp.bfloat16)
    pieces = halves(as_row(earlier[count:])) + halves(as_row(every[count:]))
    pieces = [piece.astype(jnp.float32) for piece in pieces]
    pieces.append(jnp.zeros((1, width - 4 * count), jnp.float32))
    line = jnp.concatenate(pieces, axis=1)
    send_ref[count:, :] = jnp.broadcast_to(line, (EXTRA, width)).astype(jnp.bfloat16)


def combine_kernel(sums_ref, mixed_ref, got_ref, dup_ref, out_ref):
    count = mixed_ref.shape[0]
    line = got_ref[count:, :].astype(jnp.float32)[:1]
    parts = [line[:, at * count : (at + 1) * count] for at in range(4)]
    every = sums_ref[:, 1:2] + as_column(parts[2] + parts[3])
    dup_ref[...] = jnp.log1p(as_row(sums_ref[:, 0:1]) + parts[0] + parts[1])
    mixed = mixed_ref[...] + got_ref[:count, :].astype(jnp.float32)
    out_ref[...] = mixed / jnp.sqrt(1.0 + every)


def cost(queries, keys, width):
    return pl.CostEstimate(
        flops=400 * queries * keys * width,
        bytes_accessed=8 * queries * width + 2 * keys * width,
        transcendentals=100 * queries * keys,
    )


def local(embeddings, cluster_id, priority):
    count, width = embeddings.shape
    shards = lax.axis_size("shard")
    lanes = lax.axis_size("owner")
    rounds = shards // 2
    queries = 2 * count
    bf16, f32 = jnp.bfloat16, jnp.float32
    params = pltpu.CompilerParams(vmem_limit_bytes=VMEM)

    def shape(*dims, dtype=f32):
        return jax.ShapeDtypeStruct(dims, dtype)

    ring = list(range(0, rounds, 2)) + list(range(1, rounds, 2))[::-1]

    def along(array, step):
        pairs = [
            (2 * ring[at] + side, 2 * ring[(at + step) % rounds] + side)
            for at in range(rounds)
            for side in range(2)
        ]
        return lax.ppermute(array, "shard", pairs)

    def across(array):
        return lax.ppermute(array, "shard", [(at, at ^ 1) for at in range(shards)])

    def two_ways(by_ring, step, by_side):
        pairs = []
        for at in range(rounds):
            for side in range(2):
                here, there = 2 * ring[at] + side, 2 * ring[(at + step) % rounds] + side
                pairs.append((here * lanes, there * lanes))
                pairs += [(here * lanes + lane, (here ^ 1) * lanes + lane) for lane in range(1, lanes)]
        source = jnp.where(lax.axis_index("owner") == 0, by_ring, by_side)
        return lax.ppermute(source, ("shard", "owner"), pairs)

    def swap(array):
        return lax.ppermute(array, "owner", [(at, lanes - 1 - at) for at in range(lanes)])

    def first(own, other, beside, tags, other_tags):
        return pl.pallas_call(
            first_kernel,
            out_shape=[
                shape(queries, width, dtype=bf16),
                shape(queries, 128),
                shape(queries, 128),
                shape(queries, width),
            ],
            cost_estimate=cost(queries, 3 * count, width),
            compiler_params=params,
            name="first_scores",
        )(own, other, beside, tags, other_tags)

    def more(unit, side, sums, mixed, tags, order, *blocks):
        return pl.pallas_call(
            functools.partial(more_kernel, order),
            out_shape=[shape(queries, 128), shape(queries, width)],
            input_output_aliases={2: 0, 3: 1},
            cost_estimate=cost(queries, len(blocks) * count, width),
            compiler_params=params,
            name="more_scores",
        )(unit, side, sums, mixed, tags, *blocks)

    def final(unit, side, sums, mixed, tags, order, *blocks):
        return pl.pallas_call(
            functools.partial(final_kernel, order),
            out_shape=[
                shape(count, 128),
                shape(count, width),
                shape(count + EXTRA, width, dtype=bf16),
            ],
            cost_estimate=cost(queries, len(blocks) * count, width),
            compiler_params=params,
            name="final_scores",
        )(unit, side, sums, mixed, tags, *blocks)

    own = embeddings
    moved, beside, other = along(own, 1), across(own), swap(own)
    if rounds == 4:
        other, cluster_id, priority = lax.optimization_barrier((other, cluster_id, priority))
    tags = pl.pallas_call(
        tags_kernel, out_shape=shape(2, count, dtype=jnp.int32), compiler_params=params, name="tags"
    )(cluster_id.reshape(1, count), priority.reshape(1, count))
    other_tags = swap(tags)
    pair = jnp.concatenate([tags, across(tags)], axis=0)
    moved_tags = along(pair, 1)
    if rounds == 4:
        ahead = along(own, -1)
        moved, beside = lax.optimization_barrier((moved, beside))
        opposite = along(moved, 1)
        moved_beside = across(moved)
        ahead, moved_tags = lax.optimization_barrier((ahead, moved_tags))
        ahead_beside = two_ways(beside, -1, ahead)
        unit, side, sums, mixed = first(own, other, beside, pair, other_tags)
        far_tags = along(jnp.concatenate([pair, moved_tags], axis=0), 2)
        opposite, moved_beside = lax.optimization_barrier((opposite, moved_beside))
        last = two_ways(moved_beside, 1, opposite)
        sums, mixed = more(unit, side, sums, mixed, moved_tags, (0, 1), moved, moved_beside)
        sums, mixed = more(unit, side, sums, mixed, far_tags, (2, 3, 0), ahead, ahead_beside, opposite)
        outcome = final(unit, side, sums, mixed, far_tags, (1,), last)
    else:
        unit, side, sums, mixed = first(own, other, beside, pair, other_tags)

        def turn(at, state):
            moved, tags, sums, mixed = state
            ahead, ahead_tags, beside = along(moved, 1), along(tags, 1), across(moved)
            sums, mixed = more(unit, side, sums, mixed, tags, (0, 1), moved, beside)
            return ahead, ahead_tags, sums, mixed

        state = (moved, moved_tags, sums, mixed)
        moved, moved_tags, sums, mixed = lax.fori_loop(1, rounds - 1, turn, state)
        outcome = final(unit, side, sums, mixed, moved_tags, (0, 1), moved, across(moved))
    keep_sums, keep, send = outcome
    dup, out = pl.pallas_call(
        combine_kernel,
        out_shape=[shape(1, count), shape(count, width)],
        compiler_params=params,
        name="combine",
    )(keep_sums, keep, swap(send))
    return dup[0], out


def solution(mesh):
    placed = (
        P(("groups", "shard", "owner"), None),
        P(("groups", "shard", "owner"), None),
        P(("groups", "shard", "owner")),
    )
    return jax.shard_map(
        local,
        mesh=mesh,
        in_specs=placed,
        out_specs=(P(("groups", "shard", "owner")), P(("groups", "shard", "owner"), None)),
        check_vma=False,
    )
```

```python
import jax
import jax.numpy as jnp
from jax import lax
from jax.experimental import pallas as pl
from jax.experimental.pallas import tpu as pltpu
from jax.sharding import PartitionSpec as P

EXTRA = 8
VMEM = 24 * 1024 * 1024
PACK_VMEM = 62 * 1024 * 1024


def make_unit(rows):
    wide = rows.astype(jnp.float32)
    scale = lax.rsqrt(jnp.mean(wide * wide, axis=-1, keepdims=True) + 1e-06) / jnp.sqrt(
        jnp.float32(rows.shape[-1])
    )
    return (wide * scale).astype(jnp.bfloat16)


def diagonal(count):
    down = lax.broadcasted_iota(jnp.int32, (count, count), 0)
    return down == lax.broadcasted_iota(jnp.int32, (count, count), 1)


def as_row(column):
    return jnp.sum(jnp.where(diagonal(column.shape[0]), column, 0.0), axis=0, keepdims=True)


def as_column(row):
    return jnp.sum(jnp.where(diagonal(row.shape[1]), row, 0.0), axis=1, keepdims=True)


def halves(value):
    high = value.astype(jnp.bfloat16)
    return high, (value - high.astype(jnp.float32)).astype(jnp.bfloat16)


def pack_kernel(rows_ref, label_ref, rank_ref, packed_ref, label, rank, line, sems):
    count, width = rows_ref.shape
    copies = [
        pltpu.make_async_copy(label_ref, label, sems.at[0]),
        pltpu.make_async_copy(rank_ref, rank, sems.at[1]),
        pltpu.make_async_copy(rows_ref, packed_ref.at[pl.ds(0, count), :], sems.at[2]),
    ]
    for copy in copies:
        copy.start()
    for copy in copies[:2]:
        copy.wait()
    high = lax.shift_right_logical(rank[...], 8)
    low = rank[...] - lax.shift_left(high, 8)
    pieces = [piece.astype(jnp.float32) for piece in (label[...], high, low)]
    pieces.append(jnp.zeros((1, width - 3 * count), jnp.float32))
    row = jnp.concatenate(pieces, axis=1)
    line[...] = jnp.broadcast_to(row, (EXTRA, width)).astype(jnp.bfloat16)
    added = pltpu.make_async_copy(line, packed_ref.at[pl.ds(count, EXTRA), :], sems.at[3])
    added.start()
    added.wait()
    copies[2].wait()


def labels_and_ranks(block):
    count = block.shape[0] - EXTRA
    line = block[count:, :].astype(jnp.float32)[:1]
    label, high, low = (line[:, at * count : (at + 1) * count] for at in range(3))
    return label, high * 256.0 + low


def rows_of(blocks):
    return jnp.concatenate([block[: block.shape[0] - EXTRA, :] for block in blocks], axis=0)


def score(unit, side, blocks):
    own_label, own_rank = side[:, 0:1], side[:, 1:2]
    keys = rows_of(blocks)
    sides = [labels_and_ranks(block) for block in blocks]
    label = jnp.concatenate([item[0] for item in sides], axis=1)
    rank = jnp.concatenate([item[1] for item in sides], axis=1)
    cosine = lax.dot_general(
        unit, make_unit(keys), (((1,), (1,)), ((), ())), preferred_element_type=jnp.float32
    )
    weight = 1.0 / (1.0 + jnp.exp(-40.0 * (cosine - 0.05)))
    near = jnp.where((label == own_label) & (rank != own_rank), weight, 0.0)
    earlier = jnp.sum(jnp.where(rank < own_rank, near, 0.0), axis=1, keepdims=True)
    every = jnp.sum(near, axis=1, keepdims=True)
    mixed = jnp.dot(near.astype(jnp.bfloat16), keys, preferred_element_type=jnp.float32)
    return earlier, every, mixed


def first_kernel(own_ref, other_ref, *refs):
    blocks, (unit_ref, side_ref, sums_ref, mixed_ref) = refs[:-4], refs[-4:]
    count = own_ref.shape[0] - EXTRA
    side_ref[...] = jnp.zeros_like(side_ref)
    sums_ref[...] = jnp.zeros_like(sums_ref)
    unit_ref[...] = make_unit(rows_of([own_ref, other_ref]))
    for at, ref in enumerate((own_ref, other_ref)):
        here = slice(at * count, (at + 1) * count)
        label, rank = labels_and_ranks(ref)
        side_ref[here, 0:1] = as_column(label)
        side_ref[here, 1:2] = as_column(rank)
    sums_ref[:, 0:1], sums_ref[:, 1:2], mixed_ref[...] = score(
        unit_ref[...], side_ref, (own_ref,) + blocks
    )


def more_kernel(unit_ref, side_ref, old_sums_ref, old_mixed_ref, *refs):
    blocks, (sums_ref, mixed_ref) = refs[:-2], refs[-2:]
    earlier, every, mixed = score(unit_ref[...], side_ref, blocks)
    sums_ref[...] = old_sums_ref[...]
    sums_ref[:, 0:1] += earlier
    sums_ref[:, 1:2] += every
    mixed_ref[...] = old_mixed_ref[...] + mixed


def final_kernel(unit_ref, side_ref, old_sums_ref, old_mixed_ref, *refs):
    blocks, (keep_sums_ref, keep_ref, send_ref) = refs[:-3], refs[-3:]
    count, width = keep_ref.shape
    earlier, every, mixed = score(unit_ref[...], side_ref, blocks)
    earlier += old_sums_ref[:, 0:1]
    every += old_sums_ref[:, 1:2]
    mixed += old_mixed_ref[...]
    keep_sums_ref[...] = jnp.zeros_like(keep_sums_ref)
    keep_sums_ref[:, 0:1] = earlier[:count]
    keep_sums_ref[:, 1:2] = every[:count]
    keep_ref[...] = mixed[:count]
    send_ref[:count, :] = mixed[count:].astype(jnp.bfloat16)
    pieces = halves(as_row(earlier[count:])) + halves(as_row(every[count:]))
    pieces = [piece.astype(jnp.float32) for piece in pieces]
    pieces.append(jnp.zeros((1, width - 4 * count), jnp.float32))
    line = jnp.concatenate(pieces, axis=1)
    send_ref[count:, :] = jnp.broadcast_to(line, (EXTRA, width)).astype(jnp.bfloat16)


def combine_kernel(sums_ref, mixed_ref, got_ref, dup_ref, out_ref):
    count = mixed_ref.shape[0]
    line = got_ref[count:, :].astype(jnp.float32)[:1]
    parts = [line[:, at * count : (at + 1) * count] for at in range(4)]
    every = sums_ref[:, 1:2] + as_column(parts[2] + parts[3])
    dup_ref[...] = jnp.log1p(as_row(sums_ref[:, 0:1]) + parts[0] + parts[1])
    mixed = mixed_ref[...] + got_ref[:count, :].astype(jnp.float32)
    out_ref[...] = mixed / jnp.sqrt(1.0 + every)


def cost(queries, keys, width):
    return pl.CostEstimate(
        flops=400 * queries * keys * width,
        bytes_accessed=8 * queries * width + 2 * keys * width,
        transcendentals=100 * queries * keys,
    )


def local(embeddings, cluster_id, priority):
    count, width = embeddings.shape
    height = count + EXTRA
    shards = lax.axis_size("shard")
    lanes = lax.axis_size("owner")
    rounds = shards // 2
    queries = 2 * count
    bf16, f32 = jnp.bfloat16, jnp.float32
    params = pltpu.CompilerParams(vmem_limit_bytes=VMEM)

    def shape(*dims, dtype=f32):
        return jax.ShapeDtypeStruct(dims, dtype)

    ring = list(range(0, rounds, 2)) + list(range(1, rounds, 2))[::-1]

    def along(array, step):
        pairs = [
            (2 * ring[at] + side, 2 * ring[(at + step) % rounds] + side)
            for at in range(rounds)
            for side in range(2)
        ]
        return lax.ppermute(array, "shard", pairs)

    def across(array):
        return lax.ppermute(array, "shard", [(at, at ^ 1) for at in range(shards)])

    def two_ways(by_ring, step, by_side, ring_lane):
        pairs = []
        for at in range(rounds):
            for side in range(2):
                here, there = 2 * ring[at] + side, 2 * ring[(at + step) % rounds] + side
                pairs += [
                    (here * lanes + lane, (there if lane == ring_lane else here ^ 1) * lanes + lane)
                    for lane in range(lanes)
                ]
        source = jnp.where(lax.axis_index("owner") == ring_lane, by_ring, by_side)
        return lax.ppermute(source, ("shard", "owner"), pairs)

    def swap(array):
        return lax.ppermute(array, "owner", [(at, lanes - 1 - at) for at in range(lanes)])

    def first(*blocks):
        return pl.pallas_call(
            first_kernel,
            out_shape=[
                shape(queries, width, dtype=bf16),
                shape(queries, 128),
                shape(queries, 128),
                shape(queries, width),
            ],
            cost_estimate=cost(queries, (len(blocks) - 1) * count, width),
            compiler_params=params,
            name="first_scores",
        )(*blocks)

    def more(unit, side, sums, mixed, *blocks):
        return pl.pallas_call(
            more_kernel,
            out_shape=[shape(queries, 128), shape(queries, width)],
            input_output_aliases={2: 0, 3: 1},
            cost_estimate=cost(queries, len(blocks) * count, width),
            compiler_params=params,
            name="more_scores",
        )(unit, side, sums, mixed, *blocks)

    def final(unit, side, sums, mixed, *blocks):
        return pl.pallas_call(
            final_kernel,
            out_shape=[
                shape(count, 128),
                shape(count, width),
                shape(height, width, dtype=bf16),
            ],
            cost_estimate=cost(queries, len(blocks) * count, width),
            compiler_params=params,
            name="final_scores",
        )(unit, side, sums, mixed, *blocks)

    own = pl.pallas_call(
        pack_kernel,
        in_specs=[pl.BlockSpec(memory_space=pl.ANY)] * 3,
        out_specs=pl.BlockSpec(memory_space=pl.ANY),
        out_shape=shape(height, width, dtype=bf16),
        scratch_shapes=[
            pltpu.VMEM((1, count), jnp.int32),
            pltpu.VMEM((1, count), jnp.int32),
            pltpu.VMEM((EXTRA, width), bf16),
            pltpu.SemaphoreType.DMA((4,)),
        ],
        compiler_params=pltpu.CompilerParams(vmem_limit_bytes=PACK_VMEM),
        name="pack",
    )(embeddings, cluster_id.reshape(1, count), priority.reshape(1, count))

    moved, beside = along(own, 1), across(own)
    other = swap(own)
    if rounds == 4:
        ahead = along(own, -1)
        other, beside, moved = lax.optimization_barrier((other, beside, moved))
        opposite = along(moved, 1)
        moved_beside = across(moved)
        ahead_beside = two_ways(beside, -1, ahead, 0)
        state = first(own, other, beside, ahead)
        unit, side = state[:2]
        moved_beside, opposite = lax.optimization_barrier((moved_beside, opposite))
        last = [two_ways(moved_beside, 1, opposite, lanes - 1)]
        sums, mixed = more(*state, moved, moved_beside)
        sums, mixed = more(unit, side, sums, mixed, opposite, ahead_beside)
    else:
        unit, side, sums, mixed = first(own, other, beside)

        def turn(at, state):
            moved, sums, mixed = state
            ahead, beside = along(moved, 1), across(moved)
            sums, mixed = more(unit, side, sums, mixed, moved, beside)
            return ahead, sums, mixed

        moved, sums, mixed = lax.fori_loop(1, rounds - 1, turn, (moved, sums, mixed))
        last = [moved, across(moved)]
    keep_sums, keep, send = final(unit, side, sums, mixed, *last)
    dup, out = pl.pallas_call(
        combine_kernel,
        out_shape=[shape(1, count), shape(count, width)],
        compiler_params=params,
        name="combine",
    )(keep_sums, keep, swap(send))
    return dup[0], out


def solution(mesh):
    placed = (
        P(("groups", "shard", "owner"), None),
        P(("groups", "shard", "owner"), None),
        P(("groups", "shard", "owner")),
    )
    return jax.shard_map(
        local,
        mesh=mesh,
        in_specs=placed,
        out_specs=(P(("groups", "shard", "owner")), P(("groups", "shard", "owner"), None)),
        check_vma=False,
    )
```

```python
import jax
import jax.numpy as jnp
from jax import lax
from jax.experimental import pallas as pl
from jax.experimental.pallas import tpu as pltpu
from jax.sharding import PartitionSpec as P

EXTRA = 8
VMEM = 24 * 1024 * 1024


def make_unit(rows):
    wide = rows.astype(jnp.float32)
    scale = lax.rsqrt(jnp.mean(wide * wide, axis=-1, keepdims=True) + 1e-06) / jnp.sqrt(
        jnp.float32(rows.shape[-1])
    )
    return (wide * scale).astype(jnp.bfloat16)


def diagonal(count):
    down = lax.broadcasted_iota(jnp.int32, (count, count), 0)
    return down == lax.broadcasted_iota(jnp.int32, (count, count), 1)


def as_row(column):
    return jnp.sum(jnp.where(diagonal(column.shape[0]), column, 0.0), axis=0, keepdims=True)


def as_column(row):
    return jnp.sum(jnp.where(diagonal(row.shape[1]), row, 0.0), axis=1, keepdims=True)


def halves(value):
    high = value.astype(jnp.bfloat16)
    return high, (value - high.astype(jnp.float32)).astype(jnp.bfloat16)


def pack_kernel(rows_ref, label_ref, rank_ref, packed_ref):
    count, width = rows_ref.shape
    packed_ref[:count, :] = rows_ref[...]
    rank = rank_ref[...]
    high = lax.shift_right_logical(rank, 8)
    low = rank - lax.shift_left(high, 8)
    pieces = [piece.astype(jnp.float32) for piece in (label_ref[...], high, low)]
    pieces.append(jnp.zeros((1, width - 3 * count), jnp.float32))
    line = jnp.concatenate(pieces, axis=1)
    packed_ref[count:, :] = jnp.broadcast_to(line, (EXTRA, width)).astype(jnp.bfloat16)


def labels_and_ranks(block):
    count = block.shape[0] - EXTRA
    line = block[count:, :].astype(jnp.float32)[:1]
    label, high, low = (line[:, at * count : (at + 1) * count] for at in range(3))
    return label, high * 256.0 + low


def rows_of(blocks):
    return jnp.concatenate([block[: block.shape[0] - EXTRA, :] for block in blocks], axis=0)


def score(unit, side, blocks):
    own_label, own_rank = side[:, 0:1], side[:, 1:2]
    keys = rows_of(blocks)
    sides = [labels_and_ranks(block) for block in blocks]
    label = jnp.concatenate([item[0] for item in sides], axis=1)
    rank = jnp.concatenate([item[1] for item in sides], axis=1)
    cosine = lax.dot_general(
        unit, make_unit(keys), (((1,), (1,)), ((), ())), preferred_element_type=jnp.float32
    )
    weight = 1.0 / (1.0 + jnp.exp(-40.0 * (cosine - 0.05)))
    near = jnp.where((label == own_label) & (rank != own_rank), weight, 0.0)
    earlier = jnp.sum(jnp.where(rank < own_rank, near, 0.0), axis=1, keepdims=True)
    every = jnp.sum(near, axis=1, keepdims=True)
    mixed = jnp.dot(near.astype(jnp.bfloat16), keys, preferred_element_type=jnp.float32)
    return earlier, every, mixed


def first_kernel(own_ref, other_ref, *refs):
    blocks, (unit_ref, side_ref, sums_ref, mixed_ref) = refs[:-4], refs[-4:]
    count = own_ref.shape[0] - EXTRA
    side_ref[...] = jnp.zeros_like(side_ref)
    sums_ref[...] = jnp.zeros_like(sums_ref)
    unit_ref[...] = make_unit(rows_of([own_ref, other_ref]))
    for at, ref in enumerate((own_ref, other_ref)):
        here = slice(at * count, (at + 1) * count)
        label, rank = labels_and_ranks(ref)
        side_ref[here, 0:1] = as_column(label)
        side_ref[here, 1:2] = as_column(rank)
    sums_ref[:, 0:1], sums_ref[:, 1:2], mixed_ref[...] = score(
        unit_ref[...], side_ref, (own_ref,) + blocks
    )


def more_kernel(unit_ref, side_ref, old_sums_ref, old_mixed_ref, *refs):
    blocks, (sums_ref, mixed_ref) = refs[:-2], refs[-2:]
    earlier, every, mixed = score(unit_ref[...], side_ref, blocks)
    sums_ref[...] = old_sums_ref[...]
    sums_ref[:, 0:1] += earlier
    sums_ref[:, 1:2] += every
    mixed_ref[...] = old_mixed_ref[...] + mixed


def final_kernel(unit_ref, side_ref, old_sums_ref, old_mixed_ref, *refs):
    blocks, (keep_sums_ref, keep_ref, send_ref) = refs[:-3], refs[-3:]
    count, width = keep_ref.shape
    earlier, every, mixed = score(unit_ref[...], side_ref, blocks)
    earlier += old_sums_ref[:, 0:1]
    every += old_sums_ref[:, 1:2]
    mixed += old_mixed_ref[...]
    keep_sums_ref[...] = jnp.zeros_like(keep_sums_ref)
    keep_sums_ref[:, 0:1] = earlier[:count]
    keep_sums_ref[:, 1:2] = every[:count]
    keep_ref[...] = mixed[:count]
    send_ref[:count, :] = mixed[count:].astype(jnp.bfloat16)
    pieces = halves(as_row(earlier[count:])) + halves(as_row(every[count:]))
    pieces = [piece.astype(jnp.float32) for piece in pieces]
    pieces.append(jnp.zeros((1, width - 4 * count), jnp.float32))
    line = jnp.concatenate(pieces, axis=1)
    send_ref[count:, :] = jnp.broadcast_to(line, (EXTRA, width)).astype(jnp.bfloat16)


def combine_kernel(sums_ref, mixed_ref, got_ref, dup_ref, out_ref):
    count = mixed_ref.shape[0]
    line = got_ref[count:, :].astype(jnp.float32)[:1]
    parts = [line[:, at * count : (at + 1) * count] for at in range(4)]
    every = sums_ref[:, 1:2] + as_column(parts[2] + parts[3])
    dup_ref[...] = jnp.log1p(as_row(sums_ref[:, 0:1]) + parts[0] + parts[1])
    mixed = mixed_ref[...] + got_ref[:count, :].astype(jnp.float32)
    out_ref[...] = mixed / jnp.sqrt(1.0 + every)


def cost(queries, keys, width):
    return pl.CostEstimate(
        flops=400 * queries * keys * width,
        bytes_accessed=8 * queries * width + 2 * keys * width,
        transcendentals=100 * queries * keys,
    )


def local(embeddings, cluster_id, priority):
    count, width = embeddings.shape
    height = count + EXTRA
    shards = lax.axis_size("shard")
    lanes = lax.axis_size("owner")
    rounds = shards // 2
    queries = 2 * count
    bf16, f32 = jnp.bfloat16, jnp.float32
    params = pltpu.CompilerParams(vmem_limit_bytes=VMEM)

    def shape(*dims, dtype=f32):
        return jax.ShapeDtypeStruct(dims, dtype)

    ring = list(range(0, rounds, 2)) + list(range(1, rounds, 2))[::-1]

    def along(array, step):
        pairs = [
            (2 * ring[at] + side, 2 * ring[(at + step) % rounds] + side)
            for at in range(rounds)
            for side in range(2)
        ]
        return lax.ppermute(array, "shard", pairs)

    def across(array):
        return lax.ppermute(array, "shard", [(at, at ^ 1) for at in range(shards)])

    def two_ways(by_ring, step, by_side):
        pairs = []
        for at in range(rounds):
            for side in range(2):
                here, there = 2 * ring[at] + side, 2 * ring[(at + step) % rounds] + side
                pairs.append((here * lanes, there * lanes))
                pairs += [(here * lanes + lane, (here ^ 1) * lanes + lane) for lane in range(1, lanes)]
        source = jnp.where(lax.axis_index("owner") == 0, by_ring, by_side)
        return lax.ppermute(source, ("shard", "owner"), pairs)

    def swap(array):
        return lax.ppermute(array, "owner", [(at, lanes - 1 - at) for at in range(lanes)])

    def first(*blocks):
        return pl.pallas_call(
            first_kernel,
            out_shape=[
                shape(queries, width, dtype=bf16),
                shape(queries, 128),
                shape(queries, 128),
                shape(queries, width),
            ],
            cost_estimate=cost(queries, (len(blocks) - 1) * count, width),
            compiler_params=params,
            name="first_scores",
        )(*blocks)

    def more(unit, side, sums, mixed, *blocks):
        return pl.pallas_call(
            more_kernel,
            out_shape=[shape(queries, 128), shape(queries, width)],
            input_output_aliases={2: 0, 3: 1},
            cost_estimate=cost(queries, len(blocks) * count, width),
            compiler_params=params,
            name="more_scores",
        )(unit, side, sums, mixed, *blocks)

    def final(unit, side, sums, mixed, *blocks):
        return pl.pallas_call(
            final_kernel,
            out_shape=[
                shape(count, 128),
                shape(count, width),
                shape(height, width, dtype=bf16),
            ],
            cost_estimate=cost(queries, len(blocks) * count, width),
            compiler_params=params,
            name="final_scores",
        )(unit, side, sums, mixed, *blocks)

    own = pl.pallas_call(
        pack_kernel,
        out_shape=shape(height, width, dtype=bf16),
        compiler_params=params,
        name="pack",
    )(embeddings, cluster_id.reshape(1, count), priority.reshape(1, count))

    moved, beside = along(own, 1), across(own)
    other = swap(own)
    if rounds == 4:
        ahead = along(own, -1)
        moved, beside, other = lax.optimization_barrier((moved, beside, other))
        opposite = along(moved, 1)
        moved_beside = across(moved)
        ahead_beside = two_ways(beside, -1, ahead)
        other, opposite, moved_beside = lax.optimization_barrier((other, opposite, moved_beside))
        last = [two_ways(moved_beside, 1, opposite)]
        unit, side, sums, mixed = first(own, other, beside, ahead, ahead_beside)
        sums, mixed = more(unit, side, sums, mixed, moved, moved_beside, opposite)
    else:
        unit, side, sums, mixed = first(own, other, beside)

        def turn(at, state):
            moved, sums, mixed = state
            ahead, beside = along(moved, 1), across(moved)
            sums, mixed = more(unit, side, sums, mixed, moved, beside)
            return ahead, sums, mixed

        moved, sums, mixed = lax.fori_loop(1, rounds - 1, turn, (moved, sums, mixed))
        last = [moved, across(moved)]
    keep_sums, keep, send = final(unit, side, sums, mixed, *last)
    dup, out = pl.pallas_call(
        combine_kernel,
        out_shape=[shape(1, count), shape(count, width)],
        compiler_params=params,
        name="combine",
    )(keep_sums, keep, swap(send))
    return dup[0], out


def solution(mesh):
    placed = (
        P(("groups", "shard", "owner"), None),
        P(("groups", "shard", "owner"), None),
        P(("groups", "shard", "owner")),
    )
    return jax.shard_map(
        local,
        mesh=mesh,
        in_specs=placed,
        out_specs=(P(("groups", "shard", "owner")), P(("groups", "shard", "owner"), None)),
        check_vma=False,
    )
```

```python
import jax
import jax.numpy as jnp
from jax import lax
from jax.experimental import pallas as pl
from jax.experimental.pallas import tpu as pltpu
from jax.sharding import PartitionSpec as P

SUB, LANE = 8, 128
EXTRA = 8
VMEM = 24 * 1024 * 1024


def make_unit(rows):
    wide = rows.astype(jnp.float32)
    scale = lax.rsqrt(jnp.mean(wide * wide, axis=-1, keepdims=True) + 1e-06) / jnp.sqrt(
        jnp.float32(rows.shape[-1])
    )
    return (wide * scale).astype(jnp.bfloat16)


def diagonal(count):
    down = lax.broadcasted_iota(jnp.int32, (count, count), 0)
    return down == lax.broadcasted_iota(jnp.int32, (count, count), 1)


def as_row(column):
    return jnp.sum(jnp.where(diagonal(column.shape[0]), column, 0.0), axis=0, keepdims=True)


def as_column(row):
    return jnp.sum(jnp.where(diagonal(row.shape[1]), row, 0.0), axis=1, keepdims=True)


def halves(value):
    high = value.astype(jnp.bfloat16)
    return high, (value - high.astype(jnp.float32)).astype(jnp.bfloat16)


def pack_kernel(tiles_ref, label_ref, rank_ref, packed_ref):
    many = tiles_ref.shape[0]
    packed_ref[:many] = tiles_ref[...]
    rank = rank_ref[...]
    high = lax.shift_right_logical(rank, 8)
    low = rank - lax.shift_left(high, 8)
    lines = [line.astype(jnp.float32) for line in (label_ref[...], high, low)]
    lines.append(jnp.zeros((SUB - len(lines), LANE), jnp.float32))
    packed_ref[many] = jnp.concatenate(lines, axis=0).astype(jnp.bfloat16)


def labels_and_ranks(block):
    tile = block[block.shape[0] - 1].astype(jnp.float32)
    return tile[0:1], tile[1:2] * 256.0 + tile[2:3]


def rows_of(blocks, width):
    across = width // LANE
    wide = []
    for block in blocks:
        tiles = block[: block.shape[0] - 1].astype(jnp.float32)
        tiles = tiles.reshape(-1, across, SUB, LANE)
        pieces = [tiles[:, at].reshape(-1, LANE) for at in range(across)]
        wide.append(jnp.concatenate(pieces, axis=1))
    return jnp.concatenate(wide, axis=0)


def score(unit, side, blocks):
    own_label, own_rank = side[:, 0:1], side[:, 1:2]
    wide = rows_of(blocks, unit.shape[1])
    keys = wide.astype(jnp.bfloat16)
    sides = [labels_and_ranks(block) for block in blocks]
    label = jnp.concatenate([item[0] for item in sides], axis=1)
    rank = jnp.concatenate([item[1] for item in sides], axis=1)
    cosine = lax.dot_general(
        unit, make_unit(wide), (((1,), (1,)), ((), ())), preferred_element_type=jnp.float32
    )
    weight = 1.0 / (1.0 + jnp.exp(-40.0 * (cosine - 0.05)))
    near = jnp.where((label == own_label) & (rank != own_rank), weight, 0.0)
    earlier = jnp.sum(jnp.where(rank < own_rank, near, 0.0), axis=1, keepdims=True)
    every = jnp.sum(near, axis=1, keepdims=True)
    mixed = jnp.dot(near.astype(jnp.bfloat16), keys, preferred_element_type=jnp.float32)
    return earlier, every, mixed


def first_kernel(own_ref, other_ref, *refs):
    blocks, (unit_ref, side_ref, sums_ref, mixed_ref) = refs[:-4], refs[-4:]
    count = own_ref.shape[0] // (unit_ref.shape[1] // LANE) * SUB
    side_ref[...] = jnp.zeros_like(side_ref)
    sums_ref[...] = jnp.zeros_like(sums_ref)
    unit_ref[...] = make_unit(rows_of([own_ref, other_ref], unit_ref.shape[1]))
    for at, ref in enumerate((own_ref, other_ref)):
        here = slice(at * count, (at + 1) * count)
        label, rank = labels_and_ranks(ref)
        side_ref[here, 0:1] = as_column(label)
        side_ref[here, 1:2] = as_column(rank)
    sums_ref[:, 0:1], sums_ref[:, 1:2], mixed_ref[...] = score(
        unit_ref[...], side_ref, (own_ref,) + blocks
    )


def more_kernel(unit_ref, side_ref, old_sums_ref, old_mixed_ref, *refs):
    blocks, (sums_ref, mixed_ref) = refs[:-2], refs[-2:]
    earlier, every, mixed = score(unit_ref[...], side_ref, blocks)
    sums_ref[...] = old_sums_ref[...]
    sums_ref[:, 0:1] += earlier
    sums_ref[:, 1:2] += every
    mixed_ref[...] = old_mixed_ref[...] + mixed


def final_kernel(unit_ref, side_ref, old_sums_ref, old_mixed_ref, *refs):
    blocks, (keep_sums_ref, keep_ref, send_ref) = refs[:-3], refs[-3:]
    count, width = keep_ref.shape
    earlier, every, mixed = score(unit_ref[...], side_ref, blocks)
    earlier += old_sums_ref[:, 0:1]
    every += old_sums_ref[:, 1:2]
    mixed += old_mixed_ref[...]
    keep_sums_ref[...] = jnp.zeros_like(keep_sums_ref)
    keep_sums_ref[:, 0:1] = earlier[:count]
    keep_sums_ref[:, 1:2] = every[:count]
    keep_ref[...] = mixed[:count]
    send_ref[:count, :] = mixed[count:].astype(jnp.bfloat16)
    pieces = halves(as_row(earlier[count:])) + halves(as_row(every[count:]))
    pieces = [piece.astype(jnp.float32) for piece in pieces]
    pieces.append(jnp.zeros((1, width - 4 * count), jnp.float32))
    line = jnp.concatenate(pieces, axis=1)
    send_ref[count:, :] = jnp.broadcast_to(line, (EXTRA, width)).astype(jnp.bfloat16)


def combine_kernel(sums_ref, mixed_ref, got_ref, dup_ref, out_ref):
    count = mixed_ref.shape[0]
    line = got_ref[count:, :].astype(jnp.float32)[:1]
    parts = [line[:, at * count : (at + 1) * count] for at in range(4)]
    every = sums_ref[:, 1:2] + as_column(parts[2] + parts[3])
    dup_ref[...] = jnp.log1p(as_row(sums_ref[:, 0:1]) + parts[0] + parts[1])
    mixed = mixed_ref[...] + got_ref[:count, :].astype(jnp.float32)
    out_ref[...] = mixed / jnp.sqrt(1.0 + every)


def cost(queries, keys, width):
    return pl.CostEstimate(
        flops=400 * queries * keys * width,
        bytes_accessed=8 * queries * width + 2 * keys * width,
        transcendentals=100 * queries * keys,
    )


def local(embeddings, cluster_id, priority):
    count, width = embeddings.shape
    tiles = count // SUB * (width // LANE)
    shards = lax.axis_size("shard")
    lanes = lax.axis_size("owner")
    rounds = shards // 2
    queries = 2 * count
    bf16, f32 = jnp.bfloat16, jnp.float32
    params = pltpu.CompilerParams(vmem_limit_bytes=VMEM)

    def shape(*dims, dtype=f32):
        return jax.ShapeDtypeStruct(dims, dtype)

    ring = list(range(0, rounds, 2)) + list(range(1, rounds, 2))[::-1]

    def along(array, step):
        pairs = [
            (2 * ring[at] + side, 2 * ring[(at + step) % rounds] + side)
            for at in range(rounds)
            for side in range(2)
        ]
        return lax.ppermute(array, "shard", pairs)

    def across(array):
        return lax.ppermute(array, "shard", [(at, at ^ 1) for at in range(shards)])

    def two_ways(by_ring, step, by_side):
        pairs = []
        for at in range(rounds):
            for side in range(2):
                here, there = 2 * ring[at] + side, 2 * ring[(at + step) % rounds] + side
                pairs.append((here * lanes, there * lanes))
                pairs += [(here * lanes + lane, (here ^ 1) * lanes + lane) for lane in range(1, lanes)]
        source = jnp.where(lax.axis_index("owner") == 0, by_ring, by_side)
        return lax.ppermute(source, ("shard", "owner"), pairs)

    def swap(array):
        return lax.ppermute(array, "owner", [(at, lanes - 1 - at) for at in range(lanes)])

    def first(*blocks):
        return pl.pallas_call(
            first_kernel,
            out_shape=[
                shape(queries, width, dtype=bf16),
                shape(queries, 128),
                shape(queries, 128),
                shape(queries, width),
            ],
            cost_estimate=cost(queries, (len(blocks) - 1) * count, width),
            compiler_params=params,
            name="first_scores",
        )(*blocks)

    def more(unit, side, sums, mixed, *blocks):
        return pl.pallas_call(
            more_kernel,
            out_shape=[shape(queries, 128), shape(queries, width)],
            input_output_aliases={2: 0, 3: 1},
            cost_estimate=cost(queries, len(blocks) * count, width),
            compiler_params=params,
            name="more_scores",
        )(unit, side, sums, mixed, *blocks)

    def final(unit, side, sums, mixed, *blocks):
        return pl.pallas_call(
            final_kernel,
            out_shape=[
                shape(count, 128),
                shape(count, width),
                shape(count + EXTRA, width, dtype=bf16),
            ],
            cost_estimate=cost(queries, len(blocks) * count, width),
            compiler_params=params,
            name="final_scores",
        )(unit, side, sums, mixed, *blocks)

    pieces = embeddings.reshape(count // SUB, SUB, width // LANE, LANE).transpose(0, 2, 1, 3)
    own = pl.pallas_call(
        pack_kernel,
        out_shape=shape(tiles + 1, SUB, LANE, dtype=bf16),
        compiler_params=params,
        name="pack",
    )(pieces.reshape(tiles, SUB, LANE), cluster_id.reshape(1, count), priority.reshape(1, count))

    moved, beside = along(own, 1), across(own)
    other = swap(own)
    if rounds == 4:
        ahead = along(own, -1)
        moved, beside, other = lax.optimization_barrier((moved, beside, other))
        opposite = along(moved, 1)
        moved_beside = across(moved)
        ahead_beside = two_ways(beside, -1, ahead)
        other, opposite, moved_beside = lax.optimization_barrier((other, opposite, moved_beside))
        last = [two_ways(moved_beside, 1, opposite)]
        unit, side, sums, mixed = first(own, other, beside, ahead, ahead_beside)
        sums, mixed = more(unit, side, sums, mixed, moved, moved_beside, opposite)
    else:
        unit, side, sums, mixed = first(own, other, beside)

        def turn(at, state):
            moved, sums, mixed = state
            ahead, beside = along(moved, 1), across(moved)
            sums, mixed = more(unit, side, sums, mixed, moved, beside)
            return ahead, sums, mixed

        moved, sums, mixed = lax.fori_loop(1, rounds - 1, turn, (moved, sums, mixed))
        last = [moved, across(moved)]
    keep_sums, keep, send = final(unit, side, sums, mixed, *last)
    dup, out = pl.pallas_call(
        combine_kernel,
        out_shape=[shape(1, count), shape(count, width)],
        compiler_params=params,
        name="combine",
    )(keep_sums, keep, swap(send))
    return dup[0], out


def solution(mesh):
    placed = (
        P(("groups", "shard", "owner"), None),
        P(("groups", "shard", "owner"), None),
        P(("groups", "shard", "owner")),
    )
    return jax.shard_map(
        local,
        mesh=mesh,
        in_specs=placed,
        out_specs=(P(("groups", "shard", "owner")), P(("groups", "shard", "owner"), None)),
        check_vma=False,
    )
```

```python
import jax
import jax.numpy as jnp
from jax import lax
from jax.experimental import pallas as pl
from jax.experimental.pallas import tpu as pltpu
from jax.sharding import PartitionSpec as P

SUB, LANE = 8, 128
EXTRA = 8
VMEM = 24 * 1024 * 1024


def make_unit(rows):
    wide = rows.astype(jnp.float32)
    scale = lax.rsqrt(jnp.mean(wide * wide, axis=-1, keepdims=True) + 1e-06) / jnp.sqrt(
        jnp.float32(rows.shape[-1])
    )
    return (wide * scale).astype(jnp.bfloat16)


def diagonal(count):
    down = lax.broadcasted_iota(jnp.int32, (count, count), 0)
    return down == lax.broadcasted_iota(jnp.int32, (count, count), 1)


def as_row(column):
    return jnp.sum(jnp.where(diagonal(column.shape[0]), column, 0.0), axis=0, keepdims=True)


def as_column(row):
    return jnp.sum(jnp.where(diagonal(row.shape[1]), row, 0.0), axis=1, keepdims=True)


def halves(value):
    high = value.astype(jnp.bfloat16)
    return high, (value - high.astype(jnp.float32)).astype(jnp.bfloat16)


def pack_kernel(tiles_ref, label_ref, rank_ref, packed_ref):
    many = tiles_ref.shape[0]
    packed_ref[:many] = tiles_ref[...]
    rank = rank_ref[...]
    high = lax.shift_right_logical(rank, 8)
    low = rank - lax.shift_left(high, 8)
    lines = [line.astype(jnp.float32) for line in (label_ref[...], high, low)]
    lines.append(jnp.zeros((SUB - len(lines), LANE), jnp.float32))
    packed_ref[many] = jnp.concatenate(lines, axis=0).astype(jnp.bfloat16)


def labels_and_ranks(block):
    tile = block[block.shape[0] - 1].astype(jnp.float32)
    return tile[0:1], tile[1:2] * 256.0 + tile[2:3]


def rows_of(blocks, width):
    across = width // LANE
    wide = []
    for block in blocks:
        tiles = block[: block.shape[0] - 1].astype(jnp.float32)
        tiles = tiles.reshape(-1, across, SUB, LANE)
        pieces = [tiles[:, at].reshape(-1, LANE) for at in range(across)]
        wide.append(jnp.concatenate(pieces, axis=1))
    return jnp.concatenate(wide, axis=0)


def score(unit, side, blocks):
    own_label, own_rank = side[:, 0:1], side[:, 1:2]
    wide = rows_of(blocks, unit.shape[1])
    keys = wide.astype(jnp.bfloat16)
    sides = [labels_and_ranks(block) for block in blocks]
    label = jnp.concatenate([item[0] for item in sides], axis=1)
    rank = jnp.concatenate([item[1] for item in sides], axis=1)
    cosine = lax.dot_general(
        unit, make_unit(wide), (((1,), (1,)), ((), ())), preferred_element_type=jnp.float32
    )
    weight = 1.0 / (1.0 + jnp.exp(-40.0 * (cosine - 0.05)))
    near = jnp.where((label == own_label) & (rank != own_rank), weight, 0.0)
    earlier = jnp.sum(jnp.where(rank < own_rank, near, 0.0), axis=1, keepdims=True)
    every = jnp.sum(near, axis=1, keepdims=True)
    mixed = jnp.dot(near.astype(jnp.bfloat16), keys, preferred_element_type=jnp.float32)
    return earlier, every, mixed


def first_kernel(own_ref, other_ref, *refs):
    blocks, (unit_ref, side_ref, sums_ref, mixed_ref) = refs[:-4], refs[-4:]
    count = own_ref.shape[0] // (unit_ref.shape[1] // LANE) * SUB
    side_ref[...] = jnp.zeros_like(side_ref)
    sums_ref[...] = jnp.zeros_like(sums_ref)
    unit_ref[...] = make_unit(rows_of([own_ref, other_ref], unit_ref.shape[1]))
    for at, ref in enumerate((own_ref, other_ref)):
        here = slice(at * count, (at + 1) * count)
        label, rank = labels_and_ranks(ref)
        side_ref[here, 0:1] = as_column(label)
        side_ref[here, 1:2] = as_column(rank)
    sums_ref[:, 0:1], sums_ref[:, 1:2], mixed_ref[...] = score(
        unit_ref[...], side_ref, (own_ref,) + blocks
    )


def more_kernel(unit_ref, side_ref, old_sums_ref, old_mixed_ref, *refs):
    blocks, (sums_ref, mixed_ref) = refs[:-2], refs[-2:]
    earlier, every, mixed = score(unit_ref[...], side_ref, blocks)
    sums_ref[...] = old_sums_ref[...]
    sums_ref[:, 0:1] += earlier
    sums_ref[:, 1:2] += every
    mixed_ref[...] = old_mixed_ref[...] + mixed


def final_kernel(unit_ref, side_ref, old_sums_ref, old_mixed_ref, *refs):
    blocks, (keep_sums_ref, keep_ref, send_ref) = refs[:-3], refs[-3:]
    count, width = keep_ref.shape
    earlier, every, mixed = score(unit_ref[...], side_ref, blocks)
    earlier += old_sums_ref[:, 0:1]
    every += old_sums_ref[:, 1:2]
    mixed += old_mixed_ref[...]
    keep_sums_ref[...] = jnp.zeros_like(keep_sums_ref)
    keep_sums_ref[:, 0:1] = earlier[:count]
    keep_sums_ref[:, 1:2] = every[:count]
    keep_ref[...] = mixed[:count]
    send_ref[:count, :] = mixed[count:].astype(jnp.bfloat16)
    pieces = halves(as_row(earlier[count:])) + halves(as_row(every[count:]))
    pieces = [piece.astype(jnp.float32) for piece in pieces]
    pieces.append(jnp.zeros((1, width - 4 * count), jnp.float32))
    line = jnp.concatenate(pieces, axis=1)
    send_ref[count:, :] = jnp.broadcast_to(line, (EXTRA, width)).astype(jnp.bfloat16)


def combine_kernel(sums_ref, mixed_ref, got_ref, dup_ref, out_ref):
    count = mixed_ref.shape[0]
    line = got_ref[count:, :].astype(jnp.float32)[:1]
    parts = [line[:, at * count : (at + 1) * count] for at in range(4)]
    every = sums_ref[:, 1:2] + as_column(parts[2] + parts[3])
    dup_ref[...] = jnp.log1p(as_row(sums_ref[:, 0:1]) + parts[0] + parts[1])
    mixed = mixed_ref[...] + got_ref[:count, :].astype(jnp.float32)
    out_ref[...] = mixed / jnp.sqrt(1.0 + every)


def cost(queries, keys, width):
    return pl.CostEstimate(
        flops=400 * queries * keys * width,
        bytes_accessed=8 * queries * width + 2 * keys * width,
        transcendentals=100 * queries * keys,
    )


def local(embeddings, cluster_id, priority):
    count, width = embeddings.shape
    tiles = count // SUB * (width // LANE)
    shards = lax.axis_size("shard")
    lanes = lax.axis_size("owner")
    rounds = shards // 2
    queries = 2 * count
    bf16, f32 = jnp.bfloat16, jnp.float32
    params = pltpu.CompilerParams(vmem_limit_bytes=VMEM)

    def shape(*dims, dtype=f32):
        return jax.ShapeDtypeStruct(dims, dtype)

    ring = list(range(0, rounds, 2)) + list(range(1, rounds, 2))[::-1]

    def along(array, step):
        pairs = [
            (2 * ring[at] + side, 2 * ring[(at + step) % rounds] + side)
            for at in range(rounds)
            for side in range(2)
        ]
        return lax.ppermute(array, "shard", pairs)

    def across(array):
        return lax.ppermute(array, "shard", [(at, at ^ 1) for at in range(shards)])

    def two_ways(by_ring, step, by_side):
        pairs = []
        for at in range(rounds):
            for side in range(2):
                here, there = 2 * ring[at] + side, 2 * ring[(at + step) % rounds] + side
                pairs.append((here * lanes, there * lanes))
                pairs += [(here * lanes + lane, (here ^ 1) * lanes + lane) for lane in range(1, lanes)]
        source = jnp.where(lax.axis_index("owner") == 0, by_ring, by_side)
        return lax.ppermute(source, ("shard", "owner"), pairs)

    def swap(array):
        return lax.ppermute(array, "owner", [(at, lanes - 1 - at) for at in range(lanes)])

    def first(*blocks):
        return pl.pallas_call(
            first_kernel,
            out_shape=[
                shape(queries, width, dtype=bf16),
                shape(queries, 128),
                shape(queries, 128),
                shape(queries, width),
            ],
            cost_estimate=cost(queries, (len(blocks) - 1) * count, width),
            compiler_params=params,
            name="first_scores",
        )(*blocks)

    def more(unit, side, sums, mixed, *blocks):
        return pl.pallas_call(
            more_kernel,
            out_shape=[shape(queries, 128), shape(queries, width)],
            input_output_aliases={2: 0, 3: 1},
            cost_estimate=cost(queries, len(blocks) * count, width),
            compiler_params=params,
            name="more_scores",
        )(unit, side, sums, mixed, *blocks)

    def final(unit, side, sums, mixed, *blocks):
        return pl.pallas_call(
            final_kernel,
            out_shape=[
                shape(count, 128),
                shape(count, width),
                shape(count + EXTRA, width, dtype=bf16),
            ],
            cost_estimate=cost(queries, len(blocks) * count, width),
            compiler_params=params,
            name="final_scores",
        )(unit, side, sums, mixed, *blocks)

    pieces = embeddings.reshape(count // SUB, SUB, width // LANE, LANE).transpose(0, 2, 1, 3)
    own = pl.pallas_call(
        pack_kernel,
        out_shape=shape(tiles + 1, SUB, LANE, dtype=bf16),
        compiler_params=params,
        name="pack",
    )(pieces.reshape(tiles, SUB, LANE), cluster_id.reshape(1, count), priority.reshape(1, count))

    moved, beside = along(own, 1), across(own)
    other = swap(own)
    if rounds == 4:
        ahead = along(own, -1)
        moved, beside, other = lax.optimization_barrier((moved, beside, other))
        opposite = along(moved, 1)
        moved_beside = across(moved)
        ahead_beside = across(ahead)
        other, moved_beside, opposite = lax.optimization_barrier((other, moved_beside, opposite))
        last = [two_ways(moved_beside, 1, opposite)]
        unit, side, sums, mixed = first(own, other, beside, ahead, ahead_beside)
        sums, mixed = more(unit, side, sums, mixed, moved, moved_beside, opposite)
    else:
        unit, side, sums, mixed = first(own, other, beside)

        def turn(at, state):
            moved, sums, mixed = state
            ahead, beside = along(moved, 1), across(moved)
            sums, mixed = more(unit, side, sums, mixed, moved, beside)
            return ahead, sums, mixed

        moved, sums, mixed = lax.fori_loop(1, rounds - 1, turn, (moved, sums, mixed))
        last = [moved, across(moved)]
    keep_sums, keep, send = final(unit, side, sums, mixed, *last)
    dup, out = pl.pallas_call(
        combine_kernel,
        out_shape=[shape(1, count), shape(count, width)],
        compiler_params=params,
        name="combine",
    )(keep_sums, keep, swap(send))
    return dup[0], out


def solution(mesh):
    placed = (
        P(("groups", "shard", "owner"), None),
        P(("groups", "shard", "owner"), None),
        P(("groups", "shard", "owner")),
    )
    return jax.shard_map(
        local,
        mesh=mesh,
        in_specs=placed,
        out_specs=(P(("groups", "shard", "owner")), P(("groups", "shard", "owner"), None)),
        check_vma=False,
    )
```

```python
import jax
import jax.numpy as jnp
from jax import lax
from jax.experimental import pallas as pl
from jax.experimental.pallas import tpu as pltpu
from jax.sharding import PartitionSpec as P

SUB, LANE = 8, 128
EXTRA = 8
VMEM = 24 * 1024 * 1024


def make_unit(rows):
    wide = rows.astype(jnp.float32)
    scale = lax.rsqrt(jnp.mean(wide * wide, axis=-1, keepdims=True) + 1e-06) / jnp.sqrt(
        jnp.float32(rows.shape[-1])
    )
    return (wide * scale).astype(jnp.bfloat16)


def diagonal(count):
    down = lax.broadcasted_iota(jnp.int32, (count, count), 0)
    return down == lax.broadcasted_iota(jnp.int32, (count, count), 1)


def as_row(column):
    return jnp.sum(jnp.where(diagonal(column.shape[0]), column, 0.0), axis=0, keepdims=True)


def as_column(row):
    return jnp.sum(jnp.where(diagonal(row.shape[1]), row, 0.0), axis=1, keepdims=True)


def halves(value):
    high = value.astype(jnp.bfloat16)
    return high, (value - high.astype(jnp.float32)).astype(jnp.bfloat16)


def pack_kernel(tiles_ref, label_ref, rank_ref, packed_ref):
    many = tiles_ref.shape[0]
    packed_ref[:many] = tiles_ref[...]
    rank = rank_ref[...]
    high = lax.shift_right_logical(rank, 8)
    low = rank - lax.shift_left(high, 8)
    lines = [line.astype(jnp.float32) for line in (label_ref[...], high, low)]
    lines.append(jnp.zeros((SUB - len(lines), LANE), jnp.float32))
    packed_ref[many] = jnp.concatenate(lines, axis=0).astype(jnp.bfloat16)


def labels_and_ranks(block):
    tile = block[block.shape[0] - 1].astype(jnp.float32)
    return tile[0:1], tile[1:2] * 256.0 + tile[2:3]


def rows_of(blocks, width):
    across = width // LANE
    wide = []
    for block in blocks:
        tiles = block[: block.shape[0] - 1].astype(jnp.float32)
        tiles = tiles.reshape(-1, across, SUB, LANE)
        pieces = [tiles[:, at].reshape(-1, LANE) for at in range(across)]
        wide.append(jnp.concatenate(pieces, axis=1))
    return jnp.concatenate(wide, axis=0)


def score(unit, side, blocks):
    own_label, own_rank = side[:, 0:1], side[:, 1:2]
    wide = rows_of(blocks, unit.shape[1])
    keys = wide.astype(jnp.bfloat16)
    sides = [labels_and_ranks(block) for block in blocks]
    label = jnp.concatenate([item[0] for item in sides], axis=1)
    rank = jnp.concatenate([item[1] for item in sides], axis=1)
    cosine = lax.dot_general(
        unit, make_unit(wide), (((1,), (1,)), ((), ())), preferred_element_type=jnp.float32
    )
    weight = 1.0 / (1.0 + jnp.exp(-40.0 * (cosine - 0.05)))
    near = jnp.where((label == own_label) & (rank != own_rank), weight, 0.0)
    earlier = jnp.sum(jnp.where(rank < own_rank, near, 0.0), axis=1, keepdims=True)
    every = jnp.sum(near, axis=1, keepdims=True)
    mixed = jnp.dot(near.astype(jnp.bfloat16), keys, preferred_element_type=jnp.float32)
    return earlier, every, mixed


def first_kernel(own_ref, other_ref, *refs):
    blocks, (unit_ref, side_ref, sums_ref, mixed_ref) = refs[:-4], refs[-4:]
    count = own_ref.shape[0] // (unit_ref.shape[1] // LANE) * SUB
    side_ref[...] = jnp.zeros_like(side_ref)
    sums_ref[...] = jnp.zeros_like(sums_ref)
    unit_ref[...] = make_unit(rows_of([own_ref, other_ref], unit_ref.shape[1]))
    for at, ref in enumerate((own_ref, other_ref)):
        here = slice(at * count, (at + 1) * count)
        label, rank = labels_and_ranks(ref)
        side_ref[here, 0:1] = as_column(label)
        side_ref[here, 1:2] = as_column(rank)
    sums_ref[:, 0:1], sums_ref[:, 1:2], mixed_ref[...] = score(
        unit_ref[...], side_ref, (own_ref,) + blocks
    )


def more_kernel(unit_ref, side_ref, old_sums_ref, old_mixed_ref, *refs):
    blocks, (sums_ref, mixed_ref) = refs[:-2], refs[-2:]
    earlier, every, mixed = score(unit_ref[...], side_ref, blocks)
    sums_ref[...] = old_sums_ref[...]
    sums_ref[:, 0:1] += earlier
    sums_ref[:, 1:2] += every
    mixed_ref[...] = old_mixed_ref[...] + mixed


def final_kernel(unit_ref, side_ref, old_sums_ref, old_mixed_ref, *refs):
    blocks, (keep_sums_ref, keep_ref, send_ref) = refs[:-3], refs[-3:]
    count, width = keep_ref.shape
    earlier, every, mixed = score(unit_ref[...], side_ref, blocks)
    earlier += old_sums_ref[:, 0:1]
    every += old_sums_ref[:, 1:2]
    mixed += old_mixed_ref[...]
    keep_sums_ref[...] = jnp.zeros_like(keep_sums_ref)
    keep_sums_ref[:, 0:1] = earlier[:count]
    keep_sums_ref[:, 1:2] = every[:count]
    keep_ref[...] = mixed[:count]
    send_ref[:count, :] = mixed[count:].astype(jnp.bfloat16)
    pieces = halves(as_row(earlier[count:])) + halves(as_row(every[count:]))
    pieces = [piece.astype(jnp.float32) for piece in pieces]
    pieces.append(jnp.zeros((1, width - 4 * count), jnp.float32))
    line = jnp.concatenate(pieces, axis=1)
    send_ref[count:, :] = jnp.broadcast_to(line, (EXTRA, width)).astype(jnp.bfloat16)


def combine_kernel(sums_ref, mixed_ref, got_ref, dup_ref, out_ref):
    count = mixed_ref.shape[0]
    line = got_ref[count:, :].astype(jnp.float32)[:1]
    parts = [line[:, at * count : (at + 1) * count] for at in range(4)]
    every = sums_ref[:, 1:2] + as_column(parts[2] + parts[3])
    dup_ref[...] = jnp.log1p(as_row(sums_ref[:, 0:1]) + parts[0] + parts[1])
    mixed = mixed_ref[...] + got_ref[:count, :].astype(jnp.float32)
    out_ref[...] = mixed / jnp.sqrt(1.0 + every)


def cost(queries, keys, width):
    return pl.CostEstimate(
        flops=400 * queries * keys * width,
        bytes_accessed=8 * queries * width + 2 * keys * width,
        transcendentals=100 * queries * keys,
    )


def local(embeddings, cluster_id, priority):
    count, width = embeddings.shape
    tiles = count // SUB * (width // LANE)
    shards = lax.axis_size("shard")
    lanes = lax.axis_size("owner")
    rounds = shards // 2
    queries = 2 * count
    bf16, f32 = jnp.bfloat16, jnp.float32
    params = pltpu.CompilerParams(vmem_limit_bytes=VMEM)

    def shape(*dims, dtype=f32):
        return jax.ShapeDtypeStruct(dims, dtype)

    ring = list(range(0, rounds, 2)) + list(range(1, rounds, 2))[::-1]

    def along(array, step):
        pairs = [
            (2 * ring[at] + side, 2 * ring[(at + step) % rounds] + side)
            for at in range(rounds)
            for side in range(2)
        ]
        return lax.ppermute(array, "shard", pairs)

    def across(array):
        return lax.ppermute(array, "shard", [(at, at ^ 1) for at in range(shards)])

    def two_ways(by_ring, step, by_side):
        pairs = []
        for at in range(rounds):
            for side in range(2):
                here, there = 2 * ring[at] + side, 2 * ring[(at + step) % rounds] + side
                pairs.append((here * lanes, there * lanes))
                pairs += [(here * lanes + lane, (here ^ 1) * lanes + lane) for lane in range(1, lanes)]
        source = jnp.where(lax.axis_index("owner") == 0, by_ring, by_side)
        return lax.ppermute(source, ("shard", "owner"), pairs)

    def swap(array):
        return lax.ppermute(array, "owner", [(at, lanes - 1 - at) for at in range(lanes)])

    def first(*blocks):
        return pl.pallas_call(
            first_kernel,
            out_shape=[
                shape(queries, width, dtype=bf16),
                shape(queries, 128),
                shape(queries, 128),
                shape(queries, width),
            ],
            cost_estimate=cost(queries, (len(blocks) - 1) * count, width),
            compiler_params=params,
            name="first_scores",
        )(*blocks)

    def more(unit, side, sums, mixed, *blocks):
        return pl.pallas_call(
            more_kernel,
            out_shape=[shape(queries, 128), shape(queries, width)],
            input_output_aliases={2: 0, 3: 1},
            cost_estimate=cost(queries, len(blocks) * count, width),
            compiler_params=params,
            name="more_scores",
        )(unit, side, sums, mixed, *blocks)

    def final(unit, side, sums, mixed, *blocks):
        return pl.pallas_call(
            final_kernel,
            out_shape=[
                shape(count, 128),
                shape(count, width),
                shape(count + EXTRA, width, dtype=bf16),
            ],
            cost_estimate=cost(queries, len(blocks) * count, width),
            compiler_params=params,
            name="final_scores",
        )(unit, side, sums, mixed, *blocks)

    pieces = embeddings.reshape(count // SUB, SUB, width // LANE, LANE).transpose(0, 2, 1, 3)
    own = pl.pallas_call(
        pack_kernel,
        out_shape=shape(tiles + 1, SUB, LANE, dtype=bf16),
        compiler_params=params,
        name="pack",
    )(pieces.reshape(tiles, SUB, LANE), cluster_id.reshape(1, count), priority.reshape(1, count))

    moved, beside = along(own, 1), across(own)
    other = swap(own)
    if rounds == 4:
        ahead = along(own, -1)
        moved, beside, other = lax.optimization_barrier((moved, beside, other))
        opposite = along(moved, 1)
        moved_beside = across(moved)
        ahead_beside = two_ways(beside, -1, ahead)
        other, moved_beside, opposite = lax.optimization_barrier((other, moved_beside, opposite))
        last = [two_ways(moved_beside, 1, opposite)]
        unit, side, sums, mixed = first(own, other, beside, ahead, ahead_beside)
        sums, mixed = more(unit, side, sums, mixed, moved, moved_beside, opposite)
    else:
        unit, side, sums, mixed = first(own, other, beside)

        def turn(at, state):
            moved, sums, mixed = state
            ahead, beside = along(moved, 1), across(moved)
            sums, mixed = more(unit, side, sums, mixed, moved, beside)
            return ahead, sums, mixed

        moved, sums, mixed = lax.fori_loop(1, rounds - 1, turn, (moved, sums, mixed))
        last = [moved, across(moved)]
    keep_sums, keep, send = final(unit, side, sums, mixed, *last)
    dup, out = pl.pallas_call(
        combine_kernel,
        out_shape=[shape(1, count), shape(count, width)],
        compiler_params=params,
        name="combine",
    )(keep_sums, keep, swap(send))
    return dup[0], out


def solution(mesh):
    placed = (
        P(("groups", "shard", "owner"), None),
        P(("groups", "shard", "owner"), None),
        P(("groups", "shard", "owner")),
    )
    return jax.shard_map(
        local,
        mesh=mesh,
        in_specs=placed,
        out_specs=(P(("groups", "shard", "owner")), P(("groups", "shard", "owner"), None)),
        check_vma=False,
    )
```

```python
import jax
import jax.numpy as jnp
from jax import lax
from jax.experimental import pallas as pl
from jax.experimental.pallas import tpu as pltpu
from jax.sharding import PartitionSpec as P

SUB, LANE = 8, 128
EXTRA = 8
VMEM = 24 * 1024 * 1024


def make_unit(rows):
    wide = rows.astype(jnp.float32)
    scale = lax.rsqrt(jnp.mean(wide * wide, axis=-1, keepdims=True) + 1e-06) / jnp.sqrt(
        jnp.float32(rows.shape[-1])
    )
    return (wide * scale).astype(jnp.bfloat16)


def diagonal(count):
    down = lax.broadcasted_iota(jnp.int32, (count, count), 0)
    return down == lax.broadcasted_iota(jnp.int32, (count, count), 1)


def as_row(column):
    return jnp.sum(jnp.where(diagonal(column.shape[0]), column, 0.0), axis=0, keepdims=True)


def as_column(row):
    return jnp.sum(jnp.where(diagonal(row.shape[1]), row, 0.0), axis=1, keepdims=True)


def halves(value):
    high = value.astype(jnp.bfloat16)
    return high, (value - high.astype(jnp.float32)).astype(jnp.bfloat16)


def pack_kernel(tiles_ref, label_ref, rank_ref, packed_ref):
    many = tiles_ref.shape[0]
    packed_ref[:many] = tiles_ref[...]
    rank = rank_ref[...]
    high = lax.shift_right_logical(rank, 8)
    low = rank - lax.shift_left(high, 8)
    lines = [line.astype(jnp.float32) for line in (label_ref[...], high, low)]
    lines.append(jnp.zeros((SUB - len(lines), LANE), jnp.float32))
    packed_ref[many] = jnp.concatenate(lines, axis=0).astype(jnp.bfloat16)


def labels_and_ranks(block):
    tile = block[block.shape[0] - 1].astype(jnp.float32)
    return tile[0:1], tile[1:2] * 256.0 + tile[2:3]


def rows_of(blocks, width):
    across = width // LANE
    wide = []
    for block in blocks:
        tiles = block[: block.shape[0] - 1].astype(jnp.float32)
        tiles = tiles.reshape(-1, across, SUB, LANE)
        pieces = [tiles[:, at].reshape(-1, LANE) for at in range(across)]
        wide.append(jnp.concatenate(pieces, axis=1))
    return jnp.concatenate(wide, axis=0)


def score(unit, side, blocks):
    own_label, own_rank = side[:, 0:1], side[:, 1:2]
    wide = rows_of(blocks, unit.shape[1])
    keys = wide.astype(jnp.bfloat16)
    sides = [labels_and_ranks(block) for block in blocks]
    label = jnp.concatenate([item[0] for item in sides], axis=1)
    rank = jnp.concatenate([item[1] for item in sides], axis=1)
    cosine = lax.dot_general(
        unit, make_unit(wide), (((1,), (1,)), ((), ())), preferred_element_type=jnp.float32
    )
    weight = 1.0 / (1.0 + jnp.exp(-40.0 * (cosine - 0.05)))
    near = jnp.where((label == own_label) & (rank != own_rank), weight, 0.0)
    earlier = jnp.sum(jnp.where(rank < own_rank, near, 0.0), axis=1, keepdims=True)
    every = jnp.sum(near, axis=1, keepdims=True)
    mixed = jnp.dot(near.astype(jnp.bfloat16), keys, preferred_element_type=jnp.float32)
    return earlier, every, mixed


def first_kernel(own_ref, other_ref, *refs):
    blocks, (unit_ref, side_ref, sums_ref, mixed_ref) = refs[:-4], refs[-4:]
    count = own_ref.shape[0] // (unit_ref.shape[1] // LANE) * SUB
    side_ref[...] = jnp.zeros_like(side_ref)
    sums_ref[...] = jnp.zeros_like(sums_ref)
    unit_ref[...] = make_unit(rows_of([own_ref, other_ref], unit_ref.shape[1]))
    for at, ref in enumerate((own_ref, other_ref)):
        here = slice(at * count, (at + 1) * count)
        label, rank = labels_and_ranks(ref)
        side_ref[here, 0:1] = as_column(label)
        side_ref[here, 1:2] = as_column(rank)
    sums_ref[:, 0:1], sums_ref[:, 1:2], mixed_ref[...] = score(
        unit_ref[...], side_ref, (own_ref,) + blocks
    )


def more_kernel(unit_ref, side_ref, old_sums_ref, old_mixed_ref, *refs):
    blocks, (sums_ref, mixed_ref) = refs[:-2], refs[-2:]
    earlier, every, mixed = score(unit_ref[...], side_ref, blocks)
    sums_ref[...] = old_sums_ref[...]
    sums_ref[:, 0:1] += earlier
    sums_ref[:, 1:2] += every
    mixed_ref[...] = old_mixed_ref[...] + mixed


def final_kernel(unit_ref, side_ref, old_sums_ref, old_mixed_ref, *refs):
    blocks, (keep_sums_ref, keep_ref, send_ref) = refs[:-3], refs[-3:]
    count, width = keep_ref.shape
    earlier, every, mixed = score(unit_ref[...], side_ref, blocks)
    earlier += old_sums_ref[:, 0:1]
    every += old_sums_ref[:, 1:2]
    mixed += old_mixed_ref[...]
    keep_sums_ref[...] = jnp.zeros_like(keep_sums_ref)
    keep_sums_ref[:, 0:1] = earlier[:count]
    keep_sums_ref[:, 1:2] = every[:count]
    keep_ref[...] = mixed[:count]
    send_ref[:count, :] = mixed[count:].astype(jnp.bfloat16)
    pieces = halves(as_row(earlier[count:])) + halves(as_row(every[count:]))
    pieces = [piece.astype(jnp.float32) for piece in pieces]
    pieces.append(jnp.zeros((1, width - 4 * count), jnp.float32))
    line = jnp.concatenate(pieces, axis=1)
    send_ref[count:, :] = jnp.broadcast_to(line, (EXTRA, width)).astype(jnp.bfloat16)


def combine_kernel(sums_ref, mixed_ref, got_ref, dup_ref, out_ref):
    count = mixed_ref.shape[0]
    line = got_ref[count:, :].astype(jnp.float32)[:1]
    parts = [line[:, at * count : (at + 1) * count] for at in range(4)]
    every = sums_ref[:, 1:2] + as_column(parts[2] + parts[3])
    dup_ref[...] = jnp.log1p(as_row(sums_ref[:, 0:1]) + parts[0] + parts[1])
    mixed = mixed_ref[...] + got_ref[:count, :].astype(jnp.float32)
    out_ref[...] = mixed / jnp.sqrt(1.0 + every)


def cost(queries, keys, width):
    return pl.CostEstimate(
        flops=400 * queries * keys * width,
        bytes_accessed=8 * queries * width + 2 * keys * width,
        transcendentals=100 * queries * keys,
    )


def local(embeddings, cluster_id, priority):
    count, width = embeddings.shape
    tiles = count // SUB * (width // LANE)
    shards = lax.axis_size("shard")
    lanes = lax.axis_size("owner")
    rounds = shards // 2
    queries = 2 * count
    bf16, f32 = jnp.bfloat16, jnp.float32
    params = pltpu.CompilerParams(vmem_limit_bytes=VMEM)

    def shape(*dims, dtype=f32):
        return jax.ShapeDtypeStruct(dims, dtype)

    ring = list(range(0, rounds, 2)) + list(range(1, rounds, 2))[::-1]

    def along(array, step):
        pairs = [
            (2 * ring[at] + side, 2 * ring[(at + step) % rounds] + side)
            for at in range(rounds)
            for side in range(2)
        ]
        return lax.ppermute(array, "shard", pairs)

    def across(array):
        return lax.ppermute(array, "shard", [(at, at ^ 1) for at in range(shards)])

    def two_ways(by_ring, step, by_side, ring_lane):
        pairs = []
        for at in range(rounds):
            for side in range(2):
                here, there = 2 * ring[at] + side, 2 * ring[(at + step) % rounds] + side
                pairs += [
                    (here * lanes + lane, (there if lane == ring_lane else here ^ 1) * lanes + lane)
                    for lane in range(lanes)
                ]
        source = jnp.where(lax.axis_index("owner") == ring_lane, by_ring, by_side)
        return lax.ppermute(source, ("shard", "owner"), pairs)

    def swap(array):
        return lax.ppermute(array, "owner", [(at, lanes - 1 - at) for at in range(lanes)])

    def first(*blocks):
        return pl.pallas_call(
            first_kernel,
            out_shape=[
                shape(queries, width, dtype=bf16),
                shape(queries, 128),
                shape(queries, 128),
                shape(queries, width),
            ],
            cost_estimate=cost(queries, (len(blocks) - 1) * count, width),
            compiler_params=params,
            name="first_scores",
        )(*blocks)

    def more(unit, side, sums, mixed, *blocks):
        return pl.pallas_call(
            more_kernel,
            out_shape=[shape(queries, 128), shape(queries, width)],
            input_output_aliases={2: 0, 3: 1},
            cost_estimate=cost(queries, len(blocks) * count, width),
            compiler_params=params,
            name="more_scores",
        )(unit, side, sums, mixed, *blocks)

    def final(unit, side, sums, mixed, *blocks):
        return pl.pallas_call(
            final_kernel,
            out_shape=[
                shape(count, 128),
                shape(count, width),
                shape(count + EXTRA, width, dtype=bf16),
            ],
            cost_estimate=cost(queries, len(blocks) * count, width),
            compiler_params=params,
            name="final_scores",
        )(unit, side, sums, mixed, *blocks)

    pieces = embeddings.reshape(count // SUB, SUB, width // LANE, LANE).transpose(0, 2, 1, 3)
    own = pl.pallas_call(
        pack_kernel,
        out_shape=shape(tiles + 1, SUB, LANE, dtype=bf16),
        compiler_params=params,
        name="pack",
    )(pieces.reshape(tiles, SUB, LANE), cluster_id.reshape(1, count), priority.reshape(1, count))

    moved, beside = along(own, 1), across(own)
    other = swap(own)
    if rounds == 4:
        ahead = along(own, -1)
        moved, beside, other = lax.optimization_barrier((moved, beside, other))
        opposite = along(moved, 1)
        moved_beside = across(moved)
        ahead_beside = two_ways(beside, -1, ahead, lanes - 1)
        other, moved_beside, opposite = lax.optimization_barrier((other, moved_beside, opposite))
        last = [two_ways(moved_beside, 1, opposite, lanes - 1)]
        unit, side, sums, mixed = first(own, other, beside, ahead, ahead_beside)
        sums, mixed = more(unit, side, sums, mixed, moved, moved_beside, opposite)
    else:
        unit, side, sums, mixed = first(own, other, beside)

        def turn(at, state):
            moved, sums, mixed = state
            ahead, beside = along(moved, 1), across(moved)
            sums, mixed = more(unit, side, sums, mixed, moved, beside)
            return ahead, sums, mixed

        moved, sums, mixed = lax.fori_loop(1, rounds - 1, turn, (moved, sums, mixed))
        last = [moved, across(moved)]
    keep_sums, keep, send = final(unit, side, sums, mixed, *last)
    dup, out = pl.pallas_call(
        combine_kernel,
        out_shape=[shape(1, count), shape(count, width)],
        compiler_params=params,
        name="combine",
    )(keep_sums, keep, swap(send))
    return dup[0], out


def solution(mesh):
    placed = (
        P(("groups", "shard", "owner"), None),
        P(("groups", "shard", "owner"), None),
        P(("groups", "shard", "owner")),
    )
    return jax.shard_map(
        local,
        mesh=mesh,
        in_specs=placed,
        out_specs=(P(("groups", "shard", "owner")), P(("groups", "shard", "owner"), None)),
        check_vma=False,
    )
```

```python
import jax
import jax.numpy as jnp
from jax import lax
from jax.experimental import pallas as pl
from jax.experimental.pallas import tpu as pltpu
from jax.sharding import PartitionSpec as P

SUB, LANE = 8, 128
EXTRA = 8
VMEM = 24 * 1024 * 1024


def make_unit(rows):
    wide = rows.astype(jnp.float32)
    scale = lax.rsqrt(jnp.mean(wide * wide, axis=-1, keepdims=True) + 1e-06) / jnp.sqrt(
        jnp.float32(rows.shape[-1])
    )
    return (wide * scale).astype(jnp.bfloat16)


def diagonal(count):
    down = lax.broadcasted_iota(jnp.int32, (count, count), 0)
    return down == lax.broadcasted_iota(jnp.int32, (count, count), 1)


def as_row(column):
    return jnp.sum(jnp.where(diagonal(column.shape[0]), column, 0.0), axis=0, keepdims=True)


def as_column(row):
    return jnp.sum(jnp.where(diagonal(row.shape[1]), row, 0.0), axis=1, keepdims=True)


def halves(value):
    high = value.astype(jnp.bfloat16)
    return high, (value - high.astype(jnp.float32)).astype(jnp.bfloat16)


def pack_kernel(tiles_ref, label_ref, rank_ref, packed_ref):
    many = tiles_ref.shape[0]
    packed_ref[:many] = tiles_ref[...]
    rank = rank_ref[...]
    high = lax.shift_right_logical(rank, 8)
    low = rank - lax.shift_left(high, 8)
    lines = [line.astype(jnp.float32) for line in (label_ref[...], high, low)]
    lines.append(jnp.zeros((SUB - len(lines), LANE), jnp.float32))
    packed_ref[many] = jnp.concatenate(lines, axis=0).astype(jnp.bfloat16)


def labels_and_ranks(block):
    tile = block[block.shape[0] - 1].astype(jnp.float32)
    return tile[0:1], tile[1:2] * 256.0 + tile[2:3]


def rows_of(blocks, width):
    across = width // LANE
    wide = []
    for block in blocks:
        tiles = block[: block.shape[0] - 1].astype(jnp.float32)
        tiles = tiles.reshape(-1, across, SUB, LANE)
        pieces = [tiles[:, at].reshape(-1, LANE) for at in range(across)]
        wide.append(jnp.concatenate(pieces, axis=1))
    return jnp.concatenate(wide, axis=0)


def score(unit, side, blocks):
    own_label, own_rank = side[:, 0:1], side[:, 1:2]
    wide = rows_of(blocks, unit.shape[1])
    keys = wide.astype(jnp.bfloat16)
    sides = [labels_and_ranks(block) for block in blocks]
    label = jnp.concatenate([item[0] for item in sides], axis=1)
    rank = jnp.concatenate([item[1] for item in sides], axis=1)
    cosine = lax.dot_general(
        unit, make_unit(wide), (((1,), (1,)), ((), ())), preferred_element_type=jnp.float32
    )
    weight = 1.0 / (1.0 + jnp.exp(-40.0 * (cosine - 0.05)))
    near = jnp.where((label == own_label) & (rank != own_rank), weight, 0.0)
    earlier = jnp.sum(jnp.where(rank < own_rank, near, 0.0), axis=1, keepdims=True)
    every = jnp.sum(near, axis=1, keepdims=True)
    mixed = jnp.dot(near.astype(jnp.bfloat16), keys, preferred_element_type=jnp.float32)
    return earlier, every, mixed


def first_kernel(own_ref, other_ref, *refs):
    blocks, (unit_ref, side_ref, sums_ref, mixed_ref) = refs[:-4], refs[-4:]
    count = own_ref.shape[0] // (unit_ref.shape[1] // LANE) * SUB
    side_ref[...] = jnp.zeros_like(side_ref)
    sums_ref[...] = jnp.zeros_like(sums_ref)
    unit_ref[...] = make_unit(rows_of([own_ref, other_ref], unit_ref.shape[1]))
    for at, ref in enumerate((own_ref, other_ref)):
        here = slice(at * count, (at + 1) * count)
        label, rank = labels_and_ranks(ref)
        side_ref[here, 0:1] = as_column(label)
        side_ref[here, 1:2] = as_column(rank)
    sums_ref[:, 0:1], sums_ref[:, 1:2], mixed_ref[...] = score(
        unit_ref[...], side_ref, (own_ref,) + blocks
    )


def more_kernel(unit_ref, side_ref, old_sums_ref, old_mixed_ref, *refs):
    blocks, (sums_ref, mixed_ref) = refs[:-2], refs[-2:]
    earlier, every, mixed = score(unit_ref[...], side_ref, blocks)
    sums_ref[...] = old_sums_ref[...]
    sums_ref[:, 0:1] += earlier
    sums_ref[:, 1:2] += every
    mixed_ref[...] = old_mixed_ref[...] + mixed


def final_kernel(unit_ref, side_ref, old_sums_ref, old_mixed_ref, *refs):
    blocks, (keep_sums_ref, keep_ref, send_ref) = refs[:-3], refs[-3:]
    count, width = keep_ref.shape
    earlier, every, mixed = score(unit_ref[...], side_ref, blocks)
    earlier += old_sums_ref[:, 0:1]
    every += old_sums_ref[:, 1:2]
    mixed += old_mixed_ref[...]
    keep_sums_ref[...] = jnp.zeros_like(keep_sums_ref)
    keep_sums_ref[:, 0:1] = earlier[:count]
    keep_sums_ref[:, 1:2] = every[:count]
    keep_ref[...] = mixed[:count]
    send_ref[:count, :] = mixed[count:].astype(jnp.bfloat16)
    pieces = halves(as_row(earlier[count:])) + halves(as_row(every[count:]))
    pieces = [piece.astype(jnp.float32) for piece in pieces]
    pieces.append(jnp.zeros((1, width - 4 * count), jnp.float32))
    line = jnp.concatenate(pieces, axis=1)
    send_ref[count:, :] = jnp.broadcast_to(line, (EXTRA, width)).astype(jnp.bfloat16)


def combine_kernel(sums_ref, mixed_ref, got_ref, dup_ref, out_ref):
    count = mixed_ref.shape[0]
    line = got_ref[count:, :].astype(jnp.float32)[:1]
    parts = [line[:, at * count : (at + 1) * count] for at in range(4)]
    every = sums_ref[:, 1:2] + as_column(parts[2] + parts[3])
    dup_ref[...] = jnp.log1p(as_row(sums_ref[:, 0:1]) + parts[0] + parts[1])
    mixed = mixed_ref[...] + got_ref[:count, :].astype(jnp.float32)
    out_ref[...] = mixed / jnp.sqrt(1.0 + every)


def cost(queries, keys, width):
    return pl.CostEstimate(
        flops=400 * queries * keys * width,
        bytes_accessed=8 * queries * width + 2 * keys * width,
        transcendentals=100 * queries * keys,
    )


def local(embeddings, cluster_id, priority):
    count, width = embeddings.shape
    tiles = count // SUB * (width // LANE)
    shards = lax.axis_size("shard")
    lanes = lax.axis_size("owner")
    rounds = shards // 2
    queries = 2 * count
    bf16, f32 = jnp.bfloat16, jnp.float32
    params = pltpu.CompilerParams(vmem_limit_bytes=VMEM)

    def shape(*dims, dtype=f32):
        return jax.ShapeDtypeStruct(dims, dtype)

    ring = list(range(0, rounds, 2)) + list(range(1, rounds, 2))[::-1]

    def along(array, step):
        pairs = [
            (2 * ring[at] + side, 2 * ring[(at + step) % rounds] + side)
            for at in range(rounds)
            for side in range(2)
        ]
        return lax.ppermute(array, "shard", pairs)

    def across(array):
        return lax.ppermute(array, "shard", [(at, at ^ 1) for at in range(shards)])

    def two_ways(by_ring, step, by_side, ring_lane):
        pairs = []
        for at in range(rounds):
            for side in range(2):
                here, there = 2 * ring[at] + side, 2 * ring[(at + step) % rounds] + side
                pairs += [
                    (here * lanes + lane, (there if lane == ring_lane else here ^ 1) * lanes + lane)
                    for lane in range(lanes)
                ]
        source = jnp.where(lax.axis_index("owner") == ring_lane, by_ring, by_side)
        return lax.ppermute(source, ("shard", "owner"), pairs)

    def swap(array):
        return lax.ppermute(array, "owner", [(at, lanes - 1 - at) for at in range(lanes)])

    def first(*blocks):
        return pl.pallas_call(
            first_kernel,
            out_shape=[
                shape(queries, width, dtype=bf16),
                shape(queries, 128),
                shape(queries, 128),
                shape(queries, width),
            ],
            cost_estimate=cost(queries, (len(blocks) - 1) * count, width),
            compiler_params=params,
            name="first_scores",
        )(*blocks)

    def more(unit, side, sums, mixed, *blocks):
        return pl.pallas_call(
            more_kernel,
            out_shape=[shape(queries, 128), shape(queries, width)],
            input_output_aliases={2: 0, 3: 1},
            cost_estimate=cost(queries, len(blocks) * count, width),
            compiler_params=params,
            name="more_scores",
        )(unit, side, sums, mixed, *blocks)

    def final(unit, side, sums, mixed, *blocks):
        return pl.pallas_call(
            final_kernel,
            out_shape=[
                shape(count, 128),
                shape(count, width),
                shape(count + EXTRA, width, dtype=bf16),
            ],
            cost_estimate=cost(queries, len(blocks) * count, width),
            compiler_params=params,
            name="final_scores",
        )(unit, side, sums, mixed, *blocks)

    pieces = embeddings.reshape(count // SUB, SUB, width // LANE, LANE).transpose(0, 2, 1, 3)
    own = pl.pallas_call(
        pack_kernel,
        out_shape=shape(tiles + 1, SUB, LANE, dtype=bf16),
        compiler_params=params,
        name="pack",
    )(pieces.reshape(tiles, SUB, LANE), cluster_id.reshape(1, count), priority.reshape(1, count))

    moved, beside = along(own, 1), across(own)
    other = swap(own)
    if rounds == 4:
        ahead = along(own, -1)
        moved, beside, other = lax.optimization_barrier((moved, beside, other))
        opposite = along(moved, 1)
        moved_beside = across(moved)
        ahead_beside = two_ways(beside, -1, ahead, 0)
        other, moved_beside, opposite = lax.optimization_barrier((other, moved_beside, opposite))
        last = [two_ways(moved_beside, 1, opposite, lanes - 1)]
        unit, side, sums, mixed = first(own, other, beside, ahead, ahead_beside)
        sums, mixed = more(unit, side, sums, mixed, moved, moved_beside, opposite)
    else:
        unit, side, sums, mixed = first(own, other, beside)

        def turn(at, state):
            moved, sums, mixed = state
            ahead, beside = along(moved, 1), across(moved)
            sums, mixed = more(unit, side, sums, mixed, moved, beside)
            return ahead, sums, mixed

        moved, sums, mixed = lax.fori_loop(1, rounds - 1, turn, (moved, sums, mixed))
        last = [moved, across(moved)]
    keep_sums, keep, send = final(unit, side, sums, mixed, *last)
    dup, out = pl.pallas_call(
        combine_kernel,
        out_shape=[shape(1, count), shape(count, width)],
        compiler_params=params,
        name="combine",
    )(keep_sums, keep, swap(send))
    return dup[0], out


def solution(mesh):
    placed = (
        P(("groups", "shard", "owner"), None),
        P(("groups", "shard", "owner"), None),
        P(("groups", "shard", "owner")),
    )
    return jax.shard_map(
        local,
        mesh=mesh,
        in_specs=placed,
        out_specs=(P(("groups", "shard", "owner")), P(("groups", "shard", "owner"), None)),
        check_vma=False,
    )
```

```python
import jax
import jax.numpy as jnp
from jax import lax
from jax.experimental import pallas as pl
from jax.experimental.pallas import tpu as pltpu
from jax.sharding import PartitionSpec as P

SUB, LANE = 8, 128
EXTRA = 8
VMEM = 24 * 1024 * 1024


def make_unit(rows):
    wide = rows.astype(jnp.float32)
    scale = lax.rsqrt(jnp.mean(wide * wide, axis=-1, keepdims=True) + 1e-06) / jnp.sqrt(
        jnp.float32(rows.shape[-1])
    )
    return (wide * scale).astype(jnp.bfloat16)


def diagonal(count):
    down = lax.broadcasted_iota(jnp.int32, (count, count), 0)
    return down == lax.broadcasted_iota(jnp.int32, (count, count), 1)


def as_row(column):
    return jnp.sum(jnp.where(diagonal(column.shape[0]), column, 0.0), axis=0, keepdims=True)


def as_column(row):
    return jnp.sum(jnp.where(diagonal(row.shape[1]), row, 0.0), axis=1, keepdims=True)


def halves(value):
    high = value.astype(jnp.bfloat16)
    return high, (value - high.astype(jnp.float32)).astype(jnp.bfloat16)


def pack_kernel(tiles_ref, label_ref, rank_ref, packed_ref):
    many = tiles_ref.shape[0]
    packed_ref[:many] = tiles_ref[...]
    rank = rank_ref[...]
    high = lax.shift_right_logical(rank, 8)
    low = rank - lax.shift_left(high, 8)
    lines = [line.astype(jnp.float32) for line in (label_ref[...], high, low)]
    lines.append(jnp.zeros((SUB - len(lines), LANE), jnp.float32))
    packed_ref[many] = jnp.concatenate(lines, axis=0).astype(jnp.bfloat16)


def labels_and_ranks(block):
    tile = block[block.shape[0] - 1].astype(jnp.float32)
    return tile[0:1], tile[1:2] * 256.0 + tile[2:3]


def rows_of(blocks, width):
    across = width // LANE
    wide = []
    for block in blocks:
        tiles = block[: block.shape[0] - 1].astype(jnp.float32)
        tiles = tiles.reshape(-1, across, SUB, LANE)
        pieces = [tiles[:, at].reshape(-1, LANE) for at in range(across)]
        wide.append(jnp.concatenate(pieces, axis=1))
    return jnp.concatenate(wide, axis=0)


def score(unit, side, blocks):
    own_label, own_rank = side[:, 0:1], side[:, 1:2]
    wide = rows_of(blocks, unit.shape[1])
    keys = wide.astype(jnp.bfloat16)
    sides = [labels_and_ranks(block) for block in blocks]
    label = jnp.concatenate([item[0] for item in sides], axis=1)
    rank = jnp.concatenate([item[1] for item in sides], axis=1)
    cosine = lax.dot_general(
        unit, make_unit(wide), (((1,), (1,)), ((), ())), preferred_element_type=jnp.float32
    )
    weight = 1.0 / (1.0 + jnp.exp(-40.0 * (cosine - 0.05)))
    near = jnp.where((label == own_label) & (rank != own_rank), weight, 0.0)
    earlier = jnp.sum(jnp.where(rank < own_rank, near, 0.0), axis=1, keepdims=True)
    every = jnp.sum(near, axis=1, keepdims=True)
    mixed = jnp.dot(near.astype(jnp.bfloat16), keys, preferred_element_type=jnp.float32)
    return earlier, every, mixed


def first_kernel(own_ref, other_ref, *refs):
    blocks, (unit_ref, side_ref, sums_ref, mixed_ref) = refs[:-4], refs[-4:]
    count = own_ref.shape[0] // (unit_ref.shape[1] // LANE) * SUB
    side_ref[...] = jnp.zeros_like(side_ref)
    sums_ref[...] = jnp.zeros_like(sums_ref)
    unit_ref[...] = make_unit(rows_of([own_ref, other_ref], unit_ref.shape[1]))
    for at, ref in enumerate((own_ref, other_ref)):
        here = slice(at * count, (at + 1) * count)
        label, rank = labels_and_ranks(ref)
        side_ref[here, 0:1] = as_column(label)
        side_ref[here, 1:2] = as_column(rank)
    sums_ref[:, 0:1], sums_ref[:, 1:2], mixed_ref[...] = score(
        unit_ref[...], side_ref, (own_ref,) + blocks
    )


def more_kernel(unit_ref, side_ref, old_sums_ref, old_mixed_ref, *refs):
    blocks, (sums_ref, mixed_ref) = refs[:-2], refs[-2:]
    earlier, every, mixed = score(unit_ref[...], side_ref, blocks)
    sums_ref[...] = old_sums_ref[...]
    sums_ref[:, 0:1] += earlier
    sums_ref[:, 1:2] += every
    mixed_ref[...] = old_mixed_ref[...] + mixed


def send_kernel(unit_ref, side_ref, old_sums_ref, old_mixed_ref, *refs):
    blocks, send_ref = refs[:-1], refs[-1]
    count, width = send_ref.shape[0] - EXTRA, send_ref.shape[1]
    earlier, every, mixed = score(unit_ref[count:, :], side_ref[count:, :], blocks)
    earlier += old_sums_ref[count:, 0:1]
    every += old_sums_ref[count:, 1:2]
    send_ref[:count, :] = (mixed + old_mixed_ref[count:, :]).astype(jnp.bfloat16)
    pieces = halves(as_row(earlier)) + halves(as_row(every))
    pieces = [piece.astype(jnp.float32) for piece in pieces]
    pieces.append(jnp.zeros((1, width - 4 * count), jnp.float32))
    line = jnp.concatenate(pieces, axis=1)
    send_ref[count:, :] = jnp.broadcast_to(line, (EXTRA, width)).astype(jnp.bfloat16)


def keep_kernel(unit_ref, side_ref, old_sums_ref, old_mixed_ref, *refs):
    blocks, (sums_ref, mixed_ref) = refs[:-2], refs[-2:]
    count = mixed_ref.shape[0]
    earlier, every, mixed = score(unit_ref[:count, :], side_ref[:count, :], blocks)
    sums_ref[...] = old_sums_ref[:count, :]
    sums_ref[:, 0:1] += earlier
    sums_ref[:, 1:2] += every
    mixed_ref[...] = old_mixed_ref[:count, :] + mixed


def combine_kernel(sums_ref, mixed_ref, got_ref, dup_ref, out_ref):
    count = mixed_ref.shape[0]
    line = got_ref[count:, :].astype(jnp.float32)[:1]
    parts = [line[:, at * count : (at + 1) * count] for at in range(4)]
    every = sums_ref[:, 1:2] + as_column(parts[2] + parts[3])
    dup_ref[...] = jnp.log1p(as_row(sums_ref[:, 0:1]) + parts[0] + parts[1])
    mixed = mixed_ref[...] + got_ref[:count, :].astype(jnp.float32)
    out_ref[...] = mixed / jnp.sqrt(1.0 + every)


def cost(queries, keys, width):
    return pl.CostEstimate(
        flops=400 * queries * keys * width,
        bytes_accessed=8 * queries * width + 2 * keys * width,
        transcendentals=100 * queries * keys,
    )


def local(embeddings, cluster_id, priority):
    count, width = embeddings.shape
    tiles = count // SUB * (width // LANE)
    shards = lax.axis_size("shard")
    lanes = lax.axis_size("owner")
    rounds = shards // 2
    queries = 2 * count
    bf16, f32 = jnp.bfloat16, jnp.float32
    params = pltpu.CompilerParams(vmem_limit_bytes=VMEM)

    def shape(*dims, dtype=f32):
        return jax.ShapeDtypeStruct(dims, dtype)

    ring = list(range(0, rounds, 2)) + list(range(1, rounds, 2))[::-1]

    def along(array, step):
        pairs = [
            (2 * ring[at] + side, 2 * ring[(at + step) % rounds] + side)
            for at in range(rounds)
            for side in range(2)
        ]
        return lax.ppermute(array, "shard", pairs)

    def across(array):
        return lax.ppermute(array, "shard", [(at, at ^ 1) for at in range(shards)])

    def two_ways(by_ring, step, by_side):
        pairs = []
        for at in range(rounds):
            for side in range(2):
                here, there = 2 * ring[at] + side, 2 * ring[(at + step) % rounds] + side
                pairs.append((here * lanes, there * lanes))
                pairs += [(here * lanes + lane, (here ^ 1) * lanes + lane) for lane in range(1, lanes)]
        source = jnp.where(lax.axis_index("owner") == 0, by_ring, by_side)
        return lax.ppermute(source, ("shard", "owner"), pairs)

    def swap(array):
        return lax.ppermute(array, "owner", [(at, lanes - 1 - at) for at in range(lanes)])

    def first(*blocks):
        return pl.pallas_call(
            first_kernel,
            out_shape=[
                shape(queries, width, dtype=bf16),
                shape(queries, 128),
                shape(queries, 128),
                shape(queries, width),
            ],
            cost_estimate=cost(queries, (len(blocks) - 1) * count, width),
            compiler_params=params,
            name="first_scores",
        )(*blocks)

    def more(unit, side, sums, mixed, *blocks):
        return pl.pallas_call(
            more_kernel,
            out_shape=[shape(queries, 128), shape(queries, width)],
            input_output_aliases={2: 0, 3: 1},
            cost_estimate=cost(queries, len(blocks) * count, width),
            compiler_params=params,
            name="more_scores",
        )(unit, side, sums, mixed, *blocks)

    def final(unit, side, sums, mixed, *blocks):
        send = pl.pallas_call(
            send_kernel,
            out_shape=shape(count + EXTRA, width, dtype=bf16),
            cost_estimate=cost(count, len(blocks) * count, width),
            compiler_params=params,
            name="send_scores",
        )(unit, side, sums, mixed, *blocks)
        keep_sums, keep = pl.pallas_call(
            keep_kernel,
            out_shape=[shape(count, 128), shape(count, width)],
            cost_estimate=cost(count, len(blocks) * count, width),
            compiler_params=params,
            name="keep_scores",
        )(unit, side, sums, mixed, *blocks)
        return keep_sums, keep, send

    pieces = embeddings.reshape(count // SUB, SUB, width // LANE, LANE).transpose(0, 2, 1, 3)
    own = pl.pallas_call(
        pack_kernel,
        out_shape=shape(tiles + 1, SUB, LANE, dtype=bf16),
        compiler_params=params,
        name="pack",
    )(pieces.reshape(tiles, SUB, LANE), cluster_id.reshape(1, count), priority.reshape(1, count))

    moved, beside = along(own, 1), across(own)
    other = swap(own)
    if rounds == 4:
        ahead = along(own, -1)
        moved, beside, other = lax.optimization_barrier((moved, beside, other))
        opposite = along(moved, 1)
        moved_beside = across(moved)
        ahead_beside = across(ahead)
        other, moved_beside, opposite = lax.optimization_barrier((other, moved_beside, opposite))
        last = [two_ways(moved_beside, 1, opposite)]
        unit, side, sums, mixed = first(own, other, beside, moved, moved_beside)
        sums, mixed = more(unit, side, sums, mixed, ahead, opposite, ahead_beside)
    else:
        unit, side, sums, mixed = first(own, other, beside)

        def turn(at, state):
            moved, sums, mixed = state
            ahead, beside = along(moved, 1), across(moved)
            sums, mixed = more(unit, side, sums, mixed, moved, beside)
            return ahead, sums, mixed

        moved, sums, mixed = lax.fori_loop(1, rounds - 1, turn, (moved, sums, mixed))
        last = [moved, across(moved)]
    keep_sums, keep, send = final(unit, side, sums, mixed, *last)
    dup, out = pl.pallas_call(
        combine_kernel,
        out_shape=[shape(1, count), shape(count, width)],
        compiler_params=params,
        name="combine",
    )(keep_sums, keep, swap(send))
    return dup[0], out


def solution(mesh):
    placed = (
        P(("groups", "shard", "owner"), None),
        P(("groups", "shard", "owner"), None),
        P(("groups", "shard", "owner")),
    )
    return jax.shard_map(
        local,
        mesh=mesh,
        in_specs=placed,
        out_specs=(P(("groups", "shard", "owner")), P(("groups", "shard", "owner"), None)),
        check_vma=False,
    )
```

```python
import jax
import jax.numpy as jnp
from jax import lax
from jax.experimental import pallas as pl
from jax.experimental.pallas import tpu as pltpu
from jax.sharding import PartitionSpec as P

SUB, LANE = 8, 128
EXTRA = 8
VMEM = 24 * 1024 * 1024


def make_unit(rows):
    wide = rows.astype(jnp.float32)
    scale = lax.rsqrt(jnp.mean(wide * wide, axis=-1, keepdims=True) + 1e-06) / jnp.sqrt(
        jnp.float32(rows.shape[-1])
    )
    return (wide * scale).astype(jnp.bfloat16)


def diagonal(count):
    down = lax.broadcasted_iota(jnp.int32, (count, count), 0)
    return down == lax.broadcasted_iota(jnp.int32, (count, count), 1)


def as_row(column):
    return jnp.sum(jnp.where(diagonal(column.shape[0]), column, 0.0), axis=0, keepdims=True)


def as_column(row):
    return jnp.sum(jnp.where(diagonal(row.shape[1]), row, 0.0), axis=1, keepdims=True)


def halves(value):
    high = value.astype(jnp.bfloat16)
    return high, (value - high.astype(jnp.float32)).astype(jnp.bfloat16)


def base_kernel(base_ref):
    base_ref[...] = jnp.zeros_like(base_ref)


def pack_kernel(tiles_ref, label_ref, rank_ref, base_ref, packed_ref):
    many = tiles_ref.shape[0]
    packed_ref[:many] = tiles_ref[...]
    rank = rank_ref[...]
    high = lax.shift_right_logical(rank, 8)
    low = rank - lax.shift_left(high, 8)
    lines = [line.astype(jnp.float32) for line in (label_ref[...], high, low)]
    lines.append(base_ref[len(lines) :, :])
    packed_ref[many] = jnp.concatenate(lines, axis=0).astype(jnp.bfloat16)


def labels_and_ranks(block):
    tile = block[block.shape[0] - 1].astype(jnp.float32)
    return tile[0:1], tile[1:2] * 256.0 + tile[2:3]


def rows_of(blocks, width):
    across = width // LANE
    wide = []
    for block in blocks:
        tiles = block[: block.shape[0] - 1].astype(jnp.float32)
        tiles = tiles.reshape(-1, across, SUB, LANE)
        pieces = [tiles[:, at].reshape(-1, LANE) for at in range(across)]
        wide.append(jnp.concatenate(pieces, axis=1))
    return jnp.concatenate(wide, axis=0)


def score(unit, side, blocks):
    own_label, own_rank = side[:, 0:1], side[:, 1:2]
    wide = rows_of(blocks, unit.shape[1])
    keys = wide.astype(jnp.bfloat16)
    sides = [labels_and_ranks(block) for block in blocks]
    label = jnp.concatenate([item[0] for item in sides], axis=1)
    rank = jnp.concatenate([item[1] for item in sides], axis=1)
    cosine = lax.dot_general(
        unit, make_unit(wide), (((1,), (1,)), ((), ())), preferred_element_type=jnp.float32
    )
    weight = 1.0 / (1.0 + jnp.exp(-40.0 * (cosine - 0.05)))
    near = jnp.where((label == own_label) & (rank != own_rank), weight, 0.0)
    earlier = jnp.sum(jnp.where(rank < own_rank, near, 0.0), axis=1, keepdims=True)
    every = jnp.sum(near, axis=1, keepdims=True)
    mixed = jnp.dot(near.astype(jnp.bfloat16), keys, preferred_element_type=jnp.float32)
    return earlier, every, mixed


def first_kernel(own_ref, other_ref, *refs):
    blocks, (unit_ref, side_ref, sums_ref, mixed_ref) = refs[:-4], refs[-4:]
    count = own_ref.shape[0] // (unit_ref.shape[1] // LANE) * SUB
    side_ref[...] = jnp.zeros_like(side_ref)
    sums_ref[...] = jnp.zeros_like(sums_ref)
    unit_ref[...] = make_unit(rows_of([own_ref, other_ref], unit_ref.shape[1]))
    for at, ref in enumerate((own_ref, other_ref)):
        here = slice(at * count, (at + 1) * count)
        label, rank = labels_and_ranks(ref)
        side_ref[here, 0:1] = as_column(label)
        side_ref[here, 1:2] = as_column(rank)
    sums_ref[:, 0:1], sums_ref[:, 1:2], mixed_ref[...] = score(
        unit_ref[...], side_ref, (own_ref,) + blocks
    )


def more_kernel(unit_ref, side_ref, old_sums_ref, old_mixed_ref, *refs):
    blocks, (sums_ref, mixed_ref) = refs[:-2], refs[-2:]
    earlier, every, mixed = score(unit_ref[...], side_ref, blocks)
    sums_ref[...] = old_sums_ref[...]
    sums_ref[:, 0:1] += earlier
    sums_ref[:, 1:2] += every
    mixed_ref[...] = old_mixed_ref[...] + mixed


def send_kernel(unit_ref, side_ref, old_sums_ref, old_mixed_ref, *refs):
    blocks, send_ref = refs[:-1], refs[-1]
    count, width = send_ref.shape[0] - EXTRA, send_ref.shape[1]
    earlier, every, mixed = score(unit_ref[count:, :], side_ref[count:, :], blocks)
    earlier += old_sums_ref[count:, 0:1]
    every += old_sums_ref[count:, 1:2]
    send_ref[:count, :] = (mixed + old_mixed_ref[count:, :]).astype(jnp.bfloat16)
    pieces = halves(as_row(earlier)) + halves(as_row(every))
    pieces = [piece.astype(jnp.float32) for piece in pieces]
    pieces.append(jnp.zeros((1, width - 4 * count), jnp.float32))
    line = jnp.concatenate(pieces, axis=1)
    send_ref[count:, :] = jnp.broadcast_to(line, (EXTRA, width)).astype(jnp.bfloat16)


def keep_kernel(unit_ref, side_ref, old_sums_ref, old_mixed_ref, *refs):
    blocks, (sums_ref, mixed_ref) = refs[:-2], refs[-2:]
    count = mixed_ref.shape[0]
    earlier, every, mixed = score(unit_ref[:count, :], side_ref[:count, :], blocks)
    sums_ref[...] = old_sums_ref[:count, :]
    sums_ref[:, 0:1] += earlier
    sums_ref[:, 1:2] += every
    mixed_ref[...] = old_mixed_ref[:count, :] + mixed


def combine_kernel(sums_ref, mixed_ref, got_ref, dup_ref, out_ref):
    count = mixed_ref.shape[0]
    line = got_ref[count:, :].astype(jnp.float32)[:1]
    parts = [line[:, at * count : (at + 1) * count] for at in range(4)]
    every = sums_ref[:, 1:2] + as_column(parts[2] + parts[3])
    dup_ref[...] = jnp.log1p(as_row(sums_ref[:, 0:1]) + parts[0] + parts[1])
    mixed = mixed_ref[...] + got_ref[:count, :].astype(jnp.float32)
    out_ref[...] = mixed / jnp.sqrt(1.0 + every)


def cost(queries, keys, width):
    return pl.CostEstimate(
        flops=400 * queries * keys * width,
        bytes_accessed=8 * queries * width + 2 * keys * width,
        transcendentals=100 * queries * keys,
    )


def local(embeddings, cluster_id, priority):
    count, width = embeddings.shape
    tiles = count // SUB * (width // LANE)
    shards = lax.axis_size("shard")
    lanes = lax.axis_size("owner")
    rounds = shards // 2
    queries = 2 * count
    bf16, f32 = jnp.bfloat16, jnp.float32
    params = pltpu.CompilerParams(vmem_limit_bytes=VMEM)

    def shape(*dims, dtype=f32):
        return jax.ShapeDtypeStruct(dims, dtype)

    ring = list(range(0, rounds, 2)) + list(range(1, rounds, 2))[::-1]

    def along(array, step):
        pairs = [
            (2 * ring[at] + side, 2 * ring[(at + step) % rounds] + side)
            for at in range(rounds)
            for side in range(2)
        ]
        return lax.ppermute(array, "shard", pairs)

    def across(array):
        return lax.ppermute(array, "shard", [(at, at ^ 1) for at in range(shards)])

    def two_ways(by_ring, step, by_side):
        pairs = []
        for at in range(rounds):
            for side in range(2):
                here, there = 2 * ring[at] + side, 2 * ring[(at + step) % rounds] + side
                pairs.append((here * lanes, there * lanes))
                pairs += [(here * lanes + lane, (here ^ 1) * lanes + lane) for lane in range(1, lanes)]
        source = jnp.where(lax.axis_index("owner") == 0, by_ring, by_side)
        return lax.ppermute(source, ("shard", "owner"), pairs)

    def swap(array):
        return lax.ppermute(array, "owner", [(at, lanes - 1 - at) for at in range(lanes)])

    def first(*blocks):
        return pl.pallas_call(
            first_kernel,
            out_shape=[
                shape(queries, width, dtype=bf16),
                shape(queries, 128),
                shape(queries, 128),
                shape(queries, width),
            ],
            cost_estimate=cost(queries, (len(blocks) - 1) * count, width),
            compiler_params=params,
            name="first_scores",
        )(*blocks)

    def more(unit, side, sums, mixed, *blocks):
        return pl.pallas_call(
            more_kernel,
            out_shape=[shape(queries, 128), shape(queries, width)],
            input_output_aliases={2: 0, 3: 1},
            cost_estimate=cost(queries, len(blocks) * count, width),
            compiler_params=params,
            name="more_scores",
        )(unit, side, sums, mixed, *blocks)

    def final(unit, side, sums, mixed, *blocks):
        send = pl.pallas_call(
            send_kernel,
            out_shape=shape(count + EXTRA, width, dtype=bf16),
            cost_estimate=cost(count, len(blocks) * count, width),
            compiler_params=params,
            name="send_scores",
        )(unit, side, sums, mixed, *blocks)
        keep_sums, keep = pl.pallas_call(
            keep_kernel,
            out_shape=[shape(count, 128), shape(count, width)],
            cost_estimate=cost(count, len(blocks) * count, width),
            compiler_params=params,
            name="keep_scores",
        )(unit, side, sums, mixed, *blocks)
        return keep_sums, keep, send

    pieces = embeddings.reshape(count // SUB, SUB, width // LANE, LANE).transpose(0, 2, 1, 3)
    base = pl.pallas_call(
        base_kernel,
        out_shape=shape(SUB, LANE),
        cost_estimate=pl.CostEstimate(flops=1000000000, bytes_accessed=0, transcendentals=0),
        compiler_params=params,
        name="base",
    )()
    own = pl.pallas_call(
        pack_kernel,
        out_shape=shape(tiles + 1, SUB, LANE, dtype=bf16),
        compiler_params=params,
        name="pack",
    )(pieces.reshape(tiles, SUB, LANE), cluster_id.reshape(1, count), priority.reshape(1, count), base)

    moved, beside = along(own, 1), across(own)
    other = swap(own)
    if rounds == 4:
        ahead = along(own, -1)
        moved, beside, other = lax.optimization_barrier((moved, beside, other))
        opposite = along(moved, 1)
        moved_beside = across(moved)
        ahead_beside = across(ahead)
        other, moved_beside, opposite = lax.optimization_barrier((other, moved_beside, opposite))
        last = [two_ways(moved_beside, 1, opposite)]
        unit, side, sums, mixed = first(own, other, beside, moved, moved_beside)
        sums, mixed = more(unit, side, sums, mixed, ahead, opposite, ahead_beside)
    else:
        unit, side, sums, mixed = first(own, other, beside)

        def turn(at, state):
            moved, sums, mixed = state
            ahead, beside = along(moved, 1), across(moved)
            sums, mixed = more(unit, side, sums, mixed, moved, beside)
            return ahead, sums, mixed

        moved, sums, mixed = lax.fori_loop(1, rounds - 1, turn, (moved, sums, mixed))
        last = [moved, across(moved)]
    keep_sums, keep, send = final(unit, side, sums, mixed, *last)
    dup, out = pl.pallas_call(
        combine_kernel,
        out_shape=[shape(1, count), shape(count, width)],
        compiler_params=params,
        name="combine",
    )(keep_sums, keep, swap(send))
    return dup[0], out


def solution(mesh):
    placed = (
        P(("groups", "shard", "owner"), None),
        P(("groups", "shard", "owner"), None),
        P(("groups", "shard", "owner")),
    )
    return jax.shard_map(
        local,
        mesh=mesh,
        in_specs=placed,
        out_specs=(P(("groups", "shard", "owner")), P(("groups", "shard", "owner"), None)),
        check_vma=False,
    )
```

```python
import jax
import jax.numpy as jnp
from jax import lax
from jax.experimental import pallas as pl
from jax.experimental.pallas import tpu as pltpu
from jax.sharding import PartitionSpec as P

SUB, LANE = 8, 128
EXTRA = 8
VMEM = 24 * 1024 * 1024


def make_unit(rows):
    wide = rows.astype(jnp.float32)
    scale = lax.rsqrt(jnp.mean(wide * wide, axis=-1, keepdims=True) + 1e-06) / jnp.sqrt(
        jnp.float32(rows.shape[-1])
    )
    return (wide * scale).astype(jnp.bfloat16)


def diagonal(count):
    down = lax.broadcasted_iota(jnp.int32, (count, count), 0)
    return down == lax.broadcasted_iota(jnp.int32, (count, count), 1)


def as_row(column):
    return jnp.sum(jnp.where(diagonal(column.shape[0]), column, 0.0), axis=0, keepdims=True)


def as_column(row):
    return jnp.sum(jnp.where(diagonal(row.shape[1]), row, 0.0), axis=1, keepdims=True)


def halves(value):
    high = value.astype(jnp.bfloat16)
    return high, (value - high.astype(jnp.float32)).astype(jnp.bfloat16)


def base_kernel(base_ref):
    base_ref[...] = jnp.zeros_like(base_ref)


def pack_kernel(tiles_ref, label_ref, rank_ref, base_ref, packed_ref):
    many = tiles_ref.shape[0]
    packed_ref[:many] = tiles_ref[...]
    rank = rank_ref[...]
    high = lax.shift_right_logical(rank, 8)
    low = rank - lax.shift_left(high, 8)
    lines = [line.astype(jnp.float32) for line in (label_ref[...], high, low)]
    lines.append(base_ref[len(lines) :, :])
    packed_ref[many] = jnp.concatenate(lines, axis=0).astype(jnp.bfloat16)


def labels_and_ranks(block):
    tile = block[block.shape[0] - 1].astype(jnp.float32)
    return tile[0:1], tile[1:2] * 256.0 + tile[2:3]


def rows_of(blocks, width):
    across = width // LANE
    wide = []
    for block in blocks:
        tiles = block[: block.shape[0] - 1].astype(jnp.float32)
        tiles = tiles.reshape(-1, across, SUB, LANE)
        pieces = [tiles[:, at].reshape(-1, LANE) for at in range(across)]
        wide.append(jnp.concatenate(pieces, axis=1))
    return jnp.concatenate(wide, axis=0)


def score(unit, side, blocks):
    own_label, own_rank = side[:, 0:1], side[:, 1:2]
    wide = rows_of(blocks, unit.shape[1])
    keys = wide.astype(jnp.bfloat16)
    sides = [labels_and_ranks(block) for block in blocks]
    label = jnp.concatenate([item[0] for item in sides], axis=1)
    rank = jnp.concatenate([item[1] for item in sides], axis=1)
    cosine = lax.dot_general(
        unit, make_unit(wide), (((1,), (1,)), ((), ())), preferred_element_type=jnp.float32
    )
    weight = 1.0 / (1.0 + jnp.exp(-40.0 * (cosine - 0.05)))
    near = jnp.where((label == own_label) & (rank != own_rank), weight, 0.0)
    earlier = jnp.sum(jnp.where(rank < own_rank, near, 0.0), axis=1, keepdims=True)
    every = jnp.sum(near, axis=1, keepdims=True)
    mixed = jnp.dot(near.astype(jnp.bfloat16), keys, preferred_element_type=jnp.float32)
    return earlier, every, mixed


def first_kernel(own_ref, other_ref, *refs):
    blocks, (unit_ref, side_ref, sums_ref, mixed_ref) = refs[:-4], refs[-4:]
    count = own_ref.shape[0] // (unit_ref.shape[1] // LANE) * SUB
    side_ref[...] = jnp.zeros_like(side_ref)
    sums_ref[...] = jnp.zeros_like(sums_ref)
    unit_ref[...] = make_unit(rows_of([own_ref, other_ref], unit_ref.shape[1]))
    for at, ref in enumerate((own_ref, other_ref)):
        here = slice(at * count, (at + 1) * count)
        label, rank = labels_and_ranks(ref)
        side_ref[here, 0:1] = as_column(label)
        side_ref[here, 1:2] = as_column(rank)
    sums_ref[:, 0:1], sums_ref[:, 1:2], mixed_ref[...] = score(
        unit_ref[...], side_ref, (own_ref,) + blocks
    )


def more_kernel(unit_ref, side_ref, old_sums_ref, old_mixed_ref, *refs):
    blocks, (sums_ref, mixed_ref) = refs[:-2], refs[-2:]
    earlier, every, mixed = score(unit_ref[...], side_ref, blocks)
    sums_ref[...] = old_sums_ref[...]
    sums_ref[:, 0:1] += earlier
    sums_ref[:, 1:2] += every
    mixed_ref[...] = old_mixed_ref[...] + mixed


def send_kernel(unit_ref, side_ref, old_sums_ref, old_mixed_ref, *refs):
    blocks, send_ref = refs[:-1], refs[-1]
    count, width = send_ref.shape[0] - EXTRA, send_ref.shape[1]
    earlier, every, mixed = score(unit_ref[count:, :], side_ref[count:, :], blocks)
    earlier += old_sums_ref[count:, 0:1]
    every += old_sums_ref[count:, 1:2]
    send_ref[:count, :] = (mixed + old_mixed_ref[count:, :]).astype(jnp.bfloat16)
    pieces = halves(as_row(earlier)) + halves(as_row(every))
    pieces = [piece.astype(jnp.float32) for piece in pieces]
    pieces.append(jnp.zeros((1, width - 4 * count), jnp.float32))
    line = jnp.concatenate(pieces, axis=1)
    send_ref[count:, :] = jnp.broadcast_to(line, (EXTRA, width)).astype(jnp.bfloat16)


def keep_kernel(unit_ref, side_ref, old_sums_ref, old_mixed_ref, *refs):
    blocks, (sums_ref, mixed_ref) = refs[:-2], refs[-2:]
    count = mixed_ref.shape[0]
    earlier, every, mixed = score(unit_ref[:count, :], side_ref[:count, :], blocks)
    sums_ref[...] = old_sums_ref[:count, :]
    sums_ref[:, 0:1] += earlier
    sums_ref[:, 1:2] += every
    mixed_ref[...] = old_mixed_ref[:count, :] + mixed


def combine_kernel(sums_ref, mixed_ref, got_ref, dup_ref, out_ref):
    count = mixed_ref.shape[0]
    line = got_ref[count:, :].astype(jnp.float32)[:1]
    parts = [line[:, at * count : (at + 1) * count] for at in range(4)]
    every = sums_ref[:, 1:2] + as_column(parts[2] + parts[3])
    dup_ref[...] = jnp.log1p(as_row(sums_ref[:, 0:1]) + parts[0] + parts[1])
    mixed = mixed_ref[...] + got_ref[:count, :].astype(jnp.float32)
    out_ref[...] = mixed / jnp.sqrt(1.0 + every)


def cost(queries, keys, width):
    return pl.CostEstimate(
        flops=400 * queries * keys * width,
        bytes_accessed=8 * queries * width + 2 * keys * width,
        transcendentals=100 * queries * keys,
    )


def local(embeddings, cluster_id, priority):
    count, width = embeddings.shape
    tiles = count // SUB * (width // LANE)
    shards = lax.axis_size("shard")
    lanes = lax.axis_size("owner")
    rounds = shards // 2
    queries = 2 * count
    bf16, f32 = jnp.bfloat16, jnp.float32
    params = pltpu.CompilerParams(vmem_limit_bytes=VMEM)

    def shape(*dims, dtype=f32):
        return jax.ShapeDtypeStruct(dims, dtype)

    ring = list(range(0, rounds, 2)) + list(range(1, rounds, 2))[::-1]

    def along(array, step):
        pairs = [
            (2 * ring[at] + side, 2 * ring[(at + step) % rounds] + side)
            for at in range(rounds)
            for side in range(2)
        ]
        return lax.ppermute(array, "shard", pairs)

    def across(array):
        return lax.ppermute(array, "shard", [(at, at ^ 1) for at in range(shards)])

    def one_lane(array, lane, step):
        pairs = []
        for at in range(rounds):
            for side in range(2):
                here, there = 2 * ring[at] + side, 2 * ring[(at + step) % rounds] + side
                there = there if step else here ^ 1
                pairs.append((here * lanes + lane, there * lanes + lane))
        return lax.ppermute(array, ("shard", "owner"), pairs)

    def swap(array):
        return lax.ppermute(array, "owner", [(at, lanes - 1 - at) for at in range(lanes)])

    def first(*blocks):
        return pl.pallas_call(
            first_kernel,
            out_shape=[
                shape(queries, width, dtype=bf16),
                shape(queries, 128),
                shape(queries, 128),
                shape(queries, width),
            ],
            cost_estimate=cost(queries, (len(blocks) - 1) * count, width),
            compiler_params=params,
            name="first_scores",
        )(*blocks)

    def more(unit, side, sums, mixed, *blocks):
        return pl.pallas_call(
            more_kernel,
            out_shape=[shape(queries, 128), shape(queries, width)],
            input_output_aliases={2: 0, 3: 1},
            cost_estimate=cost(queries, len(blocks) * count, width),
            compiler_params=params,
            name="more_scores",
        )(unit, side, sums, mixed, *blocks)

    def final(unit, side, sums, mixed, *blocks):
        send = pl.pallas_call(
            send_kernel,
            out_shape=shape(count + EXTRA, width, dtype=bf16),
            cost_estimate=cost(count, len(blocks) * count, width),
            compiler_params=params,
            name="send_scores",
        )(unit, side, sums, mixed, *blocks)
        keep_sums, keep = pl.pallas_call(
            keep_kernel,
            out_shape=[shape(count, 128), shape(count, width)],
            cost_estimate=cost(count, len(blocks) * count, width),
            compiler_params=params,
            name="keep_scores",
        )(unit, side, sums, mixed, *blocks)
        return keep_sums, keep, send

    pieces = embeddings.reshape(count // SUB, SUB, width // LANE, LANE).transpose(0, 2, 1, 3)
    base = pl.pallas_call(
        base_kernel,
        out_shape=shape(SUB, LANE),
        cost_estimate=pl.CostEstimate(flops=1000000000, bytes_accessed=0, transcendentals=0),
        compiler_params=params,
        name="base",
    )()
    own = pl.pallas_call(
        pack_kernel,
        out_shape=shape(tiles + 1, SUB, LANE, dtype=bf16),
        compiler_params=params,
        name="pack",
    )(pieces.reshape(tiles, SUB, LANE), cluster_id.reshape(1, count), priority.reshape(1, count), base)

    moved, beside = along(own, 1), across(own)
    other = swap(own)
    if rounds == 4:
        ahead = along(own, -1)
        moved, beside, other = lax.optimization_barrier((moved, beside, other))
        opposite = along(moved, 1)
        moved_beside = across(moved)
        ahead_beside = across(ahead)
        by_ring = one_lane(moved_beside, 0, 1)
        by_side = one_lane(opposite, lanes - 1, 0)
        unit, side, sums, mixed = first(own, other, beside, moved, moved_beside)
        sums, mixed = more(unit, side, sums, mixed, ahead, opposite, ahead_beside)
        last = [jnp.where(lax.axis_index("owner") == 0, by_ring, by_side)]
    else:
        unit, side, sums, mixed = first(own, other, beside)

        def turn(at, state):
            moved, sums, mixed = state
            ahead, beside = along(moved, 1), across(moved)
            sums, mixed = more(unit, side, sums, mixed, moved, beside)
            return ahead, sums, mixed

        moved, sums, mixed = lax.fori_loop(1, rounds - 1, turn, (moved, sums, mixed))
        last = [moved, across(moved)]
    keep_sums, keep, send = final(unit, side, sums, mixed, *last)
    dup, out = pl.pallas_call(
        combine_kernel,
        out_shape=[shape(1, count), shape(count, width)],
        compiler_params=params,
        name="combine",
    )(keep_sums, keep, swap(send))
    return dup[0], out


def solution(mesh):
    placed = (
        P(("groups", "shard", "owner"), None),
        P(("groups", "shard", "owner"), None),
        P(("groups", "shard", "owner")),
    )
    return jax.shard_map(
        local,
        mesh=mesh,
        in_specs=placed,
        out_specs=(P(("groups", "shard", "owner")), P(("groups", "shard", "owner"), None)),
        check_vma=False,
    )
```

```python
import jax
import jax.numpy as jnp
from jax import lax
from jax.experimental import pallas as pl
from jax.experimental.pallas import tpu as pltpu
from jax.sharding import PartitionSpec as P

SUB, LANE = 8, 128
EXTRA = 8
PIECES = 8
VMEM = 24 * 1024 * 1024


def make_unit(rows):
    wide = rows.astype(jnp.float32)
    scale = lax.rsqrt(jnp.mean(wide * wide, axis=-1, keepdims=True) + 1e-06) / jnp.sqrt(
        jnp.float32(rows.shape[-1])
    )
    return (wide * scale).astype(jnp.bfloat16)


def diagonal(count):
    down = lax.broadcasted_iota(jnp.int32, (count, count), 0)
    return down == lax.broadcasted_iota(jnp.int32, (count, count), 1)


def as_row(column):
    return jnp.sum(jnp.where(diagonal(column.shape[0]), column, 0.0), axis=0, keepdims=True)


def as_column(row):
    return jnp.sum(jnp.where(diagonal(row.shape[1]), row, 0.0), axis=1, keepdims=True)


def halves(value):
    high = value.astype(jnp.bfloat16)
    return high, (value - high.astype(jnp.float32)).astype(jnp.bfloat16)


def base_kernel(base_ref):
    base_ref[...] = jnp.zeros_like(base_ref)


def pack_kernel(tiles_ref, label_ref, rank_ref, base_ref, packed_ref):
    many = tiles_ref.shape[0]
    packed_ref[:many] = tiles_ref[...]
    rank = rank_ref[...]
    high = lax.shift_right_logical(rank, 8)
    low = rank - lax.shift_left(high, 8)
    lines = [line.astype(jnp.float32) for line in (label_ref[...], high, low)]
    lines.append(base_ref[len(lines) :, :])
    packed_ref[many] = jnp.concatenate(lines, axis=0).astype(jnp.bfloat16)


def labels_and_ranks(block):
    tile = block[block.shape[0] - 1].astype(jnp.float32)
    return tile[0:1], tile[1:2] * 256.0 + tile[2:3]


def rows_of(blocks, width):
    across = width // LANE
    wide = []
    for block in blocks:
        tiles = block[: block.shape[0] - 1].astype(jnp.float32)
        tiles = tiles.reshape(-1, across, SUB, LANE)
        pieces = [tiles[:, at].reshape(-1, LANE) for at in range(across)]
        wide.append(jnp.concatenate(pieces, axis=1))
    return jnp.concatenate(wide, axis=0)


def score(unit, side, blocks):
    own_label, own_rank = side[:, 0:1], side[:, 1:2]
    wide = rows_of(blocks, unit.shape[1])
    keys = wide.astype(jnp.bfloat16)
    sides = [labels_and_ranks(block) for block in blocks]
    label = jnp.concatenate([item[0] for item in sides], axis=1)
    rank = jnp.concatenate([item[1] for item in sides], axis=1)
    cosine = lax.dot_general(
        unit, make_unit(wide), (((1,), (1,)), ((), ())), preferred_element_type=jnp.float32
    )
    weight = 1.0 / (1.0 + jnp.exp(-40.0 * (cosine - 0.05)))
    near = jnp.where((label == own_label) & (rank != own_rank), weight, 0.0)
    earlier = jnp.sum(jnp.where(rank < own_rank, near, 0.0), axis=1, keepdims=True)
    every = jnp.sum(near, axis=1, keepdims=True)
    mixed = jnp.dot(near.astype(jnp.bfloat16), keys, preferred_element_type=jnp.float32)
    return earlier, every, mixed


def first_kernel(own_ref, other_ref, *refs):
    blocks, (unit_ref, side_ref, sums_ref, mixed_ref) = refs[:-4], refs[-4:]
    count = own_ref.shape[0] // (unit_ref.shape[1] // LANE) * SUB
    side_ref[...] = jnp.zeros_like(side_ref)
    sums_ref[...] = jnp.zeros_like(sums_ref)
    unit_ref[...] = make_unit(rows_of([own_ref, other_ref], unit_ref.shape[1]))
    for at, ref in enumerate((own_ref, other_ref)):
        here = slice(at * count, (at + 1) * count)
        label, rank = labels_and_ranks(ref)
        side_ref[here, 0:1] = as_column(label)
        side_ref[here, 1:2] = as_column(rank)
    sums_ref[:, 0:1], sums_ref[:, 1:2], mixed_ref[...] = score(
        unit_ref[...], side_ref, (own_ref,) + blocks
    )


def more_kernel(unit_ref, side_ref, old_sums_ref, old_mixed_ref, *refs):
    blocks, (sums_ref, mixed_ref) = refs[:-2], refs[-2:]
    earlier, every, mixed = score(unit_ref[...], side_ref, blocks)
    sums_ref[...] = old_sums_ref[...]
    sums_ref[:, 0:1] += earlier
    sums_ref[:, 1:2] += every
    mixed_ref[...] = old_mixed_ref[...] + mixed


def send_kernel(unit_ref, side_ref, old_sums_ref, old_mixed_ref, *refs):
    blocks, send_ref = refs[:-1], refs[-1]
    count, width = send_ref.shape[0] - EXTRA, send_ref.shape[1]
    earlier, every, mixed = score(unit_ref[count:, :], side_ref[count:, :], blocks)
    earlier += old_sums_ref[count:, 0:1]
    every += old_sums_ref[count:, 1:2]
    send_ref[:count, :] = (mixed + old_mixed_ref[count:, :]).astype(jnp.bfloat16)
    pieces = halves(as_row(earlier)) + halves(as_row(every))
    pieces = [piece.astype(jnp.float32) for piece in pieces]
    pieces.append(jnp.zeros((1, width - 4 * count), jnp.float32))
    line = jnp.concatenate(pieces, axis=1)
    send_ref[count:, :] = jnp.broadcast_to(line, (EXTRA, width)).astype(jnp.bfloat16)


def keep_kernel(unit_ref, side_ref, old_sums_ref, old_mixed_ref, *refs):
    blocks, (sums_ref, mixed_ref) = refs[:-2], refs[-2:]
    count = mixed_ref.shape[0]
    earlier, every, mixed = score(unit_ref[:count, :], side_ref[:count, :], blocks)
    sums_ref[...] = old_sums_ref[:count, :]
    sums_ref[:, 0:1] += earlier
    sums_ref[:, 1:2] += every
    mixed_ref[...] = old_mixed_ref[:count, :] + mixed


def combine_kernel(sums_ref, mixed_ref, got_ref, dup_ref, out_ref, dup_here, out_here, sems):
    count = mixed_ref.shape[0]
    step = count // PIECES
    line = got_ref[count:, :].astype(jnp.float32)[:1]
    parts = [line[:, at * count : (at + 1) * count] for at in range(4)]
    every = sums_ref[:, 1:2] + as_column(parts[2] + parts[3])
    root = jnp.sqrt(1.0 + every)
    copies = []
    for at in range(PIECES):
        here = pl.ds(at * step, step)
        mixed = mixed_ref[here, :] + got_ref[here, :].astype(jnp.float32)
        out_here[here, :] = mixed / root[at * step : (at + 1) * step]
        copies.append(pltpu.make_async_copy(out_here.at[here, :], out_ref.at[here, :], sems.at[at]))
        copies[-1].start()
    dup_here[...] = jnp.log1p(as_row(sums_ref[:, 0:1]) + parts[0] + parts[1])
    copies.append(pltpu.make_async_copy(dup_here, dup_ref, sems.at[PIECES]))
    copies[-1].start()
    for copy in copies:
        copy.wait()


def cost(queries, keys, width):
    return pl.CostEstimate(
        flops=400 * queries * keys * width,
        bytes_accessed=8 * queries * width + 2 * keys * width,
        transcendentals=100 * queries * keys,
    )


def local(embeddings, cluster_id, priority):
    count, width = embeddings.shape
    tiles = count // SUB * (width // LANE)
    shards = lax.axis_size("shard")
    lanes = lax.axis_size("owner")
    rounds = shards // 2
    queries = 2 * count
    bf16, f32 = jnp.bfloat16, jnp.float32
    params = pltpu.CompilerParams(vmem_limit_bytes=VMEM)

    def shape(*dims, dtype=f32):
        return jax.ShapeDtypeStruct(dims, dtype)

    ring = list(range(0, rounds, 2)) + list(range(1, rounds, 2))[::-1]

    def along(array, step):
        pairs = [
            (2 * ring[at] + side, 2 * ring[(at + step) % rounds] + side)
            for at in range(rounds)
            for side in range(2)
        ]
        return lax.ppermute(array, "shard", pairs)

    def across(array):
        return lax.ppermute(array, "shard", [(at, at ^ 1) for at in range(shards)])

    def two_ways(by_ring, step, by_side):
        pairs = []
        for at in range(rounds):
            for side in range(2):
                here, there = 2 * ring[at] + side, 2 * ring[(at + step) % rounds] + side
                pairs.append((here * lanes, there * lanes))
                pairs += [(here * lanes + lane, (here ^ 1) * lanes + lane) for lane in range(1, lanes)]
        source = jnp.where(lax.axis_index("owner") == 0, by_ring, by_side)
        return lax.ppermute(source, ("shard", "owner"), pairs)

    def swap(array):
        return lax.ppermute(array, "owner", [(at, lanes - 1 - at) for at in range(lanes)])

    def first(*blocks):
        return pl.pallas_call(
            first_kernel,
            out_shape=[
                shape(queries, width, dtype=bf16),
                shape(queries, 128),
                shape(queries, 128),
                shape(queries, width),
            ],
            cost_estimate=cost(queries, (len(blocks) - 1) * count, width),
            compiler_params=params,
            name="first_scores",
        )(*blocks)

    def more(unit, side, sums, mixed, *blocks):
        return pl.pallas_call(
            more_kernel,
            out_shape=[shape(queries, 128), shape(queries, width)],
            input_output_aliases={2: 0, 3: 1},
            cost_estimate=cost(queries, len(blocks) * count, width),
            compiler_params=params,
            name="more_scores",
        )(unit, side, sums, mixed, *blocks)

    def final(unit, side, sums, mixed, *blocks):
        send = pl.pallas_call(
            send_kernel,
            out_shape=shape(count + EXTRA, width, dtype=bf16),
            cost_estimate=cost(count, len(blocks) * count, width),
            compiler_params=params,
            name="send_scores",
        )(unit, side, sums, mixed, *blocks)
        keep_sums, keep = pl.pallas_call(
            keep_kernel,
            out_shape=[shape(count, 128), shape(count, width)],
            cost_estimate=cost(count, len(blocks) * count, width),
            compiler_params=params,
            name="keep_scores",
        )(unit, side, sums, mixed, *blocks)
        return keep_sums, keep, send

    pieces = embeddings.reshape(count // SUB, SUB, width // LANE, LANE).transpose(0, 2, 1, 3)
    base = pl.pallas_call(
        base_kernel,
        out_shape=shape(SUB, LANE),
        cost_estimate=pl.CostEstimate(flops=1000000000, bytes_accessed=0, transcendentals=0),
        compiler_params=params,
        name="base",
    )()
    own = pl.pallas_call(
        pack_kernel,
        out_shape=shape(tiles + 1, SUB, LANE, dtype=bf16),
        compiler_params=params,
        name="pack",
    )(pieces.reshape(tiles, SUB, LANE), cluster_id.reshape(1, count), priority.reshape(1, count), base)

    moved, beside = along(own, 1), across(own)
    other = swap(own)
    if rounds == 4:
        ahead = along(own, -1)
        moved, beside, other = lax.optimization_barrier((moved, beside, other))
        opposite = along(moved, 1)
        moved_beside = across(moved)
        ahead_beside = across(ahead)
        other, moved_beside, opposite = lax.optimization_barrier((other, moved_beside, opposite))
        last = [two_ways(moved_beside, 1, opposite)]
        unit, side, sums, mixed = first(own, other, beside, moved, moved_beside)
        sums, mixed = more(unit, side, sums, mixed, ahead, opposite, ahead_beside)
    else:
        unit, side, sums, mixed = first(own, other, beside)

        def turn(at, state):
            moved, sums, mixed = state
            ahead, beside = along(moved, 1), across(moved)
            sums, mixed = more(unit, side, sums, mixed, moved, beside)
            return ahead, sums, mixed

        moved, sums, mixed = lax.fori_loop(1, rounds - 1, turn, (moved, sums, mixed))
        last = [moved, across(moved)]
    keep_sums, keep, send = final(unit, side, sums, mixed, *last)
    dup, out = pl.pallas_call(
        combine_kernel,
        out_shape=[shape(1, count), shape(count, width)],
        out_specs=[pl.BlockSpec(memory_space=pl.ANY)] * 2,
        scratch_shapes=[
            pltpu.VMEM((1, count), f32),
            pltpu.VMEM((count, width), f32),
            pltpu.SemaphoreType.DMA((PIECES + 1,)),
        ],
        compiler_params=params,
        name="combine",
    )(keep_sums, keep, swap(send))
    return dup[0], out


def solution(mesh):
    placed = (
        P(("groups", "shard", "owner"), None),
        P(("groups", "shard", "owner"), None),
        P(("groups", "shard", "owner")),
    )
    return jax.shard_map(
        local,
        mesh=mesh,
        in_specs=placed,
        out_specs=(P(("groups", "shard", "owner")), P(("groups", "shard", "owner"), None)),
        check_vma=False,
    )
```

```python
import jax
import jax.numpy as jnp
from jax import lax
from jax.experimental import pallas as pl
from jax.experimental.pallas import tpu as pltpu
from jax.sharding import PartitionSpec as P

SUB, LANE = 8, 128
EXTRA = 8
VMEM = 24 * 1024 * 1024


def make_unit(rows):
    wide = rows.astype(jnp.float32)
    scale = lax.rsqrt(jnp.mean(wide * wide, axis=-1, keepdims=True) + 1e-06) / jnp.sqrt(
        jnp.float32(rows.shape[-1])
    )
    return (wide * scale).astype(jnp.bfloat16)


def diagonal(count):
    down = lax.broadcasted_iota(jnp.int32, (count, count), 0)
    return down == lax.broadcasted_iota(jnp.int32, (count, count), 1)


def as_row(column):
    return jnp.sum(jnp.where(diagonal(column.shape[0]), column, 0.0), axis=0, keepdims=True)


def as_column(row):
    return jnp.sum(jnp.where(diagonal(row.shape[1]), row, 0.0), axis=1, keepdims=True)


def halves(value):
    high = value.astype(jnp.bfloat16)
    return high, (value - high.astype(jnp.float32)).astype(jnp.bfloat16)


def base_kernel(base_ref):
    base_ref[...] = jnp.zeros_like(base_ref)


def pack_kernel(tiles_ref, label_ref, rank_ref, base_ref, packed_ref):
    many = tiles_ref.shape[0]
    packed_ref[:many] = tiles_ref[...]
    rank = rank_ref[...]
    high = lax.shift_right_logical(rank, 8)
    low = rank - lax.shift_left(high, 8)
    lines = [line.astype(jnp.float32) for line in (label_ref[...], high, low)]
    lines.append(base_ref[len(lines) :, :])
    packed_ref[many] = jnp.concatenate(lines, axis=0).astype(jnp.bfloat16)


def labels_and_ranks(block):
    tile = block[block.shape[0] - 1].astype(jnp.float32)
    return tile[0:1], tile[1:2] * 256.0 + tile[2:3]


def rows_of(blocks, width):
    across = width // LANE
    wide = []
    for block in blocks:
        tiles = block[: block.shape[0] - 1].astype(jnp.float32)
        tiles = tiles.reshape(-1, across, SUB, LANE)
        pieces = [tiles[:, at].reshape(-1, LANE) for at in range(across)]
        wide.append(jnp.concatenate(pieces, axis=1))
    return jnp.concatenate(wide, axis=0)


def score(unit, side, blocks):
    own_label, own_rank = side[:, 0:1], side[:, 1:2]
    wide = rows_of(blocks, unit.shape[1])
    keys = wide.astype(jnp.bfloat16)
    sides = [labels_and_ranks(block) for block in blocks]
    label = jnp.concatenate([item[0] for item in sides], axis=1)
    rank = jnp.concatenate([item[1] for item in sides], axis=1)
    cosine = lax.dot_general(
        unit, make_unit(wide), (((1,), (1,)), ((), ())), preferred_element_type=jnp.float32
    )
    weight = 1.0 / (1.0 + jnp.exp(-40.0 * (cosine - 0.05)))
    near = jnp.where((label == own_label) & (rank != own_rank), weight, 0.0)
    earlier = jnp.sum(jnp.where(rank < own_rank, near, 0.0), axis=1, keepdims=True)
    every = jnp.sum(near, axis=1, keepdims=True)
    mixed = jnp.dot(near.astype(jnp.bfloat16), keys, preferred_element_type=jnp.float32)
    return earlier, every, mixed


def first_kernel(own_ref, other_ref, *refs):
    blocks, (unit_ref, side_ref, sums_ref, mixed_ref) = refs[:-4], refs[-4:]
    count = own_ref.shape[0] // (unit_ref.shape[1] // LANE) * SUB
    side_ref[...] = jnp.zeros_like(side_ref)
    sums_ref[...] = jnp.zeros_like(sums_ref)
    unit_ref[...] = make_unit(rows_of([own_ref, other_ref], unit_ref.shape[1]))
    for at, ref in enumerate((own_ref, other_ref)):
        here = slice(at * count, (at + 1) * count)
        label, rank = labels_and_ranks(ref)
        side_ref[here, 0:1] = as_column(label)
        side_ref[here, 1:2] = as_column(rank)
    sums_ref[:, 0:1], sums_ref[:, 1:2], mixed_ref[...] = score(
        unit_ref[...], side_ref, (own_ref,) + blocks
    )


def more_kernel(unit_ref, side_ref, old_sums_ref, old_mixed_ref, *refs):
    blocks, (sums_ref, mixed_ref) = refs[:-2], refs[-2:]
    earlier, every, mixed = score(unit_ref[...], side_ref, blocks)
    sums_ref[...] = old_sums_ref[...]
    sums_ref[:, 0:1] += earlier
    sums_ref[:, 1:2] += every
    mixed_ref[...] = old_mixed_ref[...] + mixed


def send_kernel(unit_ref, side_ref, old_sums_ref, old_mixed_ref, *refs):
    blocks, send_ref = refs[:-1], refs[-1]
    count, width = send_ref.shape[0] - EXTRA, send_ref.shape[1]
    earlier, every, mixed = score(unit_ref[count:, :], side_ref[count:, :], blocks)
    earlier += old_sums_ref[count:, 0:1]
    every += old_sums_ref[count:, 1:2]
    send_ref[:count, :] = (mixed + old_mixed_ref[count:, :]).astype(jnp.bfloat16)
    pieces = halves(as_row(earlier)) + halves(as_row(every))
    pieces = [piece.astype(jnp.float32) for piece in pieces]
    pieces.append(jnp.zeros((1, width - 4 * count), jnp.float32))
    line = jnp.concatenate(pieces, axis=1)
    send_ref[count:, :] = jnp.broadcast_to(line, (EXTRA, width)).astype(jnp.bfloat16)


def keep_kernel(unit_ref, side_ref, old_sums_ref, old_mixed_ref, *refs):
    blocks, (sums_ref, mixed_ref) = refs[:-2], refs[-2:]
    count = mixed_ref.shape[0]
    earlier, every, mixed = score(unit_ref[:count, :], side_ref[:count, :], blocks)
    sums_ref[...] = old_sums_ref[:count, :]
    sums_ref[:, 0:1] += earlier
    sums_ref[:, 1:2] += every
    mixed_ref[...] = old_mixed_ref[:count, :] + mixed


def combine_kernel(sums_ref, mixed_ref, got_ref, dup_ref, out_ref):
    count = mixed_ref.shape[0]
    line = got_ref[count:, :].astype(jnp.float32)[:1]
    parts = [line[:, at * count : (at + 1) * count] for at in range(4)]
    every = sums_ref[:, 1:2] + as_column(parts[2] + parts[3])
    dup_ref[...] = jnp.log1p(as_row(sums_ref[:, 0:1]) + parts[0] + parts[1])
    mixed = mixed_ref[...] + got_ref[:count, :].astype(jnp.float32)
    out_ref[...] = mixed / jnp.sqrt(1.0 + every)


def cost(queries, keys, width):
    return pl.CostEstimate(
        flops=400 * queries * keys * width,
        bytes_accessed=8 * queries * width + 2 * keys * width,
        transcendentals=100 * queries * keys,
    )


def local(embeddings, cluster_id, priority):
    count, width = embeddings.shape
    tiles = count // SUB * (width // LANE)
    shards = lax.axis_size("shard")
    lanes = lax.axis_size("owner")
    rounds = shards // 2
    queries = 2 * count
    bf16, f32 = jnp.bfloat16, jnp.float32
    params = pltpu.CompilerParams(vmem_limit_bytes=VMEM)

    def shape(*dims, dtype=f32):
        return jax.ShapeDtypeStruct(dims, dtype)

    ring = list(range(0, rounds, 2)) + list(range(1, rounds, 2))[::-1]

    def along(array, step):
        pairs = [
            (2 * ring[at] + side, 2 * ring[(at + step) % rounds] + side)
            for at in range(rounds)
            for side in range(2)
        ]
        return lax.ppermute(array, "shard", pairs)

    def across(array):
        return lax.ppermute(array, "shard", [(at, at ^ 1) for at in range(shards)])

    def swap(array):
        return lax.ppermute(array, "owner", [(at, lanes - 1 - at) for at in range(lanes)])

    def first(*blocks):
        return pl.pallas_call(
            first_kernel,
            out_shape=[
                shape(queries, width, dtype=bf16),
                shape(queries, 128),
                shape(queries, 128),
                shape(queries, width),
            ],
            cost_estimate=cost(queries, (len(blocks) - 1) * count, width),
            compiler_params=params,
            name="first_scores",
        )(*blocks)

    def more(unit, side, sums, mixed, *blocks):
        return pl.pallas_call(
            more_kernel,
            out_shape=[shape(queries, 128), shape(queries, width)],
            input_output_aliases={2: 0, 3: 1},
            cost_estimate=cost(queries, len(blocks) * count, width),
            compiler_params=params,
            name="more_scores",
        )(unit, side, sums, mixed, *blocks)

    def final(unit, side, sums, mixed, *blocks):
        send = pl.pallas_call(
            send_kernel,
            out_shape=shape(count + EXTRA, width, dtype=bf16),
            cost_estimate=cost(count, len(blocks) * count, width),
            compiler_params=params,
            name="send_scores",
        )(unit, side, sums, mixed, *blocks)
        keep_sums, keep = pl.pallas_call(
            keep_kernel,
            out_shape=[shape(count, 128), shape(count, width)],
            cost_estimate=cost(count, len(blocks) * count, width),
            compiler_params=params,
            name="keep_scores",
        )(unit, side, sums, mixed, *blocks)
        return keep_sums, keep, send

    pieces = embeddings.reshape(count // SUB, SUB, width // LANE, LANE).transpose(0, 2, 1, 3)
    base = pl.pallas_call(
        base_kernel,
        out_shape=shape(SUB, LANE),
        cost_estimate=pl.CostEstimate(flops=1000000000, bytes_accessed=0, transcendentals=0),
        compiler_params=params,
        name="base",
    )()
    own = pl.pallas_call(
        pack_kernel,
        out_shape=shape(tiles + 1, SUB, LANE, dtype=bf16),
        compiler_params=params,
        name="pack",
    )(pieces.reshape(tiles, SUB, LANE), cluster_id.reshape(1, count), priority.reshape(1, count), base)

    moved, beside = along(own, 1), across(own)
    other = swap(own)
    if rounds == 4:
        ahead = along(own, -1)
        moved, beside, other = lax.optimization_barrier((moved, beside, other))
        opposite = along(moved, 1)
        moved_beside = across(moved)
        ahead_beside = across(ahead)
        last = [along(moved_beside, 1)]
        unit, side, sums, mixed = first(own, other, beside, moved, moved_beside)
        sums, mixed = more(unit, side, sums, mixed, ahead, opposite, ahead_beside)
    else:
        unit, side, sums, mixed = first(own, other, beside)

        def turn(at, state):
            moved, sums, mixed = state
            ahead, beside = along(moved, 1), across(moved)
            sums, mixed = more(unit, side, sums, mixed, moved, beside)
            return ahead, sums, mixed

        moved, sums, mixed = lax.fori_loop(1, rounds - 1, turn, (moved, sums, mixed))
        last = [moved, across(moved)]
    keep_sums, keep, send = final(unit, side, sums, mixed, *last)
    dup, out = pl.pallas_call(
        combine_kernel,
        out_shape=[shape(1, count), shape(count, width)],
        compiler_params=params,
        name="combine",
    )(keep_sums, keep, swap(send))
    return dup[0], out


def solution(mesh):
    placed = (
        P(("groups", "shard", "owner"), None),
        P(("groups", "shard", "owner"), None),
        P(("groups", "shard", "owner")),
    )
    return jax.shard_map(
        local,
        mesh=mesh,
        in_specs=placed,
        out_specs=(P(("groups", "shard", "owner")), P(("groups", "shard", "owner"), None)),
        check_vma=False,
    )
```

```python
import functools

import jax
import jax.numpy as jnp
from jax import lax
from jax.experimental import pallas as pl
from jax.experimental.pallas import tpu as pltpu
from jax.sharding import PartitionSpec as P

SUB, LANE = 8, 128
EXTRA = 8
VMEM = 24 * 1024 * 1024


def make_unit(rows):
    wide = rows.astype(jnp.float32)
    scale = lax.rsqrt(jnp.mean(wide * wide, axis=-1, keepdims=True) + 1e-06) / jnp.sqrt(
        jnp.float32(rows.shape[-1])
    )
    return (wide * scale).astype(jnp.bfloat16)


def diagonal(count):
    down = lax.broadcasted_iota(jnp.int32, (count, count), 0)
    return down == lax.broadcasted_iota(jnp.int32, (count, count), 1)


def as_row(column):
    return jnp.sum(jnp.where(diagonal(column.shape[0]), column, 0.0), axis=0, keepdims=True)


def as_column(row):
    return jnp.sum(jnp.where(diagonal(row.shape[1]), row, 0.0), axis=1, keepdims=True)


def halves(value):
    high = value.astype(jnp.bfloat16)
    return high, (value - high.astype(jnp.float32)).astype(jnp.bfloat16)


def base_kernel(base_ref):
    base_ref[...] = jnp.zeros_like(base_ref)


def pack_kernel(tiles_ref, label_ref, rank_ref, base_ref, packed_ref, tag_ref):
    many = tiles_ref.shape[0]
    packed_ref[:many] = tiles_ref[...]
    rank = rank_ref[...]
    high = lax.shift_right_logical(rank, 8)
    low = rank - lax.shift_left(high, 8)
    lines = [line.astype(jnp.float32) for line in (label_ref[...], high, low)]
    lines.append(base_ref[len(lines) :, :])
    tag = jnp.concatenate(lines, axis=0).astype(jnp.bfloat16)
    packed_ref[many] = tag
    tag_ref[...] = tag


def labels_and_ranks(block, tag=None):
    tile = block[block.shape[0] - 1] if tag is None else tag
    tile = tile.astype(jnp.float32)
    return tile[0:1], tile[1:2] * 256.0 + tile[2:3]


def rows_of(blocks, width):
    across = width // LANE
    wide = []
    for block in blocks:
        tiles = block[: block.shape[0] // across * across].astype(jnp.float32)
        tiles = tiles.reshape(-1, across, SUB, LANE)
        pieces = [tiles[:, at].reshape(-1, LANE) for at in range(across)]
        wide.append(jnp.concatenate(pieces, axis=1))
    return jnp.concatenate(wide, axis=0)


def split(marks, refs):
    blocks, arrays = refs[: len(marks)], refs[len(marks) :]
    tags = [None if m is None else arrays[m[0]][m[1] * SUB : (m[1] + 1) * SUB, :] for m in marks]
    return blocks, tags


def score(unit, side, blocks, tags):
    own_label, own_rank = side[:, 0:1], side[:, 1:2]
    wide = rows_of(blocks, unit.shape[1])
    keys = wide.astype(jnp.bfloat16)
    sides = [labels_and_ranks(block, tag) for block, tag in zip(blocks, tags)]
    label = jnp.concatenate([item[0] for item in sides], axis=1)
    rank = jnp.concatenate([item[1] for item in sides], axis=1)
    cosine = lax.dot_general(
        unit, make_unit(wide), (((1,), (1,)), ((), ())), preferred_element_type=jnp.float32
    )
    weight = 1.0 / (1.0 + jnp.exp(-40.0 * (cosine - 0.05)))
    near = jnp.where((label == own_label) & (rank != own_rank), weight, 0.0)
    earlier = jnp.sum(jnp.where(rank < own_rank, near, 0.0), axis=1, keepdims=True)
    every = jnp.sum(near, axis=1, keepdims=True)
    mixed = jnp.dot(near.astype(jnp.bfloat16), keys, preferred_element_type=jnp.float32)
    return earlier, every, mixed


def first_kernel(marks, own_ref, other_ref, *refs):
    unit_ref, side_ref, sums_ref, mixed_ref = refs[-4:]
    blocks, tags = split(marks, refs[:-4])
    count = own_ref.shape[0] // (unit_ref.shape[1] // LANE) * SUB
    side_ref[...] = jnp.zeros_like(side_ref)
    sums_ref[...] = jnp.zeros_like(sums_ref)
    unit_ref[...] = make_unit(rows_of([own_ref, other_ref], unit_ref.shape[1]))
    for at, ref in enumerate((own_ref, other_ref)):
        here = slice(at * count, (at + 1) * count)
        label, rank = labels_and_ranks(ref)
        side_ref[here, 0:1] = as_column(label)
        side_ref[here, 1:2] = as_column(rank)
    sums_ref[:, 0:1], sums_ref[:, 1:2], mixed_ref[...] = score(
        unit_ref[...], side_ref, (own_ref,) + blocks, [None] + tags
    )


def more_kernel(marks, unit_ref, side_ref, old_sums_ref, old_mixed_ref, *refs):
    sums_ref, mixed_ref = refs[-2:]
    blocks, tags = split(marks, refs[:-2])
    earlier, every, mixed = score(unit_ref[...], side_ref, blocks, tags)
    sums_ref[...] = old_sums_ref[...]
    sums_ref[:, 0:1] += earlier
    sums_ref[:, 1:2] += every
    mixed_ref[...] = old_mixed_ref[...] + mixed


def send_kernel(marks, unit_ref, side_ref, old_sums_ref, old_mixed_ref, *refs):
    send_ref = refs[-1]
    blocks, tags = split(marks, refs[:-1])
    count, width = send_ref.shape[0] - EXTRA, send_ref.shape[1]
    earlier, every, mixed = score(unit_ref[count:, :], side_ref[count:, :], blocks, tags)
    earlier += old_sums_ref[count:, 0:1]
    every += old_sums_ref[count:, 1:2]
    send_ref[:count, :] = (mixed + old_mixed_ref[count:, :]).astype(jnp.bfloat16)
    pieces = halves(as_row(earlier)) + halves(as_row(every))
    pieces = [piece.astype(jnp.float32) for piece in pieces]
    pieces.append(jnp.zeros((1, width - 4 * count), jnp.float32))
    line = jnp.concatenate(pieces, axis=1)
    send_ref[count:, :] = jnp.broadcast_to(line, (EXTRA, width)).astype(jnp.bfloat16)


def keep_kernel(marks, unit_ref, side_ref, old_sums_ref, old_mixed_ref, *refs):
    sums_ref, mixed_ref = refs[-2:]
    blocks, tags = split(marks, refs[:-2])
    count = mixed_ref.shape[0]
    earlier, every, mixed = score(unit_ref[:count, :], side_ref[:count, :], blocks, tags)
    sums_ref[...] = old_sums_ref[:count, :]
    sums_ref[:, 0:1] += earlier
    sums_ref[:, 1:2] += every
    mixed_ref[...] = old_mixed_ref[:count, :] + mixed


def combine_kernel(sums_ref, mixed_ref, got_ref, dup_ref, out_ref):
    count = mixed_ref.shape[0]
    line = got_ref[count:, :].astype(jnp.float32)[:1]
    parts = [line[:, at * count : (at + 1) * count] for at in range(4)]
    every = sums_ref[:, 1:2] + as_column(parts[2] + parts[3])
    dup_ref[...] = jnp.log1p(as_row(sums_ref[:, 0:1]) + parts[0] + parts[1])
    mixed = mixed_ref[...] + got_ref[:count, :].astype(jnp.float32)
    out_ref[...] = mixed / jnp.sqrt(1.0 + every)


def cost(queries, keys, width):
    return pl.CostEstimate(
        flops=4 * queries * keys * width,
        bytes_accessed=8 * queries * width + 2 * keys * width,
        transcendentals=queries * keys,
    )


def local(embeddings, cluster_id, priority):
    count, width = embeddings.shape
    tiles = count // SUB * (width // LANE)
    shards = lax.axis_size("shard")
    lanes = lax.axis_size("owner")
    rounds = shards // 2
    queries = 2 * count
    bf16, f32 = jnp.bfloat16, jnp.float32
    params = pltpu.CompilerParams(vmem_limit_bytes=VMEM)

    def shape(*dims, dtype=f32):
        return jax.ShapeDtypeStruct(dims, dtype)

    ring = list(range(0, rounds, 2)) + list(range(1, rounds, 2))[::-1]

    def along(array, step):
        pairs = [
            (2 * ring[at] + side, 2 * ring[(at + step) % rounds] + side)
            for at in range(rounds)
            for side in range(2)
        ]
        return lax.ppermute(array, "shard", pairs)

    def across(array):
        return lax.ppermute(array, "shard", [(at, at ^ 1) for at in range(shards)])

    def swap(array):
        return lax.ppermute(array, "owner", [(at, lanes - 1 - at) for at in range(lanes)])

    def first(marks, own, other, *refs):
        return pl.pallas_call(
            functools.partial(first_kernel, marks),
            out_shape=[
                shape(queries, width, dtype=bf16),
                shape(queries, 128),
                shape(queries, 128),
                shape(queries, width),
            ],
            cost_estimate=cost(queries, (len(marks) + 1) * count, width),
            compiler_params=params,
            name="first_scores",
        )(own, other, *refs)

    def more(marks, unit, side, sums, mixed, *refs):
        return pl.pallas_call(
            functools.partial(more_kernel, marks),
            out_shape=[shape(queries, 128), shape(queries, width)],
            input_output_aliases={2: 0, 3: 1},
            cost_estimate=cost(queries, len(marks) * count, width),
            compiler_params=params,
            name="more_scores",
        )(unit, side, sums, mixed, *refs)

    def final(marks, unit, side, sums, mixed, *refs):
        send = pl.pallas_call(
            functools.partial(send_kernel, marks),
            out_shape=shape(count + EXTRA, width, dtype=bf16),
            cost_estimate=cost(count, len(marks) * count, width),
            compiler_params=params,
            name="send_scores",
        )(unit, side, sums, mixed, *refs)
        keep_sums, keep = pl.pallas_call(
            functools.partial(keep_kernel, marks),
            out_shape=[shape(count, 128), shape(count, width)],
            cost_estimate=cost(count, len(marks) * count, width),
            compiler_params=params,
            name="keep_scores",
        )(unit, side, sums, mixed, *refs)
        return keep_sums, keep, send

    pieces = embeddings.reshape(count // SUB, SUB, width // LANE, LANE).transpose(0, 2, 1, 3)
    pieces = pieces.reshape(tiles, SUB, LANE)
    base = pl.pallas_call(
        base_kernel,
        out_shape=shape(SUB, LANE),
        cost_estimate=pl.CostEstimate(flops=1000000000, bytes_accessed=0, transcendentals=0),
        compiler_params=params,
        name="base",
    )()
    own, own_tag = pl.pallas_call(
        pack_kernel,
        out_shape=[shape(tiles + 1, SUB, LANE, dtype=bf16), shape(SUB, LANE, dtype=bf16)],
        compiler_params=params,
        name="pack",
    )(pieces, cluster_id.reshape(1, count), priority.reshape(1, count), base)

    other, beside = swap(own), across(own)
    if rounds == 4:
        moved = along(pieces, 1)
        ahead = along(own, -1)
        other, own_tag = lax.optimization_barrier((other, own_tag))
        ahead, beside = lax.optimization_barrier((ahead, beside))
        opposite = along(moved, 1)
        moved_beside = across(moved)
        ahead_beside = across(ahead)
        column = jnp.concatenate([along(own_tag, 1), along(own_tag, 2)], axis=0)
        tags = (column, across(column))
        last = along(moved_beside, 1)
        marks = (None, (0, 0), (1, 0))
        state = first(marks, own, other, beside, moved, moved_beside, *tags)
        marks = (None, (0, 1), None)
        sums, mixed = more(marks, *state, ahead, opposite, ahead_beside, *tags)
        outcome = final(((1, 1),), *state[:2], sums, mixed, last, *tags)
    else:
        moved = along(own, 1)
        unit, side, sums, mixed = first((None,), own, other, beside)
        marks = (None, None)

        def turn(at, state):
            moved, sums, mixed = state
            ahead, beside = along(moved, 1), across(moved)
            sums, mixed = more(marks, unit, side, sums, mixed, moved, beside)
            return ahead, sums, mixed

        moved, sums, mixed = lax.fori_loop(1, rounds - 1, turn, (moved, sums, mixed))
        outcome = final(marks, unit, side, sums, mixed, moved, across(moved))
    keep_sums, keep, send = outcome
    dup, out = pl.pallas_call(
        combine_kernel,
        out_shape=[shape(1, count), shape(count, width)],
        compiler_params=params,
        name="combine",
    )(keep_sums, keep, swap(send))
    return dup[0], out


def solution(mesh):
    placed = (
        P(("groups", "shard", "owner"), None),
        P(("groups", "shard", "owner"), None),
        P(("groups", "shard", "owner")),
    )
    return jax.shard_map(
        local,
        mesh=mesh,
        in_specs=placed,
        out_specs=(P(("groups", "shard", "owner")), P(("groups", "shard", "owner"), None)),
        check_vma=False,
    )
```

```python
import jax
import jax.numpy as jnp
from jax import lax
from jax.experimental import pallas as pl
from jax.experimental.pallas import tpu as pltpu
from jax.sharding import PartitionSpec as P

SUB, LANE = 8, 128
EXTRA = 8
VMEM = 24 * 1024 * 1024


def make_unit(rows):
    wide = rows.astype(jnp.float32)
    scale = lax.rsqrt(jnp.mean(wide * wide, axis=-1, keepdims=True) + 1e-06) / jnp.sqrt(
        jnp.float32(rows.shape[-1])
    )
    return (wide * scale).astype(jnp.bfloat16)


def diagonal(count):
    down = lax.broadcasted_iota(jnp.int32, (count, count), 0)
    return down == lax.broadcasted_iota(jnp.int32, (count, count), 1)


def as_row(column):
    return jnp.sum(jnp.where(diagonal(column.shape[0]), column, 0.0), axis=0, keepdims=True)


def as_column(row):
    return jnp.sum(jnp.where(diagonal(row.shape[1]), row, 0.0), axis=1, keepdims=True)


def halves(value):
    high = value.astype(jnp.bfloat16)
    return high, (value - high.astype(jnp.float32)).astype(jnp.bfloat16)


def base_kernel(base_ref):
    base_ref[...] = jnp.zeros_like(base_ref)


def pack_kernel(tiles_ref, label_ref, rank_ref, base_ref, packed_ref):
    many = tiles_ref.shape[0]
    packed_ref[:many] = tiles_ref[...]
    rank = rank_ref[...]
    high = lax.shift_right_logical(rank, 8)
    low = rank - lax.shift_left(high, 8)
    lines = [line.astype(jnp.float32) for line in (label_ref[...], high, low)]
    lines.append(base_ref[len(lines) :, :])
    packed_ref[many] = jnp.concatenate(lines, axis=0).astype(jnp.bfloat16)


def labels_and_ranks(block):
    tile = block[block.shape[0] - 1].astype(jnp.float32)
    return tile[0:1], tile[1:2] * 256.0 + tile[2:3]


def rows_of(blocks, width):
    across = width // LANE
    wide = []
    for block in blocks:
        tiles = block[: block.shape[0] - 1].astype(jnp.float32)
        tiles = tiles.reshape(-1, across, SUB, LANE)
        pieces = [tiles[:, at].reshape(-1, LANE) for at in range(across)]
        wide.append(jnp.concatenate(pieces, axis=1))
    return jnp.concatenate(wide, axis=0)


def score(unit, side, blocks):
    own_label, own_rank = side[:, 0:1], side[:, 1:2]
    wide = rows_of(blocks, unit.shape[1])
    keys = wide.astype(jnp.bfloat16)
    sides = [labels_and_ranks(block) for block in blocks]
    label = jnp.concatenate([item[0] for item in sides], axis=1)
    rank = jnp.concatenate([item[1] for item in sides], axis=1)
    cosine = lax.dot_general(
        unit, make_unit(wide), (((1,), (1,)), ((), ())), preferred_element_type=jnp.float32
    )
    weight = 1.0 / (1.0 + jnp.exp(-40.0 * (cosine - 0.05)))
    near = jnp.where((label == own_label) & (rank != own_rank), weight, 0.0)
    earlier = jnp.sum(jnp.where(rank < own_rank, near, 0.0), axis=1, keepdims=True)
    every = jnp.sum(near, axis=1, keepdims=True)
    mixed = jnp.dot(near.astype(jnp.bfloat16), keys, preferred_element_type=jnp.float32)
    return earlier, every, mixed


def first_kernel(own_ref, other_ref, *refs):
    blocks, (unit_ref, side_ref, sums_ref, mixed_ref) = refs[:-4], refs[-4:]
    count = own_ref.shape[0] // (unit_ref.shape[1] // LANE) * SUB
    side_ref[...] = jnp.zeros_like(side_ref)
    sums_ref[...] = jnp.zeros_like(sums_ref)
    unit_ref[...] = make_unit(rows_of([own_ref, other_ref], unit_ref.shape[1]))
    for at, ref in enumerate((own_ref, other_ref)):
        here = slice(at * count, (at + 1) * count)
        label, rank = labels_and_ranks(ref)
        side_ref[here, 0:1] = as_column(label)
        side_ref[here, 1:2] = as_column(rank)
    sums_ref[:, 0:1], sums_ref[:, 1:2], mixed_ref[...] = score(
        unit_ref[...], side_ref, (own_ref,) + blocks
    )


def more_kernel(unit_ref, side_ref, old_sums_ref, old_mixed_ref, *refs):
    blocks, (sums_ref, mixed_ref) = refs[:-2], refs[-2:]
    earlier, every, mixed = score(unit_ref[...], side_ref, blocks)
    sums_ref[...] = old_sums_ref[...]
    sums_ref[:, 0:1] += earlier
    sums_ref[:, 1:2] += every
    mixed_ref[...] = old_mixed_ref[...] + mixed


def send_kernel(unit_ref, side_ref, old_sums_ref, old_mixed_ref, *refs):
    blocks, send_ref = refs[:-1], refs[-1]
    count, width = send_ref.shape[0] - EXTRA, send_ref.shape[1]
    earlier, every, mixed = score(unit_ref[count:, :], side_ref[count:, :], blocks)
    earlier += old_sums_ref[count:, 0:1]
    every += old_sums_ref[count:, 1:2]
    send_ref[:count, :] = (mixed + old_mixed_ref[count:, :]).astype(jnp.bfloat16)
    pieces = halves(as_row(earlier)) + halves(as_row(every))
    pieces = [piece.astype(jnp.float32) for piece in pieces]
    pieces.append(jnp.zeros((1, width - 4 * count), jnp.float32))
    line = jnp.concatenate(pieces, axis=1)
    send_ref[count:, :] = jnp.broadcast_to(line, (EXTRA, width)).astype(jnp.bfloat16)


def keep_kernel(unit_ref, side_ref, old_sums_ref, old_mixed_ref, *refs):
    blocks, (sums_ref, mixed_ref) = refs[:-2], refs[-2:]
    count = mixed_ref.shape[0]
    earlier, every, mixed = score(unit_ref[:count, :], side_ref[:count, :], blocks)
    sums_ref[...] = old_sums_ref[:count, :]
    sums_ref[:, 0:1] += earlier
    sums_ref[:, 1:2] += every
    mixed_ref[...] = old_mixed_ref[:count, :] + mixed


def combine_kernel(sums_ref, mixed_ref, got_ref, dup_ref, out_ref):
    count = mixed_ref.shape[0]
    line = got_ref[count:, :].astype(jnp.float32)[:1]
    parts = [line[:, at * count : (at + 1) * count] for at in range(4)]
    every = sums_ref[:, 1:2] + as_column(parts[2] + parts[3])
    dup_ref[...] = jnp.log1p(as_row(sums_ref[:, 0:1]) + parts[0] + parts[1])
    mixed = mixed_ref[...] + got_ref[:count, :].astype(jnp.float32)
    out_ref[...] = mixed / jnp.sqrt(1.0 + every)


def cost(queries, keys, width):
    return pl.CostEstimate(
        flops=400 * queries * keys * width,
        bytes_accessed=8 * queries * width + 2 * keys * width,
        transcendentals=100 * queries * keys,
    )


def local(embeddings, cluster_id, priority):
    count, width = embeddings.shape
    tiles = count // SUB * (width // LANE)
    shards = lax.axis_size("shard")
    lanes = lax.axis_size("owner")
    rounds = shards // 2
    queries = 2 * count
    bf16, f32 = jnp.bfloat16, jnp.float32
    params = pltpu.CompilerParams(vmem_limit_bytes=VMEM)

    def shape(*dims, dtype=f32):
        return jax.ShapeDtypeStruct(dims, dtype)

    ring = list(range(0, rounds, 2)) + list(range(1, rounds, 2))[::-1]

    def along(array, step):
        pairs = [
            (2 * ring[at] + side, 2 * ring[(at + step) % rounds] + side)
            for at in range(rounds)
            for side in range(2)
        ]
        return lax.ppermute(array, "shard", pairs)

    def across(array):
        return lax.ppermute(array, "shard", [(at, at ^ 1) for at in range(shards)])

    def swap(array):
        return lax.ppermute(array, "owner", [(at, lanes - 1 - at) for at in range(lanes)])

    def first(*blocks):
        return pl.pallas_call(
            first_kernel,
            out_shape=[
                shape(queries, width, dtype=bf16),
                shape(queries, 128),
                shape(queries, 128),
                shape(queries, width),
            ],
            cost_estimate=cost(queries, (len(blocks) - 1) * count, width),
            compiler_params=params,
            name="first_scores",
        )(*blocks)

    def more(unit, side, sums, mixed, *blocks):
        return pl.pallas_call(
            more_kernel,
            out_shape=[shape(queries, 128), shape(queries, width)],
            input_output_aliases={2: 0, 3: 1},
            cost_estimate=cost(queries, len(blocks) * count, width),
            compiler_params=params,
            name="more_scores",
        )(unit, side, sums, mixed, *blocks)

    def final(unit, side, sums, mixed, *blocks):
        send = pl.pallas_call(
            send_kernel,
            out_shape=shape(count + EXTRA, width, dtype=bf16),
            cost_estimate=cost(count, len(blocks) * count, width),
            compiler_params=params,
            name="send_scores",
        )(unit, side, sums, mixed, *blocks)
        keep_sums, keep = pl.pallas_call(
            keep_kernel,
            out_shape=[shape(count, 128), shape(count, width)],
            cost_estimate=cost(count, len(blocks) * count, width),
            compiler_params=params,
            name="keep_scores",
        )(unit, side, sums, mixed, *blocks)
        return keep_sums, keep, send

    pieces = embeddings.reshape(count // SUB, SUB, width // LANE, LANE).transpose(0, 2, 1, 3)
    base = pl.pallas_call(
        base_kernel,
        out_shape=shape(SUB, LANE),
        cost_estimate=pl.CostEstimate(flops=1000000000, bytes_accessed=0, transcendentals=0),
        compiler_params=params,
        name="base",
    )()
    own = pl.pallas_call(
        pack_kernel,
        out_shape=shape(tiles + 1, SUB, LANE, dtype=bf16),
        compiler_params=params,
        name="pack",
    )(pieces.reshape(tiles, SUB, LANE), cluster_id.reshape(1, count), priority.reshape(1, count), base)

    moved, beside = along(own, 1), across(own)
    other = swap(own)
    if rounds == 4:
        ahead = along(own, -1)
        moved, beside, other = lax.optimization_barrier((moved, beside, other))
        opposite = along(moved, 1)
        moved_beside = across(moved)
        moved_beside, ahead = lax.optimization_barrier((moved_beside, ahead))
        last_ = along(moved_beside, 1)
        ahead_beside = across(ahead)
        last = [last_, ahead_beside]
        unit, side, sums, mixed = first(own, other, beside, moved, moved_beside)
        sums, mixed = more(unit, side, sums, mixed, ahead, opposite)
    else:
        unit, side, sums, mixed = first(own, other, beside)

        def turn(at, state):
            moved, sums, mixed = state
            ahead, beside = along(moved, 1), across(moved)
            sums, mixed = more(unit, side, sums, mixed, moved, beside)
            return ahead, sums, mixed

        moved, sums, mixed = lax.fori_loop(1, rounds - 1, turn, (moved, sums, mixed))
        last = [moved, across(moved)]
    keep_sums, keep, send = final(unit, side, sums, mixed, *last)
    dup, out = pl.pallas_call(
        combine_kernel,
        out_shape=[shape(1, count), shape(count, width)],
        compiler_params=params,
        name="combine",
    )(keep_sums, keep, swap(send))
    return dup[0], out


def solution(mesh):
    placed = (
        P(("groups", "shard", "owner"), None),
        P(("groups", "shard", "owner"), None),
        P(("groups", "shard", "owner")),
    )
    return jax.shard_map(
        local,
        mesh=mesh,
        in_specs=placed,
        out_specs=(P(("groups", "shard", "owner")), P(("groups", "shard", "owner"), None)),
        check_vma=False,
    )
```

```python
import jax
import jax.numpy as jnp
from jax import lax
from jax.experimental import pallas as pl
from jax.experimental.pallas import tpu as pltpu
from jax.sharding import PartitionSpec as P

SUB, LANE = 8, 128
EXTRA = 8
VMEM = 24 * 1024 * 1024


def make_unit(rows):
    wide = rows.astype(jnp.float32)
    scale = lax.rsqrt(jnp.mean(wide * wide, axis=-1, keepdims=True) + 1e-06) / jnp.sqrt(
        jnp.float32(rows.shape[-1])
    )
    return (wide * scale).astype(jnp.bfloat16)


def diagonal(count):
    down = lax.broadcasted_iota(jnp.int32, (count, count), 0)
    return down == lax.broadcasted_iota(jnp.int32, (count, count), 1)


def as_row(column):
    return jnp.sum(jnp.where(diagonal(column.shape[0]), column, 0.0), axis=0, keepdims=True)


def as_column(row):
    return jnp.sum(jnp.where(diagonal(row.shape[1]), row, 0.0), axis=1, keepdims=True)


def halves(value):
    high = value.astype(jnp.bfloat16)
    return high, (value - high.astype(jnp.float32)).astype(jnp.bfloat16)


def base_kernel(base_ref):
    base_ref[...] = jnp.zeros_like(base_ref)


def pack_kernel(tiles_ref, label_ref, rank_ref, base_ref, packed_ref):
    many = tiles_ref.shape[0]
    packed_ref[:many] = tiles_ref[...]
    rank = rank_ref[...]
    high = lax.shift_right_logical(rank, 8)
    low = rank - lax.shift_left(high, 8)
    lines = [line.astype(jnp.float32) for line in (label_ref[...], high, low)]
    lines.append(base_ref[len(lines) :, :])
    packed_ref[many] = jnp.concatenate(lines, axis=0).astype(jnp.bfloat16)


def labels_and_ranks(block):
    tile = block[block.shape[0] - 1].astype(jnp.float32)
    return tile[0:1], tile[1:2] * 256.0 + tile[2:3]


def rows_of(blocks, width):
    across = width // LANE
    wide = []
    for block in blocks:
        tiles = block[: block.shape[0] - 1].astype(jnp.float32)
        tiles = tiles.reshape(-1, across, SUB, LANE)
        pieces = [tiles[:, at].reshape(-1, LANE) for at in range(across)]
        wide.append(jnp.concatenate(pieces, axis=1))
    return jnp.concatenate(wide, axis=0)


def score(unit, side, blocks):
    own_label, own_rank = side[:, 0:1], side[:, 1:2]
    wide = rows_of(blocks, unit.shape[1])
    keys = wide.astype(jnp.bfloat16)
    sides = [labels_and_ranks(block) for block in blocks]
    label = jnp.concatenate([item[0] for item in sides], axis=1)
    rank = jnp.concatenate([item[1] for item in sides], axis=1)
    cosine = lax.dot_general(
        unit, make_unit(wide), (((1,), (1,)), ((), ())), preferred_element_type=jnp.float32
    )
    weight = 1.0 / (1.0 + jnp.exp(-40.0 * (cosine - 0.05)))
    near = jnp.where((label == own_label) & (rank != own_rank), weight, 0.0)
    earlier = jnp.sum(jnp.where(rank < own_rank, near, 0.0), axis=1, keepdims=True)
    every = jnp.sum(near, axis=1, keepdims=True)
    mixed = jnp.dot(near.astype(jnp.bfloat16), keys, preferred_element_type=jnp.float32)
    return earlier, every, mixed


def first_kernel(own_ref, other_ref, *refs):
    blocks, (unit_ref, side_ref, sums_ref, mixed_ref) = refs[:-4], refs[-4:]
    count = own_ref.shape[0] // (unit_ref.shape[1] // LANE) * SUB
    side_ref[...] = jnp.zeros_like(side_ref)
    sums_ref[...] = jnp.zeros_like(sums_ref)
    unit_ref[...] = make_unit(rows_of([own_ref, other_ref], unit_ref.shape[1]))
    for at, ref in enumerate((own_ref, other_ref)):
        here = slice(at * count, (at + 1) * count)
        label, rank = labels_and_ranks(ref)
        side_ref[here, 0:1] = as_column(label)
        side_ref[here, 1:2] = as_column(rank)
    sums_ref[:, 0:1], sums_ref[:, 1:2], mixed_ref[...] = score(
        unit_ref[...], side_ref, (own_ref,) + blocks
    )


def more_kernel(unit_ref, side_ref, old_sums_ref, old_mixed_ref, *refs):
    blocks, (sums_ref, mixed_ref) = refs[:-2], refs[-2:]
    earlier, every, mixed = score(unit_ref[...], side_ref, blocks)
    sums_ref[...] = old_sums_ref[...]
    sums_ref[:, 0:1] += earlier
    sums_ref[:, 1:2] += every
    mixed_ref[...] = old_mixed_ref[...] + mixed


def send_kernel(unit_ref, side_ref, old_sums_ref, old_mixed_ref, *refs):
    blocks, send_ref = refs[:-1], refs[-1]
    count, width = send_ref.shape[0] - EXTRA, send_ref.shape[1]
    earlier, every, mixed = score(unit_ref[count:, :], side_ref[count:, :], blocks)
    earlier += old_sums_ref[count:, 0:1]
    every += old_sums_ref[count:, 1:2]
    send_ref[:count, :] = (mixed + old_mixed_ref[count:, :]).astype(jnp.bfloat16)
    pieces = halves(as_row(earlier)) + halves(as_row(every))
    pieces = [piece.astype(jnp.float32) for piece in pieces]
    pieces.append(jnp.zeros((1, width - 4 * count), jnp.float32))
    line = jnp.concatenate(pieces, axis=1)
    send_ref[count:, :] = jnp.broadcast_to(line, (EXTRA, width)).astype(jnp.bfloat16)


def keep_kernel(unit_ref, side_ref, old_sums_ref, old_mixed_ref, *refs):
    blocks, (sums_ref, mixed_ref) = refs[:-2], refs[-2:]
    count = mixed_ref.shape[0]
    earlier, every, mixed = score(unit_ref[:count, :], side_ref[:count, :], blocks)
    sums_ref[...] = old_sums_ref[:count, :]
    sums_ref[:, 0:1] += earlier
    sums_ref[:, 1:2] += every
    mixed_ref[...] = old_mixed_ref[:count, :] + mixed


def combine_kernel(sums_ref, mixed_ref, got_ref, dup_ref, out_ref):
    count = mixed_ref.shape[0]
    line = got_ref[count:, :].astype(jnp.float32)[:1]
    parts = [line[:, at * count : (at + 1) * count] for at in range(4)]
    every = sums_ref[:, 1:2] + as_column(parts[2] + parts[3])
    dup_ref[...] = jnp.log1p(as_row(sums_ref[:, 0:1]) + parts[0] + parts[1])
    mixed = mixed_ref[...] + got_ref[:count, :].astype(jnp.float32)
    out_ref[...] = mixed / jnp.sqrt(1.0 + every)


def cost(queries, keys, width):
    return pl.CostEstimate(
        flops=400 * queries * keys * width,
        bytes_accessed=8 * queries * width + 2 * keys * width,
        transcendentals=100 * queries * keys,
    )


def local(embeddings, cluster_id, priority):
    count, width = embeddings.shape
    tiles = count // SUB * (width // LANE)
    shards = lax.axis_size("shard")
    lanes = lax.axis_size("owner")
    rounds = shards // 2
    queries = 2 * count
    bf16, f32 = jnp.bfloat16, jnp.float32
    params = pltpu.CompilerParams(vmem_limit_bytes=VMEM)

    def shape(*dims, dtype=f32):
        return jax.ShapeDtypeStruct(dims, dtype)

    ring = list(range(0, rounds, 2)) + list(range(1, rounds, 2))[::-1]

    def along(array, step):
        pairs = [
            (2 * ring[at] + side, 2 * ring[(at + step) % rounds] + side)
            for at in range(rounds)
            for side in range(2)
        ]
        return lax.ppermute(array, "shard", pairs)

    def across(array):
        return lax.ppermute(array, "shard", [(at, at ^ 1) for at in range(shards)])

    def two_ways(array, ring_lane):
        pairs = []
        for at in range(rounds):
            for side in range(2):
                here, there = 2 * ring[at] + side, 2 * ring[(at + 1) % rounds] + side
                pairs += [
                    (here * lanes + lane, (there if lane == ring_lane else here ^ 1) * lanes + lane)
                    for lane in range(lanes)
                ]
        return lax.ppermute(array, ("shard", "owner"), pairs)

    def swap(array):
        return lax.ppermute(array, "owner", [(at, lanes - 1 - at) for at in range(lanes)])

    def first(*blocks):
        return pl.pallas_call(
            first_kernel,
            out_shape=[
                shape(queries, width, dtype=bf16),
                shape(queries, 128),
                shape(queries, 128),
                shape(queries, width),
            ],
            cost_estimate=cost(queries, (len(blocks) - 1) * count, width),
            compiler_params=params,
            name="first_scores",
        )(*blocks)

    def more(unit, side, sums, mixed, *blocks):
        return pl.pallas_call(
            more_kernel,
            out_shape=[shape(queries, 128), shape(queries, width)],
            input_output_aliases={2: 0, 3: 1},
            cost_estimate=cost(queries, len(blocks) * count, width),
            compiler_params=params,
            name="more_scores",
        )(unit, side, sums, mixed, *blocks)

    def final(unit, side, sums, mixed, *blocks):
        send = pl.pallas_call(
            send_kernel,
            out_shape=shape(count + EXTRA, width, dtype=bf16),
            cost_estimate=cost(count, len(blocks) * count, width),
            compiler_params=params,
            name="send_scores",
        )(unit, side, sums, mixed, *blocks)
        keep_sums, keep = pl.pallas_call(
            keep_kernel,
            out_shape=[shape(count, 128), shape(count, width)],
            cost_estimate=cost(count, len(blocks) * count, width),
            compiler_params=params,
            name="keep_scores",
        )(unit, side, sums, mixed, *blocks)
        return keep_sums, keep, send

    pieces = embeddings.reshape(count // SUB, SUB, width // LANE, LANE).transpose(0, 2, 1, 3)
    base = pl.pallas_call(
        base_kernel,
        out_shape=shape(SUB, LANE),
        cost_estimate=pl.CostEstimate(flops=1000000000, bytes_accessed=0, transcendentals=0),
        compiler_params=params,
        name="base",
    )()
    own = pl.pallas_call(
        pack_kernel,
        out_shape=shape(tiles + 1, SUB, LANE, dtype=bf16),
        compiler_params=params,
        name="pack",
    )(pieces.reshape(tiles, SUB, LANE), cluster_id.reshape(1, count), priority.reshape(1, count), base)

    moved, beside = along(own, 1), across(own)
    other = swap(own)
    if rounds == 4:
        ahead = along(own, -1)
        moved, beside, other = lax.optimization_barrier((moved, beside, other))
        sooner, later = two_ways(moved, 1), two_ways(moved, 0)
        ahead_beside = across(ahead)
        last = [two_ways(sooner, 0)]
        unit, side, sums, mixed = first(own, other, beside, moved, sooner)
        sums, mixed = more(unit, side, sums, mixed, ahead, later, ahead_beside)
    else:
        unit, side, sums, mixed = first(own, other, beside)

        def turn(at, state):
            moved, sums, mixed = state
            ahead, beside = along(moved, 1), across(moved)
            sums, mixed = more(unit, side, sums, mixed, moved, beside)
            return ahead, sums, mixed

        moved, sums, mixed = lax.fori_loop(1, rounds - 1, turn, (moved, sums, mixed))
        last = [moved, across(moved)]
    keep_sums, keep, send = final(unit, side, sums, mixed, *last)
    dup, out = pl.pallas_call(
        combine_kernel,
        out_shape=[shape(1, count), shape(count, width)],
        compiler_params=params,
        name="combine",
    )(keep_sums, keep, swap(send))
    return dup[0], out


def solution(mesh):
    placed = (
        P(("groups", "shard", "owner"), None),
        P(("groups", "shard", "owner"), None),
        P(("groups", "shard", "owner")),
    )
    return jax.shard_map(
        local,
        mesh=mesh,
        in_specs=placed,
        out_specs=(P(("groups", "shard", "owner")), P(("groups", "shard", "owner"), None)),
        check_vma=False,
    )
```

```python
import jax
import jax.numpy as jnp
from jax import lax
from jax.experimental import pallas as pl
from jax.experimental.pallas import tpu as pltpu
from jax.sharding import PartitionSpec as P

SUB, LANE = 8, 128
EXTRA = 8
VMEM = 24 * 1024 * 1024


def make_unit(rows):
    wide = rows.astype(jnp.float32)
    scale = lax.rsqrt(jnp.mean(wide * wide, axis=-1, keepdims=True) + 1e-06) / jnp.sqrt(
        jnp.float32(rows.shape[-1])
    )
    return (wide * scale).astype(jnp.bfloat16)


def diagonal(count):
    down = lax.broadcasted_iota(jnp.int32, (count, count), 0)
    return down == lax.broadcasted_iota(jnp.int32, (count, count), 1)


def as_row(column):
    return jnp.sum(jnp.where(diagonal(column.shape[0]), column, 0.0), axis=0, keepdims=True)


def as_column(row):
    return jnp.sum(jnp.where(diagonal(row.shape[1]), row, 0.0), axis=1, keepdims=True)


def halves(value):
    high = value.astype(jnp.bfloat16)
    return high, (value - high.astype(jnp.float32)).astype(jnp.bfloat16)


def base_kernel(base_ref):
    base_ref[...] = jnp.zeros_like(base_ref)


def pack_kernel(tiles_ref, label_ref, rank_ref, base_ref, packed_ref):
    many = tiles_ref.shape[0]
    packed_ref[:many] = tiles_ref[...]
    rank = rank_ref[...]
    high = lax.shift_right_logical(rank, 8)
    low = rank - lax.shift_left(high, 8)
    lines = [line.astype(jnp.float32) for line in (label_ref[...], high, low)]
    lines.append(base_ref[len(lines) :, :])
    packed_ref[many] = jnp.concatenate(lines, axis=0).astype(jnp.bfloat16)


def labels_and_ranks(block):
    tile = block[block.shape[0] - 1].astype(jnp.float32)
    return tile[0:1], tile[1:2] * 256.0 + tile[2:3]


def rows_of(blocks, width):
    across = width // LANE
    wide = []
    for block in blocks:
        tiles = block[: block.shape[0] - 1].astype(jnp.float32)
        tiles = tiles.reshape(-1, across, SUB, LANE)
        pieces = [tiles[:, at].reshape(-1, LANE) for at in range(across)]
        wide.append(jnp.concatenate(pieces, axis=1))
    return jnp.concatenate(wide, axis=0)


def score(unit, side, blocks):
    own_label, own_rank = side[:, 0:1], side[:, 1:2]
    wide = rows_of(blocks, unit.shape[1])
    keys = wide.astype(jnp.bfloat16)
    sides = [labels_and_ranks(block) for block in blocks]
    label = jnp.concatenate([item[0] for item in sides], axis=1)
    rank = jnp.concatenate([item[1] for item in sides], axis=1)
    cosine = lax.dot_general(
        unit, make_unit(wide), (((1,), (1,)), ((), ())), preferred_element_type=jnp.float32
    )
    weight = 1.0 / (1.0 + jnp.exp(-40.0 * (cosine - 0.05)))
    near = jnp.where((label == own_label) & (rank != own_rank), weight, 0.0)
    earlier = jnp.sum(jnp.where(rank < own_rank, near, 0.0), axis=1, keepdims=True)
    every = jnp.sum(near, axis=1, keepdims=True)
    mixed = jnp.dot(near.astype(jnp.bfloat16), keys, preferred_element_type=jnp.float32)
    return earlier, every, mixed


def first_kernel(own_ref, other_ref, *refs):
    blocks, (unit_ref, side_ref, sums_ref, mixed_ref) = refs[:-4], refs[-4:]
    count = own_ref.shape[0] // (unit_ref.shape[1] // LANE) * SUB
    side_ref[...] = jnp.zeros_like(side_ref)
    sums_ref[...] = jnp.zeros_like(sums_ref)
    unit_ref[...] = make_unit(rows_of([own_ref, other_ref], unit_ref.shape[1]))
    for at, ref in enumerate((own_ref, other_ref)):
        here = slice(at * count, (at + 1) * count)
        label, rank = labels_and_ranks(ref)
        side_ref[here, 0:1] = as_column(label)
        side_ref[here, 1:2] = as_column(rank)
    sums_ref[:, 0:1], sums_ref[:, 1:2], mixed_ref[...] = score(
        unit_ref[...], side_ref, (own_ref,) + blocks
    )


def more_kernel(unit_ref, side_ref, old_sums_ref, old_mixed_ref, *refs):
    blocks, (sums_ref, mixed_ref) = refs[:-2], refs[-2:]
    earlier, every, mixed = score(unit_ref[...], side_ref, blocks)
    sums_ref[...] = old_sums_ref[...]
    sums_ref[:, 0:1] += earlier
    sums_ref[:, 1:2] += every
    mixed_ref[...] = old_mixed_ref[...] + mixed


def send_kernel(unit_ref, side_ref, old_sums_ref, old_mixed_ref, *refs):
    blocks, send_ref = refs[:-1], refs[-1]
    count, width = send_ref.shape[0] - EXTRA, send_ref.shape[1]
    earlier, every, mixed = score(unit_ref[count:, :], side_ref[count:, :], blocks)
    earlier += old_sums_ref[count:, 0:1]
    every += old_sums_ref[count:, 1:2]
    send_ref[:count, :] = (mixed + old_mixed_ref[count:, :]).astype(jnp.bfloat16)
    pieces = halves(as_row(earlier)) + halves(as_row(every))
    pieces = [piece.astype(jnp.float32) for piece in pieces]
    pieces.append(jnp.zeros((1, width - 4 * count), jnp.float32))
    line = jnp.concatenate(pieces, axis=1)
    send_ref[count:, :] = jnp.broadcast_to(line, (EXTRA, width)).astype(jnp.bfloat16)


def keep_kernel(unit_ref, side_ref, old_sums_ref, old_mixed_ref, *refs):
    blocks, (sums_ref, mixed_ref) = refs[:-2], refs[-2:]
    count = mixed_ref.shape[0]
    earlier, every, mixed = score(unit_ref[:count, :], side_ref[:count, :], blocks)
    sums_ref[...] = old_sums_ref[:count, :]
    sums_ref[:, 0:1] += earlier
    sums_ref[:, 1:2] += every
    mixed_ref[...] = old_mixed_ref[:count, :] + mixed


def combine_kernel(sums_ref, mixed_ref, got_ref, dup_ref, out_ref):
    count = mixed_ref.shape[0]
    line = got_ref[count:, :].astype(jnp.float32)[:1]
    parts = [line[:, at * count : (at + 1) * count] for at in range(4)]
    every = sums_ref[:, 1:2] + as_column(parts[2] + parts[3])
    dup_ref[...] = jnp.log1p(as_row(sums_ref[:, 0:1]) + parts[0] + parts[1])
    mixed = mixed_ref[...] + got_ref[:count, :].astype(jnp.float32)
    out_ref[...] = mixed / jnp.sqrt(1.0 + every)


def cost(queries, keys, width):
    return pl.CostEstimate(
        flops=400 * queries * keys * width,
        bytes_accessed=8 * queries * width + 2 * keys * width,
        transcendentals=100 * queries * keys,
    )


def local(embeddings, cluster_id, priority):
    count, width = embeddings.shape
    tiles = count // SUB * (width // LANE)
    shards = lax.axis_size("shard")
    lanes = lax.axis_size("owner")
    rounds = shards // 2
    queries = 2 * count
    bf16, f32 = jnp.bfloat16, jnp.float32
    params = pltpu.CompilerParams(vmem_limit_bytes=VMEM)

    def shape(*dims, dtype=f32):
        return jax.ShapeDtypeStruct(dims, dtype)

    ring = list(range(0, rounds, 2)) + list(range(1, rounds, 2))[::-1]

    def along(array, step):
        pairs = [
            (2 * ring[at] + side, 2 * ring[(at + step) % rounds] + side)
            for at in range(rounds)
            for side in range(2)
        ]
        return lax.ppermute(array, "shard", pairs)

    def across(array):
        return lax.ppermute(array, "shard", [(at, at ^ 1) for at in range(shards)])

    def two_ways(array, ring_lane):
        pairs = []
        for at in range(rounds):
            for side in range(2):
                here, there = 2 * ring[at] + side, 2 * ring[(at + 1) % rounds] + side
                pairs += [
                    (here * lanes + lane, (there if lane == ring_lane else here ^ 1) * lanes + lane)
                    for lane in range(lanes)
                ]
        return lax.ppermute(array, ("shard", "owner"), pairs)

    def swap(array):
        return lax.ppermute(array, "owner", [(at, lanes - 1 - at) for at in range(lanes)])

    def first(*blocks):
        return pl.pallas_call(
            first_kernel,
            out_shape=[
                shape(queries, width, dtype=bf16),
                shape(queries, 128),
                shape(queries, 128),
                shape(queries, width),
            ],
            cost_estimate=cost(queries, (len(blocks) - 1) * count, width),
            compiler_params=params,
            name="first_scores",
        )(*blocks)

    def more(unit, side, sums, mixed, *blocks):
        return pl.pallas_call(
            more_kernel,
            out_shape=[shape(queries, 128), shape(queries, width)],
            input_output_aliases={2: 0, 3: 1},
            cost_estimate=cost(queries, len(blocks) * count, width),
            compiler_params=params,
            name="more_scores",
        )(unit, side, sums, mixed, *blocks)

    def final(unit, side, sums, mixed, *blocks):
        send = pl.pallas_call(
            send_kernel,
            out_shape=shape(count + EXTRA, width, dtype=bf16),
            cost_estimate=cost(count, len(blocks) * count, width),
            compiler_params=params,
            name="send_scores",
        )(unit, side, sums, mixed, *blocks)
        keep_sums, keep = pl.pallas_call(
            keep_kernel,
            out_shape=[shape(count, 128), shape(count, width)],
            cost_estimate=cost(count, len(blocks) * count, width),
            compiler_params=params,
            name="keep_scores",
        )(unit, side, sums, mixed, *blocks)
        return keep_sums, keep, send

    pieces = embeddings.reshape(count // SUB, SUB, width // LANE, LANE).transpose(0, 2, 1, 3)
    base = pl.pallas_call(
        base_kernel,
        out_shape=shape(SUB, LANE),
        cost_estimate=pl.CostEstimate(flops=1000000000, bytes_accessed=0, transcendentals=0),
        compiler_params=params,
        name="base",
    )()
    own = pl.pallas_call(
        pack_kernel,
        out_shape=shape(tiles + 1, SUB, LANE, dtype=bf16),
        compiler_params=params,
        name="pack",
    )(pieces.reshape(tiles, SUB, LANE), cluster_id.reshape(1, count), priority.reshape(1, count), base)

    moved, beside = along(own, 1), across(own)
    other = swap(own)
    if rounds == 4:
        ahead = along(own, -1)
        moved, beside, other = lax.optimization_barrier((moved, beside, other))
        sooner, later = two_ways(moved, 1), two_ways(moved, 0)
        ahead_beside = across(ahead)
        last = [two_ways(sooner, 0), ahead_beside]
        unit, side, sums, mixed = first(own, other, beside, moved, sooner)
        sums, mixed = more(unit, side, sums, mixed, ahead, later)
    else:
        unit, side, sums, mixed = first(own, other, beside)

        def turn(at, state):
            moved, sums, mixed = state
            ahead, beside = along(moved, 1), across(moved)
            sums, mixed = more(unit, side, sums, mixed, moved, beside)
            return ahead, sums, mixed

        moved, sums, mixed = lax.fori_loop(1, rounds - 1, turn, (moved, sums, mixed))
        last = [moved, across(moved)]
    keep_sums, keep, send = final(unit, side, sums, mixed, *last)
    dup, out = pl.pallas_call(
        combine_kernel,
        out_shape=[shape(1, count), shape(count, width)],
        compiler_params=params,
        name="combine",
    )(keep_sums, keep, swap(send))
    return dup[0], out


def solution(mesh):
    placed = (
        P(("groups", "shard", "owner"), None),
        P(("groups", "shard", "owner"), None),
        P(("groups", "shard", "owner")),
    )
    return jax.shard_map(
        local,
        mesh=mesh,
        in_specs=placed,
        out_specs=(P(("groups", "shard", "owner")), P(("groups", "shard", "owner"), None)),
        check_vma=False,
    )
```

```python
import jax
import jax.numpy as jnp
from jax import lax
from jax.experimental import pallas as pl
from jax.experimental.pallas import tpu as pltpu
from jax.sharding import PartitionSpec as P

SUB, LANE = 8, 128
EXTRA = 8
VMEM = 24 * 1024 * 1024


def make_unit(rows):
    wide = rows.astype(jnp.float32)
    scale = lax.rsqrt(jnp.mean(wide * wide, axis=-1, keepdims=True) + 1e-06) / jnp.sqrt(
        jnp.float32(rows.shape[-1])
    )
    return (wide * scale).astype(jnp.bfloat16)


def diagonal(count):
    down = lax.broadcasted_iota(jnp.int32, (count, count), 0)
    return down == lax.broadcasted_iota(jnp.int32, (count, count), 1)


def as_row(column):
    return jnp.sum(jnp.where(diagonal(column.shape[0]), column, 0.0), axis=0, keepdims=True)


def as_column(row):
    return jnp.sum(jnp.where(diagonal(row.shape[1]), row, 0.0), axis=1, keepdims=True)


def halves(value):
    high = value.astype(jnp.bfloat16)
    return high, (value - high.astype(jnp.float32)).astype(jnp.bfloat16)


def base_kernel(base_ref):
    base_ref[...] = jnp.zeros_like(base_ref)


def pack_kernel(tiles_ref, label_ref, rank_ref, base_ref, packed_ref):
    many = tiles_ref.shape[0]
    packed_ref[:many] = tiles_ref[...]
    rank = rank_ref[...]
    high = lax.shift_right_logical(rank, 8)
    low = rank - lax.shift_left(high, 8)
    lines = [line.astype(jnp.float32) for line in (label_ref[...], high, low)]
    lines.append(base_ref[len(lines) :, :])
    packed_ref[many] = jnp.concatenate(lines, axis=0).astype(jnp.bfloat16)


def labels_and_ranks(block):
    tile = block[block.shape[0] - 1].astype(jnp.float32)
    return tile[0:1], tile[1:2] * 256.0 + tile[2:3]


def rows_of(blocks, width):
    across = width // LANE
    wide = []
    for block in blocks:
        tiles = block[: block.shape[0] - 1].astype(jnp.float32)
        tiles = tiles.reshape(-1, across, SUB, LANE)
        pieces = [tiles[:, at].reshape(-1, LANE) for at in range(across)]
        wide.append(jnp.concatenate(pieces, axis=1))
    return jnp.concatenate(wide, axis=0)


def score(unit, side, blocks):
    own_label, own_rank = side[:, 0:1], side[:, 1:2]
    wide = rows_of(blocks, unit.shape[1])
    keys = wide.astype(jnp.bfloat16)
    sides = [labels_and_ranks(block) for block in blocks]
    label = jnp.concatenate([item[0] for item in sides], axis=1)
    rank = jnp.concatenate([item[1] for item in sides], axis=1)
    cosine = lax.dot_general(
        unit, make_unit(wide), (((1,), (1,)), ((), ())), preferred_element_type=jnp.float32
    )
    weight = 1.0 / (1.0 + jnp.exp(-40.0 * (cosine - 0.05)))
    near = jnp.where((label == own_label) & (rank != own_rank), weight, 0.0)
    earlier = jnp.sum(jnp.where(rank < own_rank, near, 0.0), axis=1, keepdims=True)
    every = jnp.sum(near, axis=1, keepdims=True)
    mixed = jnp.dot(near.astype(jnp.bfloat16), keys, preferred_element_type=jnp.float32)
    return earlier, every, mixed


def first_kernel(own_ref, other_ref, *refs):
    blocks, (unit_ref, side_ref, sums_ref, mixed_ref) = refs[:-4], refs[-4:]
    count = own_ref.shape[0] // (unit_ref.shape[1] // LANE) * SUB
    side_ref[...] = jnp.zeros_like(side_ref)
    sums_ref[...] = jnp.zeros_like(sums_ref)
    unit_ref[...] = make_unit(rows_of([own_ref, other_ref], unit_ref.shape[1]))
    for at, ref in enumerate((own_ref, other_ref)):
        here = slice(at * count, (at + 1) * count)
        label, rank = labels_and_ranks(ref)
        side_ref[here, 0:1] = as_column(label)
        side_ref[here, 1:2] = as_column(rank)
    sums_ref[:, 0:1], sums_ref[:, 1:2], mixed_ref[...] = score(
        unit_ref[...], side_ref, (own_ref,) + blocks
    )


def more_kernel(unit_ref, side_ref, old_sums_ref, old_mixed_ref, *refs):
    blocks, (sums_ref, mixed_ref) = refs[:-2], refs[-2:]
    earlier, every, mixed = score(unit_ref[...], side_ref, blocks)
    sums_ref[...] = old_sums_ref[...]
    sums_ref[:, 0:1] += earlier
    sums_ref[:, 1:2] += every
    mixed_ref[...] = old_mixed_ref[...] + mixed


def send_kernel(unit_ref, side_ref, old_sums_ref, old_mixed_ref, *refs):
    blocks, send_ref = refs[:-1], refs[-1]
    count, width = send_ref.shape[0] - EXTRA, send_ref.shape[1]
    earlier, every, mixed = score(unit_ref[count:, :], side_ref[count:, :], blocks)
    earlier += old_sums_ref[count:, 0:1]
    every += old_sums_ref[count:, 1:2]
    send_ref[:count, :] = (mixed + old_mixed_ref[count:, :]).astype(jnp.bfloat16)
    pieces = halves(as_row(earlier)) + halves(as_row(every))
    pieces = [piece.astype(jnp.float32) for piece in pieces]
    pieces.append(jnp.zeros((1, width - 4 * count), jnp.float32))
    line = jnp.concatenate(pieces, axis=1)
    send_ref[count:, :] = jnp.broadcast_to(line, (EXTRA, width)).astype(jnp.bfloat16)


def keep_kernel(unit_ref, side_ref, old_sums_ref, old_mixed_ref, *refs):
    blocks, (sums_ref, mixed_ref) = refs[:-2], refs[-2:]
    count = mixed_ref.shape[0]
    earlier, every, mixed = score(unit_ref[:count, :], side_ref[:count, :], blocks)
    sums_ref[...] = old_sums_ref[:count, :]
    sums_ref[:, 0:1] += earlier
    sums_ref[:, 1:2] += every
    mixed_ref[...] = old_mixed_ref[:count, :] + mixed


def combine_kernel(sums_ref, mixed_ref, got_ref, dup_ref, out_ref):
    count = mixed_ref.shape[0]
    line = got_ref[count:, :].astype(jnp.float32)[:1]
    parts = [line[:, at * count : (at + 1) * count] for at in range(4)]
    every = sums_ref[:, 1:2] + as_column(parts[2] + parts[3])
    dup_ref[...] = jnp.log1p(as_row(sums_ref[:, 0:1]) + parts[0] + parts[1])
    mixed = mixed_ref[...] + got_ref[:count, :].astype(jnp.float32)
    out_ref[...] = mixed / jnp.sqrt(1.0 + every)


def cost(queries, keys, width):
    return pl.CostEstimate(
        flops=400 * queries * keys * width,
        bytes_accessed=8 * queries * width + 2 * keys * width,
        transcendentals=100 * queries * keys,
    )


def local(embeddings, cluster_id, priority):
    count, width = embeddings.shape
    tiles = count // SUB * (width // LANE)
    shards = lax.axis_size("shard")
    lanes = lax.axis_size("owner")
    rounds = shards // 2
    queries = 2 * count
    bf16, f32 = jnp.bfloat16, jnp.float32
    params = pltpu.CompilerParams(vmem_limit_bytes=VMEM)

    def shape(*dims, dtype=f32):
        return jax.ShapeDtypeStruct(dims, dtype)

    ring = [0] + list(range(1, rounds, 2)) + list(range(2, rounds, 2))[::-1]

    def along(array, step):
        pairs = [
            (2 * ring[at] + side, 2 * ring[(at + step) % rounds] + side)
            for at in range(rounds)
            for side in range(2)
        ]
        return lax.ppermute(array, "shard", pairs)

    def across(array):
        return lax.ppermute(array, "shard", [(at, at ^ 1) for at in range(shards)])

    def swap(array):
        return lax.ppermute(array, "owner", [(at, lanes - 1 - at) for at in range(lanes)])

    def first(*blocks):
        return pl.pallas_call(
            first_kernel,
            out_shape=[
                shape(queries, width, dtype=bf16),
                shape(queries, 128),
                shape(queries, 128),
                shape(queries, width),
            ],
            cost_estimate=cost(queries, (len(blocks) - 1) * count, width),
            compiler_params=params,
            name="first_scores",
        )(*blocks)

    def more(unit, side, sums, mixed, *blocks):
        return pl.pallas_call(
            more_kernel,
            out_shape=[shape(queries, 128), shape(queries, width)],
            input_output_aliases={2: 0, 3: 1},
            cost_estimate=cost(queries, len(blocks) * count, width),
            compiler_params=params,
            name="more_scores",
        )(unit, side, sums, mixed, *blocks)

    def final(unit, side, sums, mixed, *blocks):
        send = pl.pallas_call(
            send_kernel,
            out_shape=shape(count + EXTRA, width, dtype=bf16),
            cost_estimate=cost(count, len(blocks) * count, width),
            compiler_params=params,
            name="send_scores",
        )(unit, side, sums, mixed, *blocks)
        keep_sums, keep = pl.pallas_call(
            keep_kernel,
            out_shape=[shape(count, 128), shape(count, width)],
            cost_estimate=cost(count, len(blocks) * count, width),
            compiler_params=params,
            name="keep_scores",
        )(unit, side, sums, mixed, *blocks)
        return keep_sums, keep, send

    pieces = embeddings.reshape(count // SUB, SUB, width // LANE, LANE).transpose(0, 2, 1, 3)
    base = pl.pallas_call(
        base_kernel,
        out_shape=shape(SUB, LANE),
        cost_estimate=pl.CostEstimate(flops=1000000000, bytes_accessed=0, transcendentals=0),
        compiler_params=params,
        name="base",
    )()
    own = pl.pallas_call(
        pack_kernel,
        out_shape=shape(tiles + 1, SUB, LANE, dtype=bf16),
        compiler_params=params,
        name="pack",
    )(pieces.reshape(tiles, SUB, LANE), cluster_id.reshape(1, count), priority.reshape(1, count), base)

    moved, beside = along(own, 1), across(own)
    other = swap(own)
    if rounds == 4:
        ahead = along(own, -1)
        moved, beside, other = lax.optimization_barrier((moved, beside, other))
        opposite = along(moved, 1)
        moved_beside = across(moved)
        ahead_beside = across(ahead)
        last = [along(moved_beside, 1)]
        unit, side, sums, mixed = first(own, other, beside, moved, moved_beside)
        sums, mixed = more(unit, side, sums, mixed, ahead, opposite, ahead_beside)
    else:
        unit, side, sums, mixed = first(own, other, beside)

        def turn(at, state):
            moved, sums, mixed = state
            ahead, beside = along(moved, 1), across(moved)
            sums, mixed = more(unit, side, sums, mixed, moved, beside)
            return ahead, sums, mixed

        moved, sums, mixed = lax.fori_loop(1, rounds - 1, turn, (moved, sums, mixed))
        last = [moved, across(moved)]
    keep_sums, keep, send = final(unit, side, sums, mixed, *last)
    dup, out = pl.pallas_call(
        combine_kernel,
        out_shape=[shape(1, count), shape(count, width)],
        compiler_params=params,
        name="combine",
    )(keep_sums, keep, swap(send))
    return dup[0], out


def solution(mesh):
    placed = (
        P(("groups", "shard", "owner"), None),
        P(("groups", "shard", "owner"), None),
        P(("groups", "shard", "owner")),
    )
    return jax.shard_map(
        local,
        mesh=mesh,
        in_specs=placed,
        out_specs=(P(("groups", "shard", "owner")), P(("groups", "shard", "owner"), None)),
        check_vma=False,
    )
```

```python
import jax
import jax.numpy as jnp
from jax import lax
from jax.experimental import pallas as pl
from jax.experimental.pallas import tpu as pltpu
from jax.sharding import PartitionSpec as P

SUB, LANE = 8, 128
EXTRA = 8
VMEM = 24 * 1024 * 1024


def make_unit(rows):
    wide = rows.astype(jnp.float32)
    scale = lax.rsqrt(jnp.mean(wide * wide, axis=-1, keepdims=True) + 1e-06) / jnp.sqrt(
        jnp.float32(rows.shape[-1])
    )
    return (wide * scale).astype(jnp.bfloat16)


def diagonal(count):
    down = lax.broadcasted_iota(jnp.int32, (count, count), 0)
    return down == lax.broadcasted_iota(jnp.int32, (count, count), 1)


def as_row(column):
    return jnp.sum(jnp.where(diagonal(column.shape[0]), column, 0.0), axis=0, keepdims=True)


def as_column(row):
    return jnp.sum(jnp.where(diagonal(row.shape[1]), row, 0.0), axis=1, keepdims=True)


def halves(value):
    high = value.astype(jnp.bfloat16)
    return high, (value - high.astype(jnp.float32)).astype(jnp.bfloat16)


def base_kernel(base_ref):
    base_ref[...] = jnp.zeros_like(base_ref)


def pack_kernel(tiles_ref, label_ref, rank_ref, base_ref, packed_ref):
    many = tiles_ref.shape[0]
    packed_ref[:many] = tiles_ref[...]
    rank = rank_ref[...]
    high = lax.shift_right_logical(rank, 8)
    low = rank - lax.shift_left(high, 8)
    lines = [line.astype(jnp.float32) for line in (label_ref[...], high, low)]
    lines.append(base_ref[len(lines) :, :])
    packed_ref[many] = jnp.concatenate(lines, axis=0).astype(jnp.bfloat16)


def labels_and_ranks(block):
    tile = block[block.shape[0] - 1].astype(jnp.float32)
    return tile[0:1], tile[1:2] * 256.0 + tile[2:3]


def rows_of(blocks, width):
    across = width // LANE
    wide = []
    for block in blocks:
        tiles = block[: block.shape[0] - 1].astype(jnp.float32)
        tiles = tiles.reshape(-1, across, SUB, LANE)
        pieces = [tiles[:, at].reshape(-1, LANE) for at in range(across)]
        wide.append(jnp.concatenate(pieces, axis=1))
    return jnp.concatenate(wide, axis=0)


def score(unit, side, blocks):
    own_label, own_rank = side[:, 0:1], side[:, 1:2]
    wide = rows_of(blocks, unit.shape[1])
    keys = wide.astype(jnp.bfloat16)
    sides = [labels_and_ranks(block) for block in blocks]
    label = jnp.concatenate([item[0] for item in sides], axis=1)
    rank = jnp.concatenate([item[1] for item in sides], axis=1)
    cosine = lax.dot_general(
        unit, make_unit(wide), (((1,), (1,)), ((), ())), preferred_element_type=jnp.float32
    )
    weight = 1.0 / (1.0 + jnp.exp(-40.0 * (cosine - 0.05)))
    near = jnp.where((label == own_label) & (rank != own_rank), weight, 0.0)
    earlier = jnp.sum(jnp.where(rank < own_rank, near, 0.0), axis=1, keepdims=True)
    every = jnp.sum(near, axis=1, keepdims=True)
    mixed = jnp.dot(near.astype(jnp.bfloat16), keys, preferred_element_type=jnp.float32)
    return earlier, every, mixed


def first_kernel(own_ref, other_ref, *refs):
    blocks, (unit_ref, side_ref, sums_ref, mixed_ref) = refs[:-4], refs[-4:]
    count = own_ref.shape[0] // (unit_ref.shape[1] // LANE) * SUB
    side_ref[...] = jnp.zeros_like(side_ref)
    sums_ref[...] = jnp.zeros_like(sums_ref)
    unit_ref[...] = make_unit(rows_of([own_ref, other_ref], unit_ref.shape[1]))
    for at, ref in enumerate((own_ref, other_ref)):
        here = slice(at * count, (at + 1) * count)
        label, rank = labels_and_ranks(ref)
        side_ref[here, 0:1] = as_column(label)
        side_ref[here, 1:2] = as_column(rank)
    sums_ref[:, 0:1], sums_ref[:, 1:2], mixed_ref[...] = score(
        unit_ref[...], side_ref, (own_ref,) + blocks
    )


def more_kernel(unit_ref, side_ref, old_sums_ref, old_mixed_ref, *refs):
    blocks, (sums_ref, mixed_ref) = refs[:-2], refs[-2:]
    earlier, every, mixed = score(unit_ref[...], side_ref, blocks)
    sums_ref[...] = old_sums_ref[...]
    sums_ref[:, 0:1] += earlier
    sums_ref[:, 1:2] += every
    mixed_ref[...] = old_mixed_ref[...] + mixed


def send_kernel(unit_ref, side_ref, old_sums_ref, old_mixed_ref, *refs):
    blocks, (front_ref, rear_ref) = refs[:-2], refs[-2:]
    half, width = front_ref.shape
    count = 2 * half
    earlier, every, mixed = score(unit_ref[count:, :], side_ref[count:, :], blocks)
    earlier += old_sums_ref[count:, 0:1]
    every += old_sums_ref[count:, 1:2]
    mixed = (mixed + old_mixed_ref[count:, :]).astype(jnp.bfloat16)
    front_ref[...] = mixed[:half]
    rear_ref[:half, :] = mixed[half:]
    pieces = halves(as_row(earlier)) + halves(as_row(every))
    pieces = [piece.astype(jnp.float32) for piece in pieces]
    pieces.append(jnp.zeros((1, width - 4 * count), jnp.float32))
    line = jnp.concatenate(pieces, axis=1)
    rear_ref[half:, :] = jnp.broadcast_to(line, (EXTRA, width)).astype(jnp.bfloat16)


def keep_kernel(unit_ref, side_ref, old_sums_ref, old_mixed_ref, *refs):
    blocks, (sums_ref, mixed_ref) = refs[:-2], refs[-2:]
    count = mixed_ref.shape[0]
    earlier, every, mixed = score(unit_ref[:count, :], side_ref[:count, :], blocks)
    sums_ref[...] = old_sums_ref[:count, :]
    sums_ref[:, 0:1] += earlier
    sums_ref[:, 1:2] += every
    mixed_ref[...] = old_mixed_ref[:count, :] + mixed


def combine_kernel(sums_ref, mixed_ref, front_ref, rear_ref, dup_ref, out_ref):
    count = mixed_ref.shape[0]
    half = count // 2
    line = rear_ref[half:, :].astype(jnp.float32)[:1]
    parts = [line[:, at * count : (at + 1) * count] for at in range(4)]
    every = sums_ref[:, 1:2] + as_column(parts[2] + parts[3])
    dup_ref[...] = jnp.log1p(as_row(sums_ref[:, 0:1]) + parts[0] + parts[1])
    root = jnp.sqrt(1.0 + every)
    out_ref[:half, :] = (mixed_ref[:half, :] + front_ref[...].astype(jnp.float32)) / root[:half]
    rear = rear_ref[:half, :].astype(jnp.float32)
    out_ref[half:, :] = (mixed_ref[half:, :] + rear) / root[half:]


def cost(queries, keys, width):
    return pl.CostEstimate(
        flops=400 * queries * keys * width,
        bytes_accessed=8 * queries * width + 2 * keys * width,
        transcendentals=100 * queries * keys,
    )


def local(embeddings, cluster_id, priority):
    count, width = embeddings.shape
    tiles = count // SUB * (width // LANE)
    shards = lax.axis_size("shard")
    lanes = lax.axis_size("owner")
    rounds = shards // 2
    queries = 2 * count
    bf16, f32 = jnp.bfloat16, jnp.float32
    params = pltpu.CompilerParams(vmem_limit_bytes=VMEM)

    def shape(*dims, dtype=f32):
        return jax.ShapeDtypeStruct(dims, dtype)

    ring = list(range(0, rounds, 2)) + list(range(1, rounds, 2))[::-1]

    def along(array, step):
        pairs = [
            (2 * ring[at] + side, 2 * ring[(at + step) % rounds] + side)
            for at in range(rounds)
            for side in range(2)
        ]
        return lax.ppermute(array, "shard", pairs)

    def across(array):
        return lax.ppermute(array, "shard", [(at, at ^ 1) for at in range(shards)])

    def swap(array):
        return lax.ppermute(array, "owner", [(at, lanes - 1 - at) for at in range(lanes)])

    def first(*blocks):
        return pl.pallas_call(
            first_kernel,
            out_shape=[
                shape(queries, width, dtype=bf16),
                shape(queries, 128),
                shape(queries, 128),
                shape(queries, width),
            ],
            cost_estimate=cost(queries, (len(blocks) - 1) * count, width),
            compiler_params=params,
            name="first_scores",
        )(*blocks)

    def more(unit, side, sums, mixed, *blocks):
        return pl.pallas_call(
            more_kernel,
            out_shape=[shape(queries, 128), shape(queries, width)],
            input_output_aliases={2: 0, 3: 1},
            cost_estimate=cost(queries, len(blocks) * count, width),
            compiler_params=params,
            name="more_scores",
        )(unit, side, sums, mixed, *blocks)

    def final(unit, side, sums, mixed, *blocks):
        send = pl.pallas_call(
            send_kernel,
            out_shape=[
                shape(count // 2, width, dtype=bf16),
                shape(count // 2 + EXTRA, width, dtype=bf16),
            ],
            cost_estimate=cost(count, len(blocks) * count, width),
            compiler_params=params,
            name="send_scores",
        )(unit, side, sums, mixed, *blocks)
        keep_sums, keep = pl.pallas_call(
            keep_kernel,
            out_shape=[shape(count, 128), shape(count, width)],
            cost_estimate=cost(count, len(blocks) * count, width),
            compiler_params=params,
            name="keep_scores",
        )(unit, side, sums, mixed, *blocks)
        return keep_sums, keep, send

    pieces = embeddings.reshape(count // SUB, SUB, width // LANE, LANE).transpose(0, 2, 1, 3)
    base = pl.pallas_call(
        base_kernel,
        out_shape=shape(SUB, LANE),
        cost_estimate=pl.CostEstimate(flops=1000000000, bytes_accessed=0, transcendentals=0),
        compiler_params=params,
        name="base",
    )()
    own = pl.pallas_call(
        pack_kernel,
        out_shape=shape(tiles + 1, SUB, LANE, dtype=bf16),
        compiler_params=params,
        name="pack",
    )(pieces.reshape(tiles, SUB, LANE), cluster_id.reshape(1, count), priority.reshape(1, count), base)

    moved, beside = along(own, 1), across(own)
    other = swap(own)
    if rounds == 4:
        ahead = along(own, -1)
        moved, beside, other = lax.optimization_barrier((moved, beside, other))
        opposite = along(moved, 1)
        moved_beside = across(moved)
        ahead_beside = across(ahead)
        last = [along(moved_beside, 1)]
        unit, side, sums, mixed = first(own, other, beside, moved, moved_beside)
        sums, mixed = more(unit, side, sums, mixed, ahead, opposite, ahead_beside)
    else:
        unit, side, sums, mixed = first(own, other, beside)

        def turn(at, state):
            moved, sums, mixed = state
            ahead, beside = along(moved, 1), across(moved)
            sums, mixed = more(unit, side, sums, mixed, moved, beside)
            return ahead, sums, mixed

        moved, sums, mixed = lax.fori_loop(1, rounds - 1, turn, (moved, sums, mixed))
        last = [moved, across(moved)]
    keep_sums, keep, send = final(unit, side, sums, mixed, *last)
    dup, out = pl.pallas_call(
        combine_kernel,
        out_shape=[shape(1, count), shape(count, width)],
        compiler_params=params,
        name="combine",
    )(keep_sums, keep, *[swap(piece) for piece in send])
    return dup[0], out


def solution(mesh):
    placed = (
        P(("groups", "shard", "owner"), None),
        P(("groups", "shard", "owner"), None),
        P(("groups", "shard", "owner")),
    )
    return jax.shard_map(
        local,
        mesh=mesh,
        in_specs=placed,
        out_specs=(P(("groups", "shard", "owner")), P(("groups", "shard", "owner"), None)),
        check_vma=False,
    )
```

```python
import jax
import jax.numpy as jnp
from jax import lax
from jax.experimental import pallas as pl
from jax.experimental.pallas import tpu as pltpu
from jax.sharding import PartitionSpec as P

SUB, LANE = 8, 128
EXTRA = 8
VMEM = 24 * 1024 * 1024


def make_unit(rows):
    wide = rows.astype(jnp.float32)
    scale = lax.rsqrt(jnp.mean(wide * wide, axis=-1, keepdims=True) + 1e-06) / jnp.sqrt(
        jnp.float32(rows.shape[-1])
    )
    return (wide * scale).astype(jnp.bfloat16)


def diagonal(count):
    down = lax.broadcasted_iota(jnp.int32, (count, count), 0)
    return down == lax.broadcasted_iota(jnp.int32, (count, count), 1)


def as_row(column):
    return jnp.sum(jnp.where(diagonal(column.shape[0]), column, 0.0), axis=0, keepdims=True)


def as_column(row):
    return jnp.sum(jnp.where(diagonal(row.shape[1]), row, 0.0), axis=1, keepdims=True)


def halves(value):
    high = value.astype(jnp.bfloat16)
    return high, (value - high.astype(jnp.float32)).astype(jnp.bfloat16)


def base_kernel(base_ref):
    base_ref[...] = jnp.zeros_like(base_ref)


def pack_kernel(tiles_ref, label_ref, rank_ref, base_ref, packed_ref):
    many = tiles_ref.shape[0]
    packed_ref[:many] = tiles_ref[...]
    rank = rank_ref[...]
    high = lax.shift_right_logical(rank, 8)
    low = rank - lax.shift_left(high, 8)
    lines = [line.astype(jnp.float32) for line in (label_ref[...], high, low)]
    lines.append(base_ref[len(lines) :, :])
    packed_ref[many] = jnp.concatenate(lines, axis=0).astype(jnp.bfloat16)


def labels_and_ranks(block):
    tile = block[block.shape[0] - 1].astype(jnp.float32)
    return tile[0:1], tile[1:2] * 256.0 + tile[2:3]


def rows_of(blocks, width):
    across = width // LANE
    wide = []
    for block in blocks:
        tiles = block[: block.shape[0] - 1].astype(jnp.float32)
        tiles = tiles.reshape(-1, across, SUB, LANE)
        pieces = [tiles[:, at].reshape(-1, LANE) for at in range(across)]
        wide.append(jnp.concatenate(pieces, axis=1))
    return jnp.concatenate(wide, axis=0)


def score(unit, side, blocks):
    own_label, own_rank = side[:, 0:1], side[:, 1:2]
    wide = rows_of(blocks, unit.shape[1])
    keys = wide.astype(jnp.bfloat16)
    sides = [labels_and_ranks(block) for block in blocks]
    label = jnp.concatenate([item[0] for item in sides], axis=1)
    rank = jnp.concatenate([item[1] for item in sides], axis=1)
    cosine = lax.dot_general(
        unit, make_unit(wide), (((1,), (1,)), ((), ())), preferred_element_type=jnp.float32
    )
    weight = 1.0 / (1.0 + jnp.exp(-40.0 * (cosine - 0.05)))
    near = jnp.where((label == own_label) & (rank != own_rank), weight, 0.0)
    earlier = jnp.sum(jnp.where(rank < own_rank, near, 0.0), axis=1, keepdims=True)
    every = jnp.sum(near, axis=1, keepdims=True)
    mixed = jnp.dot(near.astype(jnp.bfloat16), keys, preferred_element_type=jnp.float32)
    return earlier, every, mixed


def first_kernel(own_ref, other_ref, *refs):
    blocks, (unit_ref, side_ref, sums_ref, mixed_ref) = refs[:-4], refs[-4:]
    count = own_ref.shape[0] // (unit_ref.shape[1] // LANE) * SUB
    side_ref[...] = jnp.zeros_like(side_ref)
    sums_ref[...] = jnp.zeros_like(sums_ref)
    unit_ref[...] = make_unit(rows_of([own_ref, other_ref], unit_ref.shape[1]))
    for at, ref in enumerate((own_ref, other_ref)):
        here = slice(at * count, (at + 1) * count)
        label, rank = labels_and_ranks(ref)
        side_ref[here, 0:1] = as_column(label)
        side_ref[here, 1:2] = as_column(rank)
    sums_ref[:, 0:1], sums_ref[:, 1:2], mixed_ref[...] = score(
        unit_ref[...], side_ref, (own_ref,) + blocks
    )


def more_kernel(unit_ref, side_ref, old_sums_ref, old_mixed_ref, *refs):
    blocks, (sums_ref, mixed_ref) = refs[:-2], refs[-2:]
    earlier, every, mixed = score(unit_ref[...], side_ref, blocks)
    sums_ref[...] = old_sums_ref[...]
    sums_ref[:, 0:1] += earlier
    sums_ref[:, 1:2] += every
    mixed_ref[...] = old_mixed_ref[...] + mixed


def send_kernel(unit_ref, side_ref, old_sums_ref, old_mixed_ref, *refs):
    blocks, send_ref = refs[:-1], refs[-1]
    count, width = send_ref.shape[0] - EXTRA, send_ref.shape[1]
    earlier, every, mixed = score(unit_ref[count:, :], side_ref[count:, :], blocks)
    earlier += old_sums_ref[count:, 0:1]
    every += old_sums_ref[count:, 1:2]
    send_ref[:count, :] = (mixed + old_mixed_ref[count:, :]).astype(jnp.bfloat16)
    pieces = halves(as_row(earlier)) + halves(as_row(every))
    pieces = [piece.astype(jnp.float32) for piece in pieces]
    pieces.append(jnp.zeros((1, width - 4 * count), jnp.float32))
    line = jnp.concatenate(pieces, axis=1)
    send_ref[count:, :] = jnp.broadcast_to(line, (EXTRA, width)).astype(jnp.bfloat16)


def keep_kernel(unit_ref, side_ref, old_sums_ref, old_mixed_ref, *refs):
    blocks, (sums_ref, mixed_ref) = refs[:-2], refs[-2:]
    count = mixed_ref.shape[0]
    earlier, every, mixed = score(unit_ref[:count, :], side_ref[:count, :], blocks)
    sums_ref[...] = old_sums_ref[:count, :]
    sums_ref[:, 0:1] += earlier
    sums_ref[:, 1:2] += every
    mixed_ref[...] = old_mixed_ref[:count, :] + mixed


def combine_kernel(sums_ref, mixed_ref, got_ref, dup_ref, out_ref):
    count = mixed_ref.shape[0]
    line = got_ref[count:, :].astype(jnp.float32)[:1]
    parts = [line[:, at * count : (at + 1) * count] for at in range(4)]
    every = sums_ref[:, 1:2] + as_column(parts[2] + parts[3])
    dup_ref[...] = jnp.log1p(as_row(sums_ref[:, 0:1]) + parts[0] + parts[1])
    mixed = mixed_ref[...] + got_ref[:count, :].astype(jnp.float32)
    out_ref[...] = mixed / jnp.sqrt(1.0 + every)


def cost(queries, keys, width):
    return pl.CostEstimate(
        flops=400 * queries * keys * width,
        bytes_accessed=8 * queries * width + 2 * keys * width,
        transcendentals=100 * queries * keys,
    )


def local(embeddings, cluster_id, priority):
    count, width = embeddings.shape
    tiles = count // SUB * (width // LANE)
    shards = lax.axis_size("shard")
    lanes = lax.axis_size("owner")
    rounds = shards // 2
    queries = 2 * count
    bf16, f32 = jnp.bfloat16, jnp.float32
    params = pltpu.CompilerParams(vmem_limit_bytes=VMEM)

    def shape(*dims, dtype=f32):
        return jax.ShapeDtypeStruct(dims, dtype)

    ring = list(range(0, rounds, 2)) + list(range(1, rounds, 2))[::-1]

    def along(array, step):
        pairs = [
            (2 * ring[at] + side, 2 * ring[(at + step) % rounds] + side)
            for at in range(rounds)
            for side in range(2)
        ]
        return lax.ppermute(array, "shard", pairs)

    def across(array):
        return lax.ppermute(array, "shard", [(at, at ^ 1) for at in range(shards)])

    def swap(array):
        return lax.ppermute(array, "owner", [(at, lanes - 1 - at) for at in range(lanes)])

    def first(*blocks):
        return pl.pallas_call(
            first_kernel,
            out_shape=[
                shape(queries, width, dtype=bf16),
                shape(queries, 128),
                shape(queries, 128),
                shape(queries, width),
            ],
            cost_estimate=cost(queries, (len(blocks) - 1) * count, width),
            compiler_params=params,
            name="first_scores",
        )(*blocks)

    def more(unit, side, sums, mixed, *blocks):
        return pl.pallas_call(
            more_kernel,
            out_shape=[shape(queries, 128), shape(queries, width)],
            input_output_aliases={2: 0, 3: 1},
            cost_estimate=cost(queries, len(blocks) * count, width),
            compiler_params=params,
            name="more_scores",
        )(unit, side, sums, mixed, *blocks)

    def final(unit, side, sums, mixed, *blocks):
        send = pl.pallas_call(
            send_kernel,
            out_shape=shape(count + EXTRA, width, dtype=bf16),
            cost_estimate=cost(count, len(blocks) * count, width),
            compiler_params=params,
            name="send_scores",
        )(unit, side, sums, mixed, *blocks)
        keep_sums, keep = pl.pallas_call(
            keep_kernel,
            out_shape=[shape(count, 128), shape(count, width)],
            cost_estimate=cost(count, len(blocks) * count, width),
            compiler_params=params,
            name="keep_scores",
        )(unit, side, sums, mixed, *blocks)
        return keep_sums, keep, send

    pieces = embeddings.reshape(count // SUB, SUB, width // LANE, LANE).transpose(0, 2, 1, 3)
    base = pl.pallas_call(
        base_kernel,
        out_shape=shape(SUB, LANE),
        cost_estimate=pl.CostEstimate(flops=1000000000, bytes_accessed=0, transcendentals=0),
        compiler_params=params,
        name="base",
    )()
    own = pl.pallas_call(
        pack_kernel,
        out_shape=shape(tiles + 1, SUB, LANE, dtype=bf16),
        compiler_params=params,
        name="pack",
    )(pieces.reshape(tiles, SUB, LANE), cluster_id.reshape(1, count), priority.reshape(1, count), base)

    moved, beside = along(own, 1), across(own)
    other = swap(own)
    if rounds == 4:
        ahead = along(own, -1)
        moved, beside, other = lax.optimization_barrier((moved, beside, other))
        opposite = along(moved, 1)
        moved_beside = across(moved)
        unit, side, sums, mixed = first(own, other, beside, moved, ahead)
        sums, ahead = lax.optimization_barrier((sums, ahead))
        ahead_beside = across(ahead)
        last = [along(moved_beside, 1), ahead_beside]
        sums, mixed = more(unit, side, sums, mixed, moved_beside, opposite)
    else:
        unit, side, sums, mixed = first(own, other, beside)

        def turn(at, state):
            moved, sums, mixed = state
            ahead, beside = along(moved, 1), across(moved)
            sums, mixed = more(unit, side, sums, mixed, moved, beside)
            return ahead, sums, mixed

        moved, sums, mixed = lax.fori_loop(1, rounds - 1, turn, (moved, sums, mixed))
        last = [moved, across(moved)]
    keep_sums, keep, send = final(unit, side, sums, mixed, *last)
    dup, out = pl.pallas_call(
        combine_kernel,
        out_shape=[shape(1, count), shape(count, width)],
        compiler_params=params,
        name="combine",
    )(keep_sums, keep, swap(send))
    return dup[0], out


def solution(mesh):
    placed = (
        P(("groups", "shard", "owner"), None),
        P(("groups", "shard", "owner"), None),
        P(("groups", "shard", "owner")),
    )
    return jax.shard_map(
        local,
        mesh=mesh,
        in_specs=placed,
        out_specs=(P(("groups", "shard", "owner")), P(("groups", "shard", "owner"), None)),
        check_vma=False,
    )
```

```python
import jax
import jax.numpy as jnp
from jax import lax
from jax.experimental import pallas as pl
from jax.experimental.pallas import tpu as pltpu
from jax.sharding import PartitionSpec as P

SUB, LANE = 8, 128
EXTRA = 8
VMEM = 24 * 1024 * 1024


def make_unit(rows):
    wide = rows.astype(jnp.float32)
    scale = lax.rsqrt(jnp.mean(wide * wide, axis=-1, keepdims=True) + 1e-06) / jnp.sqrt(
        jnp.float32(rows.shape[-1])
    )
    return (wide * scale).astype(jnp.bfloat16)


def diagonal(count):
    down = lax.broadcasted_iota(jnp.int32, (count, count), 0)
    return down == lax.broadcasted_iota(jnp.int32, (count, count), 1)


def as_row(column):
    return jnp.sum(jnp.where(diagonal(column.shape[0]), column, 0.0), axis=0, keepdims=True)


def as_column(row):
    return jnp.sum(jnp.where(diagonal(row.shape[1]), row, 0.0), axis=1, keepdims=True)


def halves(value):
    high = value.astype(jnp.bfloat16)
    return high, (value - high.astype(jnp.float32)).astype(jnp.bfloat16)


def base_kernel(base_ref):
    base_ref[...] = jnp.zeros_like(base_ref)


def pack_kernel(tiles_ref, label_ref, rank_ref, base_ref, packed_ref):
    many = tiles_ref.shape[0]
    packed_ref[:many] = tiles_ref[...]
    rank = rank_ref[...]
    high = lax.shift_right_logical(rank, 8)
    low = rank - lax.shift_left(high, 8)
    lines = [line.astype(jnp.float32) for line in (label_ref[...], high, low)]
    lines.append(base_ref[len(lines) :, :])
    packed_ref[many] = jnp.concatenate(lines, axis=0).astype(jnp.bfloat16)


def labels_and_ranks(block):
    tile = block[block.shape[0] - 1].astype(jnp.float32)
    return tile[0:1], tile[1:2] * 256.0 + tile[2:3]


def rows_of(blocks, width):
    across = width // LANE
    wide = []
    for block in blocks:
        tiles = block[: block.shape[0] - 1].astype(jnp.float32)
        tiles = tiles.reshape(-1, across, SUB, LANE)
        pieces = [tiles[:, at].reshape(-1, LANE) for at in range(across)]
        wide.append(jnp.concatenate(pieces, axis=1))
    return jnp.concatenate(wide, axis=0)


def score(unit, side, blocks):
    own_label, own_rank = side[:, 0:1], side[:, 1:2]
    wide = rows_of(blocks, unit.shape[1])
    keys = wide.astype(jnp.bfloat16)
    sides = [labels_and_ranks(block) for block in blocks]
    label = jnp.concatenate([item[0] for item in sides], axis=1)
    rank = jnp.concatenate([item[1] for item in sides], axis=1)
    cosine = lax.dot_general(
        unit, make_unit(wide), (((1,), (1,)), ((), ())), preferred_element_type=jnp.float32
    )
    weight = 1.0 / (1.0 + jnp.exp(-40.0 * (cosine - 0.05)))
    near = jnp.where((label == own_label) & (rank != own_rank), weight, 0.0)
    earlier = jnp.sum(jnp.where(rank < own_rank, near, 0.0), axis=1, keepdims=True)
    every = jnp.sum(near, axis=1, keepdims=True)
    mixed = jnp.dot(near.astype(jnp.bfloat16), keys, preferred_element_type=jnp.float32)
    return earlier, every, mixed


def first_kernel(own_ref, other_ref, *refs):
    blocks, (unit_ref, side_ref, sums_ref, mixed_ref) = refs[:-4], refs[-4:]
    count = own_ref.shape[0] // (unit_ref.shape[1] // LANE) * SUB
    side_ref[...] = jnp.zeros_like(side_ref)
    sums_ref[...] = jnp.zeros_like(sums_ref)
    unit_ref[...] = make_unit(rows_of([own_ref, other_ref], unit_ref.shape[1]))
    for at, ref in enumerate((own_ref, other_ref)):
        here = slice(at * count, (at + 1) * count)
        label, rank = labels_and_ranks(ref)
        side_ref[here, 0:1] = as_column(label)
        side_ref[here, 1:2] = as_column(rank)
    sums_ref[:, 0:1], sums_ref[:, 1:2], mixed_ref[...] = score(
        unit_ref[...], side_ref, (own_ref,) + blocks
    )


def more_kernel(unit_ref, side_ref, old_sums_ref, old_mixed_ref, *refs):
    blocks, (sums_ref, mixed_ref) = refs[:-2], refs[-2:]
    earlier, every, mixed = score(unit_ref[...], side_ref, blocks)
    sums_ref[...] = old_sums_ref[...]
    sums_ref[:, 0:1] += earlier
    sums_ref[:, 1:2] += every
    mixed_ref[...] = old_mixed_ref[...] + mixed


def send_kernel(unit_ref, side_ref, old_sums_ref, old_mixed_ref, *refs):
    blocks, send_ref = refs[:-1], refs[-1]
    count, width = send_ref.shape[0] - EXTRA, send_ref.shape[1]
    earlier, every, mixed = score(unit_ref[count:, :], side_ref[count:, :], blocks)
    earlier += old_sums_ref[count:, 0:1]
    every += old_sums_ref[count:, 1:2]
    send_ref[:count, :] = (mixed + old_mixed_ref[count:, :]).astype(jnp.bfloat16)
    pieces = halves(as_row(earlier)) + halves(as_row(every))
    pieces = [piece.astype(jnp.float32) for piece in pieces]
    pieces.append(jnp.zeros((1, width - 4 * count), jnp.float32))
    line = jnp.concatenate(pieces, axis=1)
    send_ref[count:, :] = jnp.broadcast_to(line, (EXTRA, width)).astype(jnp.bfloat16)


def keep_kernel(unit_ref, side_ref, old_sums_ref, old_mixed_ref, *refs):
    blocks, (sums_ref, mixed_ref) = refs[:-2], refs[-2:]
    count = mixed_ref.shape[0]
    earlier, every, mixed = score(unit_ref[:count, :], side_ref[:count, :], blocks)
    sums_ref[...] = old_sums_ref[:count, :]
    sums_ref[:, 0:1] += earlier
    sums_ref[:, 1:2] += every
    mixed_ref[...] = old_mixed_ref[:count, :] + mixed


def combine_kernel(sums_ref, mixed_ref, got_ref, dup_ref, out_ref):
    count = mixed_ref.shape[0]
    line = got_ref[count:, :].astype(jnp.float32)[:1]
    parts = [line[:, at * count : (at + 1) * count] for at in range(4)]
    every = sums_ref[:, 1:2] + as_column(parts[2] + parts[3])
    dup_ref[...] = jnp.log1p(as_row(sums_ref[:, 0:1]) + parts[0] + parts[1])
    mixed = mixed_ref[...] + got_ref[:count, :].astype(jnp.float32)
    out_ref[...] = mixed / jnp.sqrt(1.0 + every)


def cost(queries, keys, width):
    return pl.CostEstimate(
        flops=400 * queries * keys * width,
        bytes_accessed=8 * queries * width + 2 * keys * width,
        transcendentals=100 * queries * keys,
    )


def local(embeddings, cluster_id, priority):
    count, width = embeddings.shape
    tiles = count // SUB * (width // LANE)
    shards = lax.axis_size("shard")
    lanes = lax.axis_size("owner")
    rounds = shards // 2
    queries = 2 * count
    bf16, f32 = jnp.bfloat16, jnp.float32
    params = pltpu.CompilerParams(vmem_limit_bytes=VMEM)

    def shape(*dims, dtype=f32):
        return jax.ShapeDtypeStruct(dims, dtype)

    ring = list(range(0, rounds, 2)) + list(range(1, rounds, 2))[::-1]

    def along(array, step):
        pairs = [
            (2 * ring[at] + side, 2 * ring[(at + step) % rounds] + side)
            for at in range(rounds)
            for side in range(2)
        ]
        return lax.ppermute(array, "shard", pairs)

    def across(array):
        return lax.ppermute(array, "shard", [(at, at ^ 1) for at in range(shards)])

    def swap(array):
        return lax.ppermute(array, "owner", [(at, lanes - 1 - at) for at in range(lanes)])

    def first(*blocks):
        return pl.pallas_call(
            first_kernel,
            out_shape=[
                shape(queries, width, dtype=bf16),
                shape(queries, 128),
                shape(queries, 128),
                shape(queries, width),
            ],
            cost_estimate=cost(queries, (len(blocks) - 1) * count, width),
            compiler_params=params,
            name="first_scores",
        )(*blocks)

    def more(unit, side, sums, mixed, *blocks):
        return pl.pallas_call(
            more_kernel,
            out_shape=[shape(queries, 128), shape(queries, width)],
            input_output_aliases={2: 0, 3: 1},
            cost_estimate=cost(queries, len(blocks) * count, width),
            compiler_params=params,
            name="more_scores",
        )(unit, side, sums, mixed, *blocks)

    def final(unit, side, sums, mixed, *blocks):
        send = pl.pallas_call(
            send_kernel,
            out_shape=shape(count + EXTRA, width, dtype=bf16),
            cost_estimate=cost(count, len(blocks) * count, width),
            compiler_params=params,
            name="send_scores",
        )(unit, side, sums, mixed, *blocks)
        keep_sums, keep = pl.pallas_call(
            keep_kernel,
            out_shape=[shape(count, 128), shape(count, width)],
            cost_estimate=cost(count, len(blocks) * count, width),
            compiler_params=params,
            name="keep_scores",
        )(unit, side, sums, mixed, *blocks)
        return keep_sums, keep, send

    pieces = embeddings.reshape(count // SUB, SUB, width // LANE, LANE).transpose(0, 2, 1, 3)
    base = pl.pallas_call(
        base_kernel,
        out_shape=shape(SUB, LANE),
        cost_estimate=pl.CostEstimate(flops=1000000000, bytes_accessed=0, transcendentals=0),
        compiler_params=params,
        name="base",
    )()
    own = pl.pallas_call(
        pack_kernel,
        out_shape=shape(tiles + 1, SUB, LANE, dtype=bf16),
        compiler_params=params,
        name="pack",
    )(pieces.reshape(tiles, SUB, LANE), cluster_id.reshape(1, count), priority.reshape(1, count), base)

    moved, beside = along(own, 1), across(own)
    other = swap(own)
    if rounds == 4:
        ahead = along(own, -1)
        moved, beside = lax.optimization_barrier((moved, beside))
        opposite = along(moved, 1)
        moved_beside = across(moved)
        ahead_beside = across(ahead)
        last = [along(moved_beside, 1)]
        unit, side, sums, mixed = first(own, other, beside, moved, moved_beside)
        sums, mixed = more(unit, side, sums, mixed, ahead, opposite, ahead_beside)
    else:
        unit, side, sums, mixed = first(own, other, beside)

        def turn(at, state):
            moved, sums, mixed = state
            ahead, beside = along(moved, 1), across(moved)
            sums, mixed = more(unit, side, sums, mixed, moved, beside)
            return ahead, sums, mixed

        moved, sums, mixed = lax.fori_loop(1, rounds - 1, turn, (moved, sums, mixed))
        last = [moved, across(moved)]
    keep_sums, keep, send = final(unit, side, sums, mixed, *last)
    dup, out = pl.pallas_call(
        combine_kernel,
        out_shape=[shape(1, count), shape(count, width)],
        compiler_params=params,
        name="combine",
    )(keep_sums, keep, swap(send))
    return dup[0], out


def solution(mesh):
    placed = (
        P(("groups", "shard", "owner"), None),
        P(("groups", "shard", "owner"), None),
        P(("groups", "shard", "owner")),
    )
    return jax.shard_map(
        local,
        mesh=mesh,
        in_specs=placed,
        out_specs=(P(("groups", "shard", "owner")), P(("groups", "shard", "owner"), None)),
        check_vma=False,
    )
```

```python
import jax
import jax.numpy as jnp
from jax import lax
from jax.experimental import pallas as pl
from jax.experimental.pallas import tpu as pltpu
from jax.sharding import PartitionSpec as P

SUB, LANE = 8, 128
EXTRA = 8
VMEM = 24 * 1024 * 1024


def make_unit(rows):
    wide = rows.astype(jnp.float32)
    scale = lax.rsqrt(jnp.mean(wide * wide, axis=-1, keepdims=True) + 1e-06) / jnp.sqrt(
        jnp.float32(rows.shape[-1])
    )
    return (wide * scale).astype(jnp.bfloat16)


def diagonal(count):
    down = lax.broadcasted_iota(jnp.int32, (count, count), 0)
    return down == lax.broadcasted_iota(jnp.int32, (count, count), 1)


def as_row(column):
    return jnp.sum(jnp.where(diagonal(column.shape[0]), column, 0.0), axis=0, keepdims=True)


def as_column(row):
    return jnp.sum(jnp.where(diagonal(row.shape[1]), row, 0.0), axis=1, keepdims=True)


def halves(value):
    high = value.astype(jnp.bfloat16)
    return high, (value - high.astype(jnp.float32)).astype(jnp.bfloat16)


def base_kernel(base_ref):
    base_ref[...] = jnp.zeros_like(base_ref)


def pack_kernel(tiles_ref, label_ref, rank_ref, base_ref, packed_ref):
    many = tiles_ref.shape[0]
    packed_ref[:many] = tiles_ref[...]
    rank = rank_ref[...]
    high = lax.shift_right_logical(rank, 8)
    low = rank - lax.shift_left(high, 8)
    lines = [line.astype(jnp.float32) for line in (label_ref[...], high, low)]
    lines.append(base_ref[len(lines) :, :])
    packed_ref[many] = jnp.concatenate(lines, axis=0).astype(jnp.bfloat16)


def labels_and_ranks(block):
    tile = block[block.shape[0] - 1].astype(jnp.float32)
    return tile[0:1], tile[1:2] * 256.0 + tile[2:3]


def rows_of(blocks, width):
    across = width // LANE
    wide = []
    for block in blocks:
        tiles = block[: block.shape[0] - 1].astype(jnp.float32)
        tiles = tiles.reshape(-1, across, SUB, LANE)
        pieces = [tiles[:, at].reshape(-1, LANE) for at in range(across)]
        wide.append(jnp.concatenate(pieces, axis=1))
    return jnp.concatenate(wide, axis=0)


def score(unit, side, blocks):
    own_label, own_rank = side[:, 0:1], side[:, 1:2]
    wide = rows_of(blocks, unit.shape[1])
    keys = wide.astype(jnp.bfloat16)
    sides = [labels_and_ranks(block) for block in blocks]
    label = jnp.concatenate([item[0] for item in sides], axis=1)
    rank = jnp.concatenate([item[1] for item in sides], axis=1)
    cosine = lax.dot_general(
        unit, make_unit(wide), (((1,), (1,)), ((), ())), preferred_element_type=jnp.float32
    )
    weight = 1.0 / (1.0 + jnp.exp(-40.0 * (cosine - 0.05)))
    near = jnp.where((label == own_label) & (rank != own_rank), weight, 0.0)
    earlier = jnp.sum(jnp.where(rank < own_rank, near, 0.0), axis=1, keepdims=True)
    every = jnp.sum(near, axis=1, keepdims=True)
    mixed = jnp.dot(near.astype(jnp.bfloat16), keys, preferred_element_type=jnp.float32)
    return earlier, every, mixed


def first_kernel(own_ref, other_ref, *refs):
    blocks, (unit_ref, side_ref, sums_ref, mixed_ref) = refs[:-4], refs[-4:]
    count = own_ref.shape[0] // (unit_ref.shape[1] // LANE) * SUB
    side_ref[...] = jnp.zeros_like(side_ref)
    sums_ref[...] = jnp.zeros_like(sums_ref)
    unit_ref[...] = make_unit(rows_of([own_ref, other_ref], unit_ref.shape[1]))
    for at, ref in enumerate((own_ref, other_ref)):
        here = slice(at * count, (at + 1) * count)
        label, rank = labels_and_ranks(ref)
        side_ref[here, 0:1] = as_column(label)
        side_ref[here, 1:2] = as_column(rank)
    sums_ref[:, 0:1], sums_ref[:, 1:2], mixed_ref[...] = score(
        unit_ref[...], side_ref, (own_ref,) + blocks
    )


def more_kernel(unit_ref, side_ref, old_sums_ref, old_mixed_ref, *refs):
    blocks, (sums_ref, mixed_ref) = refs[:-2], refs[-2:]
    earlier, every, mixed = score(unit_ref[...], side_ref, blocks)
    sums_ref[...] = old_sums_ref[...]
    sums_ref[:, 0:1] += earlier
    sums_ref[:, 1:2] += every
    mixed_ref[...] = old_mixed_ref[...] + mixed


def send_kernel(unit_ref, side_ref, old_sums_ref, old_mixed_ref, *refs):
    blocks, send_ref = refs[:-1], refs[-1]
    count, width = send_ref.shape[0] - EXTRA, send_ref.shape[1]
    earlier, every, mixed = score(unit_ref[count:, :], side_ref[count:, :], blocks)
    earlier += old_sums_ref[count:, 0:1]
    every += old_sums_ref[count:, 1:2]
    send_ref[:count, :] = (mixed + old_mixed_ref[count:, :]).astype(jnp.bfloat16)
    pieces = halves(as_row(earlier)) + halves(as_row(every))
    pieces = [piece.astype(jnp.float32) for piece in pieces]
    pieces.append(jnp.zeros((1, width - 4 * count), jnp.float32))
    line = jnp.concatenate(pieces, axis=1)
    send_ref[count:, :] = jnp.broadcast_to(line, (EXTRA, width)).astype(jnp.bfloat16)


def keep_kernel(unit_ref, side_ref, old_sums_ref, old_mixed_ref, *refs):
    blocks, (sums_ref, mixed_ref) = refs[:-2], refs[-2:]
    count = mixed_ref.shape[0]
    earlier, every, mixed = score(unit_ref[:count, :], side_ref[:count, :], blocks)
    sums_ref[...] = old_sums_ref[:count, :]
    sums_ref[:, 0:1] += earlier
    sums_ref[:, 1:2] += every
    mixed_ref[...] = old_mixed_ref[:count, :] + mixed


def combine_kernel(sums_ref, mixed_ref, got_ref, dup_ref, out_ref):
    count = mixed_ref.shape[0]
    line = got_ref[count:, :].astype(jnp.float32)[:1]
    parts = [line[:, at * count : (at + 1) * count] for at in range(4)]
    every = sums_ref[:, 1:2] + as_column(parts[2] + parts[3])
    dup_ref[...] = jnp.log1p(as_row(sums_ref[:, 0:1]) + parts[0] + parts[1])
    mixed = mixed_ref[...] + got_ref[:count, :].astype(jnp.float32)
    out_ref[...] = mixed / jnp.sqrt(1.0 + every)


def cost(queries, keys, width):
    return pl.CostEstimate(
        flops=400 * queries * keys * width,
        bytes_accessed=8 * queries * width + 2 * keys * width,
        transcendentals=100 * queries * keys,
    )


def local(embeddings, cluster_id, priority):
    count, width = embeddings.shape
    tiles = count // SUB * (width // LANE)
    shards = lax.axis_size("shard")
    lanes = lax.axis_size("owner")
    rounds = shards // 2
    queries = 2 * count
    bf16, f32 = jnp.bfloat16, jnp.float32
    params = pltpu.CompilerParams(vmem_limit_bytes=VMEM)

    def shape(*dims, dtype=f32):
        return jax.ShapeDtypeStruct(dims, dtype)

    ring = list(range(0, rounds, 2)) + list(range(1, rounds, 2))[::-1]

    def along(array, step):
        pairs = [
            (2 * ring[at] + side, 2 * ring[(at + step) % rounds] + side)
            for at in range(rounds)
            for side in range(2)
        ]
        return lax.ppermute(array, "shard", pairs)

    def across(array):
        return lax.ppermute(array, "shard", [(at, at ^ 1) for at in range(shards)])

    def two_ways(array, ring_lane):
        pairs = []
        for at in range(rounds):
            for side in range(2):
                here, there = 2 * ring[at] + side, 2 * ring[(at + 1) % rounds] + side
                pairs += [
                    (here * lanes + lane, (there if lane == ring_lane else here ^ 1) * lanes + lane)
                    for lane in range(lanes)
                ]
        return lax.ppermute(array, ("shard", "owner"), pairs)

    def swap(array):
        return lax.ppermute(array, "owner", [(at, lanes - 1 - at) for at in range(lanes)])

    def first(*blocks):
        return pl.pallas_call(
            first_kernel,
            out_shape=[
                shape(queries, width, dtype=bf16),
                shape(queries, 128),
                shape(queries, 128),
                shape(queries, width),
            ],
            cost_estimate=cost(queries, (len(blocks) - 1) * count, width),
            compiler_params=params,
            name="first_scores",
        )(*blocks)

    def more(unit, side, sums, mixed, *blocks):
        return pl.pallas_call(
            more_kernel,
            out_shape=[shape(queries, 128), shape(queries, width)],
            input_output_aliases={2: 0, 3: 1},
            cost_estimate=cost(queries, len(blocks) * count, width),
            compiler_params=params,
            name="more_scores",
        )(unit, side, sums, mixed, *blocks)

    def final(unit, side, sums, mixed, *blocks):
        send = pl.pallas_call(
            send_kernel,
            out_shape=shape(count + EXTRA, width, dtype=bf16),
            cost_estimate=cost(count, len(blocks) * count, width),
            compiler_params=params,
            name="send_scores",
        )(unit, side, sums, mixed, *blocks)
        keep_sums, keep = pl.pallas_call(
            keep_kernel,
            out_shape=[shape(count, 128), shape(count, width)],
            cost_estimate=cost(count, len(blocks) * count, width),
            compiler_params=params,
            name="keep_scores",
        )(unit, side, sums, mixed, *blocks)
        return keep_sums, keep, send

    pieces = embeddings.reshape(count // SUB, SUB, width // LANE, LANE).transpose(0, 2, 1, 3)
    base = pl.pallas_call(
        base_kernel,
        out_shape=shape(SUB, LANE),
        cost_estimate=pl.CostEstimate(flops=1000000000, bytes_accessed=0, transcendentals=0),
        compiler_params=params,
        name="base",
    )()
    own = pl.pallas_call(
        pack_kernel,
        out_shape=shape(tiles + 1, SUB, LANE, dtype=bf16),
        compiler_params=params,
        name="pack",
    )(pieces.reshape(tiles, SUB, LANE), cluster_id.reshape(1, count), priority.reshape(1, count), base)

    moved, beside = along(own, 1), across(own)
    other = swap(own)
    if rounds == 4:
        ahead = along(own, -1)
        moved, beside = lax.optimization_barrier((moved, beside))
        sooner, later = two_ways(moved, 1), two_ways(moved, 0)
        ahead_beside = across(ahead)
        last = [two_ways(sooner, 0), ahead_beside]
        unit, side, sums, mixed = first(own, other, beside, moved, sooner)
        sums, mixed = more(unit, side, sums, mixed, ahead, later)
    else:
        unit, side, sums, mixed = first(own, other, beside)

        def turn(at, state):
            moved, sums, mixed = state
            ahead, beside = along(moved, 1), across(moved)
            sums, mixed = more(unit, side, sums, mixed, moved, beside)
            return ahead, sums, mixed

        moved, sums, mixed = lax.fori_loop(1, rounds - 1, turn, (moved, sums, mixed))
        last = [moved, across(moved)]
    keep_sums, keep, send = final(unit, side, sums, mixed, *last)
    dup, out = pl.pallas_call(
        combine_kernel,
        out_shape=[shape(1, count), shape(count, width)],
        compiler_params=params,
        name="combine",
    )(keep_sums, keep, swap(send))
    return dup[0], out


def solution(mesh):
    placed = (
        P(("groups", "shard", "owner"), None),
        P(("groups", "shard", "owner"), None),
        P(("groups", "shard", "owner")),
    )
    return jax.shard_map(
        local,
        mesh=mesh,
        in_specs=placed,
        out_specs=(P(("groups", "shard", "owner")), P(("groups", "shard", "owner"), None)),
        check_vma=False,
    )
```

```python
import jax
import jax.numpy as jnp
from jax import lax
from jax.experimental import pallas as pl
from jax.experimental.pallas import tpu as pltpu
from jax.sharding import PartitionSpec as P

SUB, LANE = 8, 128
EXTRA = 8
VMEM = 24 * 1024 * 1024


def make_unit(rows):
    wide = rows.astype(jnp.float32)
    scale = lax.rsqrt(jnp.mean(wide * wide, axis=-1, keepdims=True) + 1e-06) / jnp.sqrt(
        jnp.float32(rows.shape[-1])
    )
    return (wide * scale).astype(jnp.bfloat16)


def diagonal(count):
    down = lax.broadcasted_iota(jnp.int32, (count, count), 0)
    return down == lax.broadcasted_iota(jnp.int32, (count, count), 1)


def as_row(column):
    return jnp.sum(jnp.where(diagonal(column.shape[0]), column, 0.0), axis=0, keepdims=True)


def as_column(row):
    return jnp.sum(jnp.where(diagonal(row.shape[1]), row, 0.0), axis=1, keepdims=True)


def halves(value):
    high = value.astype(jnp.bfloat16)
    return high, (value - high.astype(jnp.float32)).astype(jnp.bfloat16)


def base_kernel(base_ref):
    base_ref[...] = jnp.zeros_like(base_ref)


def pack_kernel(tiles_ref, label_ref, rank_ref, base_ref, packed_ref):
    many = tiles_ref.shape[0]
    packed_ref[:many] = tiles_ref[...]
    rank = rank_ref[...]
    high = lax.shift_right_logical(rank, 8)
    low = rank - lax.shift_left(high, 8)
    lines = [line.astype(jnp.float32) for line in (label_ref[...], high, low)]
    lines.append(base_ref[len(lines) :, :])
    packed_ref[many] = jnp.concatenate(lines, axis=0).astype(jnp.bfloat16)


def labels_and_ranks(block):
    tile = block[block.shape[0] - 1].astype(jnp.float32)
    return tile[0:1], tile[1:2] * 256.0 + tile[2:3]


def rows_of(blocks, width):
    across = width // LANE
    wide = []
    for block in blocks:
        tiles = block[: block.shape[0] - 1].astype(jnp.float32)
        tiles = tiles.reshape(-1, across, SUB, LANE)
        pieces = [tiles[:, at].reshape(-1, LANE) for at in range(across)]
        wide.append(jnp.concatenate(pieces, axis=1))
    return jnp.concatenate(wide, axis=0)


def score(unit, side, blocks):
    own_label, own_rank = side[:, 0:1], side[:, 1:2]
    wide = rows_of(blocks, unit.shape[1])
    keys = wide.astype(jnp.bfloat16)
    sides = [labels_and_ranks(block) for block in blocks]
    label = jnp.concatenate([item[0] for item in sides], axis=1)
    rank = jnp.concatenate([item[1] for item in sides], axis=1)
    cosine = lax.dot_general(
        unit, make_unit(wide), (((1,), (1,)), ((), ())), preferred_element_type=jnp.float32
    )
    weight = 1.0 / (1.0 + jnp.exp(-40.0 * (cosine - 0.05)))
    near = jnp.where((label == own_label) & (rank != own_rank), weight, 0.0)
    earlier = jnp.sum(jnp.where(rank < own_rank, near, 0.0), axis=1, keepdims=True)
    every = jnp.sum(near, axis=1, keepdims=True)
    mixed = jnp.dot(near.astype(jnp.bfloat16), keys, preferred_element_type=jnp.float32)
    return earlier, every, mixed


def first_kernel(own_ref, other_ref, *refs):
    blocks, (unit_ref, side_ref, sums_ref, mixed_ref) = refs[:-4], refs[-4:]
    count = own_ref.shape[0] // (unit_ref.shape[1] // LANE) * SUB
    side_ref[...] = jnp.zeros_like(side_ref)
    sums_ref[...] = jnp.zeros_like(sums_ref)
    unit_ref[...] = make_unit(rows_of([own_ref, other_ref], unit_ref.shape[1]))
    for at, ref in enumerate((own_ref, other_ref)):
        here = slice(at * count, (at + 1) * count)
        label, rank = labels_and_ranks(ref)
        side_ref[here, 0:1] = as_column(label)
        side_ref[here, 1:2] = as_column(rank)
    sums_ref[:, 0:1], sums_ref[:, 1:2], mixed_ref[...] = score(
        unit_ref[...], side_ref, (own_ref,) + blocks
    )


def more_kernel(unit_ref, side_ref, old_sums_ref, old_mixed_ref, *refs):
    blocks, (sums_ref, mixed_ref) = refs[:-2], refs[-2:]
    earlier, every, mixed = score(unit_ref[...], side_ref, blocks)
    sums_ref[...] = old_sums_ref[...]
    sums_ref[:, 0:1] += earlier
    sums_ref[:, 1:2] += every
    mixed_ref[...] = old_mixed_ref[...] + mixed


def send_kernel(unit_ref, side_ref, old_sums_ref, old_mixed_ref, *refs):
    blocks, send_ref = refs[:-1], refs[-1]
    count, width = send_ref.shape[0] - EXTRA, send_ref.shape[1]
    earlier, every, mixed = score(unit_ref[count:, :], side_ref[count:, :], blocks)
    earlier += old_sums_ref[count:, 0:1]
    every += old_sums_ref[count:, 1:2]
    send_ref[:count, :] = (mixed + old_mixed_ref[count:, :]).astype(jnp.bfloat16)
    pieces = halves(as_row(earlier)) + halves(as_row(every))
    pieces = [piece.astype(jnp.float32) for piece in pieces]
    pieces.append(jnp.zeros((1, width - 4 * count), jnp.float32))
    line = jnp.concatenate(pieces, axis=1)
    send_ref[count:, :] = jnp.broadcast_to(line, (EXTRA, width)).astype(jnp.bfloat16)


def keep_kernel(unit_ref, side_ref, old_sums_ref, old_mixed_ref, *refs):
    blocks, (sums_ref, mixed_ref) = refs[:-2], refs[-2:]
    count = mixed_ref.shape[0]
    earlier, every, mixed = score(unit_ref[:count, :], side_ref[:count, :], blocks)
    sums_ref[...] = old_sums_ref[:count, :]
    sums_ref[:, 0:1] += earlier
    sums_ref[:, 1:2] += every
    mixed_ref[...] = old_mixed_ref[:count, :] + mixed


def combine_kernel(sums_ref, mixed_ref, got_ref, dup_ref, out_ref):
    count = mixed_ref.shape[0]
    line = got_ref[count:, :].astype(jnp.float32)[:1]
    parts = [line[:, at * count : (at + 1) * count] for at in range(4)]
    every = sums_ref[:, 1:2] + as_column(parts[2] + parts[3])
    dup_ref[...] = jnp.log1p(as_row(sums_ref[:, 0:1]) + parts[0] + parts[1])
    mixed = mixed_ref[...] + got_ref[:count, :].astype(jnp.float32)
    out_ref[...] = mixed / jnp.sqrt(1.0 + every)


def cost(queries, keys, width):
    return pl.CostEstimate(
        flops=400 * queries * keys * width,
        bytes_accessed=8 * queries * width + 2 * keys * width,
        transcendentals=100 * queries * keys,
    )


def local(embeddings, cluster_id, priority):
    count, width = embeddings.shape
    tiles = count // SUB * (width // LANE)
    shards = lax.axis_size("shard")
    lanes = lax.axis_size("owner")
    rounds = shards // 2
    queries = 2 * count
    bf16, f32 = jnp.bfloat16, jnp.float32
    params = pltpu.CompilerParams(vmem_limit_bytes=VMEM)

    def shape(*dims, dtype=f32):
        return jax.ShapeDtypeStruct(dims, dtype)

    ring = list(range(0, rounds, 2)) + list(range(1, rounds, 2))[::-1]

    def along(array, step):
        pairs = [
            (2 * ring[at] + side, 2 * ring[(at + step) % rounds] + side)
            for at in range(rounds)
            for side in range(2)
        ]
        return lax.ppermute(array, "shard", pairs)

    def across(array):
        return lax.ppermute(array, "shard", [(at, at ^ 1) for at in range(shards)])

    def swap(array):
        return lax.ppermute(array, "owner", [(at, lanes - 1 - at) for at in range(lanes)])

    def first(*blocks):
        return pl.pallas_call(
            first_kernel,
            out_shape=[
                shape(queries, width, dtype=bf16),
                shape(queries, 128),
                shape(queries, 128),
                shape(queries, width),
            ],
            cost_estimate=cost(queries, (len(blocks) - 1) * count, width),
            compiler_params=params,
            name="first_scores",
        )(*blocks)

    def more(unit, side, sums, mixed, *blocks):
        return pl.pallas_call(
            more_kernel,
            out_shape=[shape(queries, 128), shape(queries, width)],
            input_output_aliases={2: 0, 3: 1},
            cost_estimate=cost(queries, len(blocks) * count, width),
            compiler_params=params,
            name="more_scores",
        )(unit, side, sums, mixed, *blocks)

    def final(unit, side, sums, mixed, *blocks):
        send = pl.pallas_call(
            send_kernel,
            out_shape=shape(count + EXTRA, width, dtype=bf16),
            cost_estimate=cost(count, len(blocks) * count, width),
            compiler_params=params,
            name="send_scores",
        )(unit, side, sums, mixed, *blocks)
        keep_sums, keep = pl.pallas_call(
            keep_kernel,
            out_shape=[shape(count, 128), shape(count, width)],
            cost_estimate=cost(count, len(blocks) * count, width),
            compiler_params=params,
            name="keep_scores",
        )(unit, side, sums, mixed, *blocks)
        return keep_sums, keep, send

    pieces = embeddings.reshape(count // SUB, SUB, width // LANE, LANE).transpose(0, 2, 1, 3)
    base = pl.pallas_call(
        base_kernel,
        out_shape=shape(SUB, LANE),
        cost_estimate=pl.CostEstimate(flops=1000000000, bytes_accessed=0, transcendentals=0),
        compiler_params=params,
        name="base",
    )()
    own = pl.pallas_call(
        pack_kernel,
        out_shape=shape(tiles + 1, SUB, LANE, dtype=bf16),
        compiler_params=params,
        name="pack",
    )(pieces.reshape(tiles, SUB, LANE), cluster_id.reshape(1, count), priority.reshape(1, count), base)

    moved, beside = along(own, 1), across(own)
    if rounds == 4:
        ahead = along(own, -1)
        moved, beside = lax.optimization_barrier((moved, beside))
        opposite = along(moved, 1)
        moved_beside = across(moved)
        packed, ahead = lax.optimization_barrier((own, ahead))
        other = swap(packed)
        ahead_beside = across(ahead)
        last = [along(moved_beside, 1)]
        unit, side, sums, mixed = first(own, other, beside, moved, moved_beside)
        sums, mixed = more(unit, side, sums, mixed, ahead, opposite, ahead_beside)
    else:
        other = swap(own)
        unit, side, sums, mixed = first(own, other, beside)

        def turn(at, state):
            moved, sums, mixed = state
            ahead, beside = along(moved, 1), across(moved)
            sums, mixed = more(unit, side, sums, mixed, moved, beside)
            return ahead, sums, mixed

        moved, sums, mixed = lax.fori_loop(1, rounds - 1, turn, (moved, sums, mixed))
        last = [moved, across(moved)]
    keep_sums, keep, send = final(unit, side, sums, mixed, *last)
    dup, out = pl.pallas_call(
        combine_kernel,
        out_shape=[shape(1, count), shape(count, width)],
        compiler_params=params,
        name="combine",
    )(keep_sums, keep, swap(send))
    return dup[0], out


def solution(mesh):
    placed = (
        P(("groups", "shard", "owner"), None),
        P(("groups", "shard", "owner"), None),
        P(("groups", "shard", "owner")),
    )
    return jax.shard_map(
        local,
        mesh=mesh,
        in_specs=placed,
        out_specs=(P(("groups", "shard", "owner")), P(("groups", "shard", "owner"), None)),
        check_vma=False,
    )
```

```python
import jax
import jax.numpy as jnp
from jax import lax
from jax.experimental import pallas as pl
from jax.experimental.pallas import tpu as pltpu
from jax.sharding import PartitionSpec as P

SUB, LANE = 8, 128
EXTRA = 8
VMEM = 24 * 1024 * 1024


def make_unit(rows):
    wide = rows.astype(jnp.float32)
    scale = lax.rsqrt(jnp.mean(wide * wide, axis=-1, keepdims=True) + 1e-06) / jnp.sqrt(
        jnp.float32(rows.shape[-1])
    )
    return (wide * scale).astype(jnp.bfloat16)


def diagonal(count):
    down = lax.broadcasted_iota(jnp.int32, (count, count), 0)
    return down == lax.broadcasted_iota(jnp.int32, (count, count), 1)


def as_row(column):
    return jnp.sum(jnp.where(diagonal(column.shape[0]), column, 0.0), axis=0, keepdims=True)


def as_column(row):
    return jnp.sum(jnp.where(diagonal(row.shape[1]), row, 0.0), axis=1, keepdims=True)


def halves(value):
    high = value.astype(jnp.bfloat16)
    return high, (value - high.astype(jnp.float32)).astype(jnp.bfloat16)


def base_kernel(base_ref):
    base_ref[...] = jnp.zeros_like(base_ref)


def pack_kernel(tiles_ref, label_ref, rank_ref, base_ref, packed_ref):
    many = tiles_ref.shape[0]
    packed_ref[:many] = tiles_ref[...]
    rank = rank_ref[...]
    high = lax.shift_right_logical(rank, 8)
    low = rank - lax.shift_left(high, 8)
    lines = [line.astype(jnp.float32) for line in (label_ref[...], high, low)]
    lines.append(base_ref[len(lines) :, :])
    packed_ref[many] = jnp.concatenate(lines, axis=0).astype(jnp.bfloat16)


def labels_and_ranks(block):
    tile = block[block.shape[0] - 1].astype(jnp.float32)
    return tile[0:1], tile[1:2] * 256.0 + tile[2:3]


def rows_of(blocks, width):
    across = width // LANE
    wide = []
    for block in blocks:
        tiles = block[: block.shape[0] - 1].astype(jnp.float32)
        tiles = tiles.reshape(-1, across, SUB, LANE)
        pieces = [tiles[:, at].reshape(-1, LANE) for at in range(across)]
        wide.append(jnp.concatenate(pieces, axis=1))
    return jnp.concatenate(wide, axis=0)


def score(unit, side, blocks):
    own_label, own_rank = side[:, 0:1], side[:, 1:2]
    wide = rows_of(blocks, unit.shape[1])
    keys = wide.astype(jnp.bfloat16)
    sides = [labels_and_ranks(block) for block in blocks]
    label = jnp.concatenate([item[0] for item in sides], axis=1)
    rank = jnp.concatenate([item[1] for item in sides], axis=1)
    cosine = lax.dot_general(
        unit, make_unit(wide), (((1,), (1,)), ((), ())), preferred_element_type=jnp.float32
    )
    weight = 1.0 / (1.0 + jnp.exp(-40.0 * (cosine - 0.05)))
    near = jnp.where((label == own_label) & (rank != own_rank), weight, 0.0)
    earlier = jnp.sum(jnp.where(rank < own_rank, near, 0.0), axis=1, keepdims=True)
    every = jnp.sum(near, axis=1, keepdims=True)
    mixed = jnp.dot(near.astype(jnp.bfloat16), keys, preferred_element_type=jnp.float32)
    return earlier, every, mixed


def first_kernel(own_ref, other_ref, *refs):
    blocks, (unit_ref, side_ref, sums_ref, mixed_ref) = refs[:-4], refs[-4:]
    count = own_ref.shape[0] // (unit_ref.shape[1] // LANE) * SUB
    side_ref[...] = jnp.zeros_like(side_ref)
    sums_ref[...] = jnp.zeros_like(sums_ref)
    unit_ref[...] = make_unit(rows_of([own_ref, other_ref], unit_ref.shape[1]))
    for at, ref in enumerate((own_ref, other_ref)):
        here = slice(at * count, (at + 1) * count)
        label, rank = labels_and_ranks(ref)
        side_ref[here, 0:1] = as_column(label)
        side_ref[here, 1:2] = as_column(rank)
    sums_ref[:, 0:1], sums_ref[:, 1:2], mixed_ref[...] = score(
        unit_ref[...], side_ref, (own_ref,) + blocks
    )


def more_kernel(unit_ref, side_ref, old_sums_ref, old_mixed_ref, *refs):
    blocks, (sums_ref, mixed_ref) = refs[:-2], refs[-2:]
    earlier, every, mixed = score(unit_ref[...], side_ref, blocks)
    sums_ref[...] = old_sums_ref[...]
    sums_ref[:, 0:1] += earlier
    sums_ref[:, 1:2] += every
    mixed_ref[...] = old_mixed_ref[...] + mixed


def send_kernel(unit_ref, side_ref, old_sums_ref, old_mixed_ref, *refs):
    blocks, send_ref = refs[:-1], refs[-1]
    count, width = send_ref.shape[0] - EXTRA, send_ref.shape[1]
    earlier, every, mixed = score(unit_ref[count:, :], side_ref[count:, :], blocks)
    earlier += old_sums_ref[count:, 0:1]
    every += old_sums_ref[count:, 1:2]
    send_ref[:count, :] = (mixed + old_mixed_ref[count:, :]).astype(jnp.bfloat16)
    pieces = halves(as_row(earlier)) + halves(as_row(every))
    pieces = [piece.astype(jnp.float32) for piece in pieces]
    pieces.append(jnp.zeros((1, width - 4 * count), jnp.float32))
    line = jnp.concatenate(pieces, axis=1)
    send_ref[count:, :] = jnp.broadcast_to(line, (EXTRA, width)).astype(jnp.bfloat16)


def keep_kernel(unit_ref, side_ref, old_sums_ref, old_mixed_ref, *refs):
    blocks, (sums_ref, mixed_ref) = refs[:-2], refs[-2:]
    count = mixed_ref.shape[0]
    earlier, every, mixed = score(unit_ref[:count, :], side_ref[:count, :], blocks)
    sums_ref[...] = old_sums_ref[:count, :]
    sums_ref[:, 0:1] += earlier
    sums_ref[:, 1:2] += every
    mixed_ref[...] = old_mixed_ref[:count, :] + mixed


def combine_kernel(sums_ref, mixed_ref, got_ref, dup_ref, out_ref):
    count = mixed_ref.shape[0]
    line = got_ref[count:, :].astype(jnp.float32)[:1]
    parts = [line[:, at * count : (at + 1) * count] for at in range(4)]
    every = sums_ref[:, 1:2] + as_column(parts[2] + parts[3])
    dup_ref[...] = jnp.log1p(as_row(sums_ref[:, 0:1]) + parts[0] + parts[1])
    mixed = mixed_ref[...] + got_ref[:count, :].astype(jnp.float32)
    out_ref[...] = mixed / jnp.sqrt(1.0 + every)


def cost(queries, keys, width):
    return pl.CostEstimate(
        flops=400 * queries * keys * width,
        bytes_accessed=8 * queries * width + 2 * keys * width,
        transcendentals=100 * queries * keys,
    )


def local(embeddings, cluster_id, priority):
    count, width = embeddings.shape
    tiles = count // SUB * (width // LANE)
    shards = lax.axis_size("shard")
    lanes = lax.axis_size("owner")
    rounds = shards // 2
    queries = 2 * count
    bf16, f32 = jnp.bfloat16, jnp.float32
    params = pltpu.CompilerParams(vmem_limit_bytes=VMEM)

    def shape(*dims, dtype=f32):
        return jax.ShapeDtypeStruct(dims, dtype)

    ring = list(range(0, rounds, 2)) + list(range(1, rounds, 2))[::-1]

    def along(array, step):
        pairs = [
            (2 * ring[at] + side, 2 * ring[(at + step) % rounds] + side)
            for at in range(rounds)
            for side in range(2)
        ]
        return lax.ppermute(array, "shard", pairs)

    def across(array):
        return lax.ppermute(array, "shard", [(at, at ^ 1) for at in range(shards)])

    def swap(array):
        return lax.ppermute(array, "owner", [(at, lanes - 1 - at) for at in range(lanes)])

    def first(*blocks):
        return pl.pallas_call(
            first_kernel,
            out_shape=[
                shape(queries, width, dtype=bf16),
                shape(queries, 128),
                shape(queries, 128),
                shape(queries, width),
            ],
            cost_estimate=cost(queries, (len(blocks) - 1) * count, width),
            compiler_params=params,
            name="first_scores",
        )(*blocks)

    def more(unit, side, sums, mixed, *blocks):
        return pl.pallas_call(
            more_kernel,
            out_shape=[shape(queries, 128), shape(queries, width)],
            input_output_aliases={2: 0, 3: 1},
            cost_estimate=cost(queries, len(blocks) * count, width),
            compiler_params=params,
            name="more_scores",
        )(unit, side, sums, mixed, *blocks)

    def final(unit, side, sums, mixed, *blocks):
        send = pl.pallas_call(
            send_kernel,
            out_shape=shape(count + EXTRA, width, dtype=bf16),
            cost_estimate=cost(count, len(blocks) * count, width),
            compiler_params=params,
            name="send_scores",
        )(unit, side, sums, mixed, *blocks)
        keep_sums, keep = pl.pallas_call(
            keep_kernel,
            out_shape=[shape(count, 128), shape(count, width)],
            cost_estimate=cost(count, len(blocks) * count, width),
            compiler_params=params,
            name="keep_scores",
        )(unit, side, sums, mixed, *blocks)
        return keep_sums, keep, send

    pieces = embeddings.reshape(count // SUB, SUB, width // LANE, LANE).transpose(0, 2, 1, 3)
    base = pl.pallas_call(
        base_kernel,
        out_shape=shape(SUB, LANE),
        cost_estimate=pl.CostEstimate(flops=1000000000, bytes_accessed=0, transcendentals=0),
        compiler_params=params,
        name="base",
    )()
    own = pl.pallas_call(
        pack_kernel,
        out_shape=shape(tiles + 1, SUB, LANE, dtype=bf16),
        compiler_params=params,
        name="pack",
    )(pieces.reshape(tiles, SUB, LANE), cluster_id.reshape(1, count), priority.reshape(1, count), base)

    moved, beside = along(own, 1), across(own)
    other = swap(own)
    if rounds == 4:
        ahead = along(own, -1)
        moved, beside, other = lax.optimization_barrier((moved, beside, other))
        opposite = along(moved, 1)
        moved_beside = across(moved)
        ahead_beside = across(ahead)
        last = [along(moved_beside, 1), ahead_beside]
        unit, side, sums, mixed = first(own, other, beside, moved, moved_beside)
        sums, mixed = more(unit, side, sums, mixed, ahead, opposite)
    else:
        unit, side, sums, mixed = first(own, other, beside)

        def turn(at, state):
            moved, sums, mixed = state
            ahead, beside = along(moved, 1), across(moved)
            sums, mixed = more(unit, side, sums, mixed, moved, beside)
            return ahead, sums, mixed

        moved, sums, mixed = lax.fori_loop(1, rounds - 1, turn, (moved, sums, mixed))
        last = [moved, across(moved)]
    keep_sums, keep, send = final(unit, side, sums, mixed, *last)
    dup, out = pl.pallas_call(
        combine_kernel,
        out_shape=[shape(1, count), shape(count, width)],
        compiler_params=params,
        name="combine",
    )(keep_sums, keep, swap(send))
    return dup[0], out


def solution(mesh):
    placed = (
        P(("groups", "shard", "owner"), None),
        P(("groups", "shard", "owner"), None),
        P(("groups", "shard", "owner")),
    )
    return jax.shard_map(
        local,
        mesh=mesh,
        in_specs=placed,
        out_specs=(P(("groups", "shard", "owner")), P(("groups", "shard", "owner"), None)),
        check_vma=False,
    )
```

```python
import jax
import jax.numpy as jnp
from jax import lax
from jax.experimental import pallas as pl
from jax.experimental.pallas import tpu as pltpu
from jax.sharding import PartitionSpec as P

SUB, LANE = 8, 128
EXTRA = 8
VMEM = 24 * 1024 * 1024


def make_unit(rows):
    wide = rows.astype(jnp.float32)
    scale = lax.rsqrt(jnp.mean(wide * wide, axis=-1, keepdims=True) + 1e-06) / jnp.sqrt(
        jnp.float32(rows.shape[-1])
    )
    return (wide * scale).astype(jnp.bfloat16)


def diagonal(count):
    down = lax.broadcasted_iota(jnp.int32, (count, count), 0)
    return down == lax.broadcasted_iota(jnp.int32, (count, count), 1)


def as_row(column):
    return jnp.sum(jnp.where(diagonal(column.shape[0]), column, 0.0), axis=0, keepdims=True)


def as_column(row):
    return jnp.sum(jnp.where(diagonal(row.shape[1]), row, 0.0), axis=1, keepdims=True)


def halves(value):
    high = value.astype(jnp.bfloat16)
    return high, (value - high.astype(jnp.float32)).astype(jnp.bfloat16)


def base_kernel(base_ref):
    base_ref[...] = jnp.zeros_like(base_ref)


def pack_kernel(tiles_ref, label_ref, rank_ref, base_ref, packed_ref):
    many = tiles_ref.shape[0]
    packed_ref[:many] = tiles_ref[...]
    rank = rank_ref[...]
    high = lax.shift_right_logical(rank, 8)
    low = rank - lax.shift_left(high, 8)
    lines = [line.astype(jnp.float32) for line in (label_ref[...], high, low)]
    lines.append(base_ref[len(lines) :, :])
    packed_ref[many] = jnp.concatenate(lines, axis=0).astype(jnp.bfloat16)


def labels_and_ranks(block):
    tile = block[block.shape[0] - 1].astype(jnp.float32)
    return tile[0:1], tile[1:2] * 256.0 + tile[2:3]


def rows_of(blocks, width):
    across = width // LANE
    wide = []
    for block in blocks:
        tiles = block[: block.shape[0] - 1].astype(jnp.float32)
        tiles = tiles.reshape(-1, across, SUB, LANE)
        pieces = [tiles[:, at].reshape(-1, LANE) for at in range(across)]
        wide.append(jnp.concatenate(pieces, axis=1))
    return jnp.concatenate(wide, axis=0)


def score(unit, side, blocks):
    own_label, own_rank = side[:, 0:1], side[:, 1:2]
    wide = rows_of(blocks, unit.shape[1])
    keys = wide.astype(jnp.bfloat16)
    sides = [labels_and_ranks(block) for block in blocks]
    label = jnp.concatenate([item[0] for item in sides], axis=1)
    rank = jnp.concatenate([item[1] for item in sides], axis=1)
    cosine = lax.dot_general(
        unit, make_unit(wide), (((1,), (1,)), ((), ())), preferred_element_type=jnp.float32
    )
    weight = 1.0 / (1.0 + jnp.exp(-40.0 * (cosine - 0.05)))
    near = jnp.where((label == own_label) & (rank != own_rank), weight, 0.0)
    earlier = jnp.sum(jnp.where(rank < own_rank, near, 0.0), axis=1, keepdims=True)
    every = jnp.sum(near, axis=1, keepdims=True)
    mixed = jnp.dot(near.astype(jnp.bfloat16), keys, preferred_element_type=jnp.float32)
    return earlier, every, mixed


def first_kernel(own_ref, other_ref, *refs):
    blocks, (unit_ref, side_ref, sums_ref, mixed_ref) = refs[:-4], refs[-4:]
    count = own_ref.shape[0] // (unit_ref.shape[1] // LANE) * SUB
    side_ref[...] = jnp.zeros_like(side_ref)
    sums_ref[...] = jnp.zeros_like(sums_ref)
    unit_ref[...] = make_unit(rows_of([own_ref, other_ref], unit_ref.shape[1]))
    for at, ref in enumerate((own_ref, other_ref)):
        here = slice(at * count, (at + 1) * count)
        label, rank = labels_and_ranks(ref)
        side_ref[here, 0:1] = as_column(label)
        side_ref[here, 1:2] = as_column(rank)
    sums_ref[:, 0:1], sums_ref[:, 1:2], mixed_ref[...] = score(
        unit_ref[...], side_ref, (own_ref,) + blocks
    )


def more_kernel(unit_ref, side_ref, old_sums_ref, old_mixed_ref, *refs):
    blocks, (sums_ref, mixed_ref) = refs[:-2], refs[-2:]
    earlier, every, mixed = score(unit_ref[...], side_ref, blocks)
    sums_ref[...] = old_sums_ref[...]
    sums_ref[:, 0:1] += earlier
    sums_ref[:, 1:2] += every
    mixed_ref[...] = old_mixed_ref[...] + mixed


def send_kernel(unit_ref, side_ref, old_sums_ref, old_mixed_ref, *refs):
    blocks, send_ref = refs[:-1], refs[-1]
    count, width = send_ref.shape[0] - EXTRA, send_ref.shape[1]
    earlier, every, mixed = score(unit_ref[count:, :], side_ref[count:, :], blocks)
    earlier += old_sums_ref[count:, 0:1]
    every += old_sums_ref[count:, 1:2]
    send_ref[:count, :] = (mixed + old_mixed_ref[count:, :]).astype(jnp.bfloat16)
    pieces = halves(as_row(earlier)) + halves(as_row(every))
    pieces = [piece.astype(jnp.float32) for piece in pieces]
    pieces.append(jnp.zeros((1, width - 4 * count), jnp.float32))
    line = jnp.concatenate(pieces, axis=1)
    send_ref[count:, :] = jnp.broadcast_to(line, (EXTRA, width)).astype(jnp.bfloat16)


def keep_kernel(unit_ref, side_ref, old_sums_ref, old_mixed_ref, *refs):
    blocks, (sums_ref, mixed_ref) = refs[:-2], refs[-2:]
    count = mixed_ref.shape[0]
    earlier, every, mixed = score(unit_ref[:count, :], side_ref[:count, :], blocks)
    sums_ref[...] = old_sums_ref[:count, :]
    sums_ref[:, 0:1] += earlier
    sums_ref[:, 1:2] += every
    mixed_ref[...] = old_mixed_ref[:count, :] + mixed


def combine_kernel(sums_ref, mixed_ref, got_ref, dup_ref, out_ref):
    count = mixed_ref.shape[0]
    line = got_ref[count:, :].astype(jnp.float32)[:1]
    parts = [line[:, at * count : (at + 1) * count] for at in range(4)]
    every = sums_ref[:, 1:2] + as_column(parts[2] + parts[3])
    dup_ref[...] = jnp.log1p(as_row(sums_ref[:, 0:1]) + parts[0] + parts[1])
    mixed = mixed_ref[...] + got_ref[:count, :].astype(jnp.float32)
    out_ref[...] = mixed / jnp.sqrt(1.0 + every)


def cost(queries, keys, width):
    return pl.CostEstimate(
        flops=400 * queries * keys * width,
        bytes_accessed=8 * queries * width + 2 * keys * width,
        transcendentals=100 * queries * keys,
    )


def local(embeddings, cluster_id, priority):
    count, width = embeddings.shape
    tiles = count // SUB * (width // LANE)
    shards = lax.axis_size("shard")
    lanes = lax.axis_size("owner")
    rounds = shards // 2
    queries = 2 * count
    bf16, f32 = jnp.bfloat16, jnp.float32
    params = pltpu.CompilerParams(vmem_limit_bytes=VMEM)

    def shape(*dims, dtype=f32):
        return jax.ShapeDtypeStruct(dims, dtype)

    ring = list(range(0, rounds, 2)) + list(range(1, rounds, 2))[::-1]

    def along(array, step):
        pairs = [
            (2 * ring[at] + side, 2 * ring[(at + step) % rounds] + side)
            for at in range(rounds)
            for side in range(2)
        ]
        return lax.ppermute(array, "shard", pairs)

    def across(array):
        return lax.ppermute(array, "shard", [(at, at ^ 1) for at in range(shards)])

    def swap(array):
        return lax.ppermute(array, "owner", [(at, lanes - 1 - at) for at in range(lanes)])

    def first(*blocks):
        return pl.pallas_call(
            first_kernel,
            out_shape=[
                shape(queries, width, dtype=bf16),
                shape(queries, 128),
                shape(queries, 128),
                shape(queries, width),
            ],
            cost_estimate=cost(queries, (len(blocks) - 1) * count, width),
            compiler_params=params,
            name="first_scores",
        )(*blocks)

    def more(unit, side, sums, mixed, *blocks):
        return pl.pallas_call(
            more_kernel,
            out_shape=[shape(queries, 128), shape(queries, width)],
            input_output_aliases={2: 0, 3: 1},
            cost_estimate=cost(queries, len(blocks) * count, width),
            compiler_params=params,
            name="more_scores",
        )(unit, side, sums, mixed, *blocks)

    def final(unit, side, sums, mixed, *blocks):
        send = pl.pallas_call(
            send_kernel,
            out_shape=shape(count + EXTRA, width, dtype=bf16),
            cost_estimate=cost(count, len(blocks) * count, width),
            compiler_params=params,
            name="send_scores",
        )(unit, side, sums, mixed, *blocks)
        keep_sums, keep = pl.pallas_call(
            keep_kernel,
            out_shape=[shape(count, 128), shape(count, width)],
            cost_estimate=cost(count, len(blocks) * count, width),
            compiler_params=params,
            name="keep_scores",
        )(unit, side, sums, mixed, *blocks)
        return keep_sums, keep, send

    pieces = embeddings.reshape(count // SUB, SUB, width // LANE, LANE).transpose(0, 2, 1, 3)
    base = pl.pallas_call(
        base_kernel,
        out_shape=shape(SUB, LANE),
        cost_estimate=pl.CostEstimate(flops=1000000000, bytes_accessed=0, transcendentals=0),
        compiler_params=params,
        name="base",
    )()
    own = pl.pallas_call(
        pack_kernel,
        out_shape=shape(tiles + 1, SUB, LANE, dtype=bf16),
        compiler_params=params,
        name="pack",
    )(pieces.reshape(tiles, SUB, LANE), cluster_id.reshape(1, count), priority.reshape(1, count), base)

    moved, beside = along(own, 1), across(own)
    other = swap(own)
    if rounds == 4:
        ahead = along(own, -1)
        moved, beside = lax.optimization_barrier((moved, beside))
        opposite = along(moved, 1)
        moved_beside = across(moved)
        ahead_beside = across(ahead)
        last = [along(moved_beside, 1), ahead_beside]
        unit, side, sums, mixed = first(own, other, beside, moved, moved_beside)
        sums, mixed = more(unit, side, sums, mixed, ahead, opposite)
    else:
        unit, side, sums, mixed = first(own, other, beside)

        def turn(at, state):
            moved, sums, mixed = state
            ahead, beside = along(moved, 1), across(moved)
            sums, mixed = more(unit, side, sums, mixed, moved, beside)
            return ahead, sums, mixed

        moved, sums, mixed = lax.fori_loop(1, rounds - 1, turn, (moved, sums, mixed))
        last = [moved, across(moved)]
    keep_sums, keep, send = final(unit, side, sums, mixed, *last)
    dup, out = pl.pallas_call(
        combine_kernel,
        out_shape=[shape(1, count), shape(count, width)],
        compiler_params=params,
        name="combine",
    )(keep_sums, keep, swap(send))
    return dup[0], out


def solution(mesh):
    placed = (
        P(("groups", "shard", "owner"), None),
        P(("groups", "shard", "owner"), None),
        P(("groups", "shard", "owner")),
    )
    return jax.shard_map(
        local,
        mesh=mesh,
        in_specs=placed,
        out_specs=(P(("groups", "shard", "owner")), P(("groups", "shard", "owner"), None)),
        check_vma=False,
    )
```

```python
import jax
import jax.numpy as jnp
from jax import lax
from jax.experimental import pallas as pl
from jax.experimental.pallas import tpu as pltpu
from jax.sharding import PartitionSpec as P

SUB, LANE = 8, 128
EXTRA = 8
VMEM = 24 * 1024 * 1024


def make_unit(rows):
    wide = rows.astype(jnp.float32)
    scale = lax.rsqrt(jnp.mean(wide * wide, axis=-1, keepdims=True) + 1e-06) / jnp.sqrt(
        jnp.float32(rows.shape[-1])
    )
    return (wide * scale).astype(jnp.bfloat16)


def diagonal(count):
    down = lax.broadcasted_iota(jnp.int32, (count, count), 0)
    return down == lax.broadcasted_iota(jnp.int32, (count, count), 1)


def as_row(column):
    return jnp.sum(jnp.where(diagonal(column.shape[0]), column, 0.0), axis=0, keepdims=True)


def as_column(row):
    return jnp.sum(jnp.where(diagonal(row.shape[1]), row, 0.0), axis=1, keepdims=True)


def halves(value):
    high = value.astype(jnp.bfloat16)
    return high, (value - high.astype(jnp.float32)).astype(jnp.bfloat16)


def base_kernel(base_ref):
    base_ref[...] = jnp.zeros_like(base_ref)


def pack_kernel(tiles_ref, label_ref, rank_ref, base_ref, packed_ref):
    many = tiles_ref.shape[0]
    packed_ref[:many] = tiles_ref[...]
    rank = rank_ref[...]
    high = lax.shift_right_logical(rank, 8)
    low = rank - lax.shift_left(high, 8)
    lines = [line.astype(jnp.float32) for line in (label_ref[...], high, low)]
    lines.append(base_ref[len(lines) :, :])
    packed_ref[many] = jnp.concatenate(lines, axis=0).astype(jnp.bfloat16)


def labels_and_ranks(block):
    tile = block[block.shape[0] - 1].astype(jnp.float32)
    return tile[0:1], tile[1:2] * 256.0 + tile[2:3]


def rows_of(blocks, width):
    across = width // LANE
    wide = []
    for block in blocks:
        tiles = block[: block.shape[0] - 1].astype(jnp.float32)
        tiles = tiles.reshape(-1, across, SUB, LANE)
        pieces = [tiles[:, at].reshape(-1, LANE) for at in range(across)]
        wide.append(jnp.concatenate(pieces, axis=1))
    return jnp.concatenate(wide, axis=0)


def score(unit, side, blocks):
    own_label, own_rank = side[:, 0:1], side[:, 1:2]
    wide = rows_of(blocks, unit.shape[1])
    keys = wide.astype(jnp.bfloat16)
    sides = [labels_and_ranks(block) for block in blocks]
    label = jnp.concatenate([item[0] for item in sides], axis=1)
    rank = jnp.concatenate([item[1] for item in sides], axis=1)
    cosine = lax.dot_general(
        unit, make_unit(wide), (((1,), (1,)), ((), ())), preferred_element_type=jnp.float32
    )
    weight = 1.0 / (1.0 + jnp.exp(-40.0 * (cosine - 0.05)))
    near = jnp.where((label == own_label) & (rank != own_rank), weight, 0.0)
    earlier = jnp.sum(jnp.where(rank < own_rank, near, 0.0), axis=1, keepdims=True)
    every = jnp.sum(near, axis=1, keepdims=True)
    mixed = jnp.dot(near.astype(jnp.bfloat16), keys, preferred_element_type=jnp.float32)
    return earlier, every, mixed


def first_kernel(own_ref, other_ref, *refs):
    blocks, (unit_ref, side_ref, sums_ref, mixed_ref) = refs[:-4], refs[-4:]
    count = own_ref.shape[0] // (unit_ref.shape[1] // LANE) * SUB
    side_ref[...] = jnp.zeros_like(side_ref)
    sums_ref[...] = jnp.zeros_like(sums_ref)
    unit_ref[...] = make_unit(rows_of([own_ref, other_ref], unit_ref.shape[1]))
    for at, ref in enumerate((own_ref, other_ref)):
        here = slice(at * count, (at + 1) * count)
        label, rank = labels_and_ranks(ref)
        side_ref[here, 0:1] = as_column(label)
        side_ref[here, 1:2] = as_column(rank)
    sums_ref[:, 0:1], sums_ref[:, 1:2], mixed_ref[...] = score(
        unit_ref[...], side_ref, (own_ref,) + blocks
    )


def more_kernel(unit_ref, side_ref, old_sums_ref, old_mixed_ref, *refs):
    blocks, (sums_ref, mixed_ref) = refs[:-2], refs[-2:]
    earlier, every, mixed = score(unit_ref[...], side_ref, blocks)
    sums_ref[...] = old_sums_ref[...]
    sums_ref[:, 0:1] += earlier
    sums_ref[:, 1:2] += every
    mixed_ref[...] = old_mixed_ref[...] + mixed


def send_kernel(unit_ref, side_ref, old_sums_ref, old_mixed_ref, *refs):
    blocks, send_ref = refs[:-1], refs[-1]
    count, width = send_ref.shape[0] - EXTRA, send_ref.shape[1]
    earlier, every, mixed = score(unit_ref[count:, :], side_ref[count:, :], blocks)
    earlier += old_sums_ref[count:, 0:1]
    every += old_sums_ref[count:, 1:2]
    send_ref[:count, :] = (mixed + old_mixed_ref[count:, :]).astype(jnp.bfloat16)
    pieces = halves(as_row(earlier)) + halves(as_row(every))
    pieces = [piece.astype(jnp.float32) for piece in pieces]
    pieces.append(jnp.zeros((1, width - 4 * count), jnp.float32))
    line = jnp.concatenate(pieces, axis=1)
    send_ref[count:, :] = jnp.broadcast_to(line, (EXTRA, width)).astype(jnp.bfloat16)


def keep_kernel(unit_ref, side_ref, old_sums_ref, old_mixed_ref, *refs):
    blocks, (sums_ref, mixed_ref) = refs[:-2], refs[-2:]
    count = mixed_ref.shape[0]
    earlier, every, mixed = score(unit_ref[:count, :], side_ref[:count, :], blocks)
    sums_ref[...] = old_sums_ref[:count, :]
    sums_ref[:, 0:1] += earlier
    sums_ref[:, 1:2] += every
    mixed_ref[...] = old_mixed_ref[:count, :] + mixed


def combine_kernel(sums_ref, mixed_ref, got_ref, dup_ref, out_ref):
    count = mixed_ref.shape[0]
    line = got_ref[count:, :].astype(jnp.float32)[:1]
    parts = [line[:, at * count : (at + 1) * count] for at in range(4)]
    every = sums_ref[:, 1:2] + as_column(parts[2] + parts[3])
    dup_ref[...] = jnp.log1p(as_row(sums_ref[:, 0:1]) + parts[0] + parts[1])
    mixed = mixed_ref[...] + got_ref[:count, :].astype(jnp.float32)
    out_ref[...] = mixed / jnp.sqrt(1.0 + every)


def cost(queries, keys, width):
    return pl.CostEstimate(
        flops=400 * queries * keys * width,
        bytes_accessed=8 * queries * width + 2 * keys * width,
        transcendentals=100 * queries * keys,
    )


def local(embeddings, cluster_id, priority):
    count, width = embeddings.shape
    tiles = count // SUB * (width // LANE)
    shards = lax.axis_size("shard")
    lanes = lax.axis_size("owner")
    rounds = shards // 2
    queries = 2 * count
    bf16, f32 = jnp.bfloat16, jnp.float32
    params = pltpu.CompilerParams(vmem_limit_bytes=VMEM)

    def shape(*dims, dtype=f32):
        return jax.ShapeDtypeStruct(dims, dtype)

    ring = list(range(0, rounds, 2)) + list(range(1, rounds, 2))[::-1]

    def along(array, step):
        pairs = [
            (2 * ring[at] + side, 2 * ring[(at + step) % rounds] + side)
            for at in range(rounds)
            for side in range(2)
        ]
        return lax.ppermute(array, "shard", pairs)

    def across(array):
        return lax.ppermute(array, "shard", [(at, at ^ 1) for at in range(shards)])

    def swap(array):
        return lax.ppermute(array, "owner", [(at, lanes - 1 - at) for at in range(lanes)])

    def first(*blocks):
        return pl.pallas_call(
            first_kernel,
            out_shape=[
                shape(queries, width, dtype=bf16),
                shape(queries, 128),
                shape(queries, 128),
                shape(queries, width),
            ],
            cost_estimate=cost(queries, (len(blocks) - 1) * count, width),
            compiler_params=params,
            name="first_scores",
        )(*blocks)

    def more(unit, side, sums, mixed, *blocks):
        return pl.pallas_call(
            more_kernel,
            out_shape=[shape(queries, 128), shape(queries, width)],
            input_output_aliases={2: 0, 3: 1},
            cost_estimate=cost(queries, len(blocks) * count, width),
            compiler_params=params,
            name="more_scores",
        )(unit, side, sums, mixed, *blocks)

    def final(unit, side, sums, mixed, *blocks):
        send = pl.pallas_call(
            send_kernel,
            out_shape=shape(count + EXTRA, width, dtype=bf16),
            cost_estimate=cost(count, len(blocks) * count, width),
            compiler_params=params,
            name="send_scores",
        )(unit, side, sums, mixed, *blocks)
        keep_sums, keep = pl.pallas_call(
            keep_kernel,
            out_shape=[shape(count, 128), shape(count, width)],
            cost_estimate=cost(count, len(blocks) * count, width),
            compiler_params=params,
            name="keep_scores",
        )(unit, side, sums, mixed, *blocks)
        return keep_sums, keep, send

    pieces = embeddings.reshape(count // SUB, SUB, width // LANE, LANE).transpose(0, 2, 1, 3)
    base = pl.pallas_call(
        base_kernel,
        out_shape=shape(SUB, LANE),
        cost_estimate=pl.CostEstimate(flops=1000000000, bytes_accessed=0, transcendentals=0),
        compiler_params=params,
        name="base",
    )()
    own = pl.pallas_call(
        pack_kernel,
        out_shape=shape(tiles + 1, SUB, LANE, dtype=bf16),
        compiler_params=params,
        name="pack",
    )(pieces.reshape(tiles, SUB, LANE), cluster_id.reshape(1, count), priority.reshape(1, count), base)

    moved, beside = along(own, 1), across(own)
    other = swap(own)
    if rounds == 4:
        ahead = along(own, -1)
        beside, moved = lax.optimization_barrier((beside, moved))
        opposite = along(moved, 1)
        moved_beside = across(moved)
        ahead_beside = across(ahead)
        last = [along(moved_beside, 1)]
        unit, side, sums, mixed = first(own, other, beside, moved, moved_beside)
        sums, mixed = more(unit, side, sums, mixed, ahead, opposite, ahead_beside)
    else:
        unit, side, sums, mixed = first(own, other, beside)

        def turn(at, state):
            moved, sums, mixed = state
            ahead, beside = along(moved, 1), across(moved)
            sums, mixed = more(unit, side, sums, mixed, moved, beside)
            return ahead, sums, mixed

        moved, sums, mixed = lax.fori_loop(1, rounds - 1, turn, (moved, sums, mixed))
        last = [moved, across(moved)]
    keep_sums, keep, send = final(unit, side, sums, mixed, *last)
    dup, out = pl.pallas_call(
        combine_kernel,
        out_shape=[shape(1, count), shape(count, width)],
        compiler_params=params,
        name="combine",
    )(keep_sums, keep, swap(send))
    return dup[0], out


def solution(mesh):
    placed = (
        P(("groups", "shard", "owner"), None),
        P(("groups", "shard", "owner"), None),
        P(("groups", "shard", "owner")),
    )
    return jax.shard_map(
        local,
        mesh=mesh,
        in_specs=placed,
        out_specs=(P(("groups", "shard", "owner")), P(("groups", "shard", "owner"), None)),
        check_vma=False,
    )
```
